256 devices in a mesh: grp: 2 (over x_hi), ctx: 16 (over z, x_lo), mp: 8 (over y, core).
Axes of the slice: x: 4 (x_hi: 2, x_lo: 2; x = x_hi * 2 + x_lo), y: 4, z: 8, core: 2. Of those that a mesh axis runs over, the one named last changes fastest.
Arguments:
- states: bfloat16 [2, 6144, 5120], P('grp', 'ctx', 'mp'), may hold values from -6 to 6
- noise: bfloat16 [2, 6144, 5120], P('grp', 'ctx', 'mp'), may hold values from -6 to 6
- span_lengths: int32 [2, 4], P('grp'), may hold values from 1 to 3072, 6144 in all within a row
- step_index: int32 [2, 4], P('grp'), may hold values from 0 to 3
- gain: float32 [2, 5120], P('grp'), may hold values from 0.1 to 1.9
- in_weights: bfloat16 [2, 5120, 3, 3072], P('grp', 'ctx', None, 'mp'), may hold values from -0.169658223 to 0.169658223
- out_weights: bfloat16 [2, 3072, 5120], P('grp', 'mp'), may hold values from -0.109375 to 0.109375
Outputs:
- received: bfloat16 [2, 6144, 5120], P('grp', 'ctx', 'mp')
The draws below stay inside these ranges and needn't reach their ends.
Inputs may be any that keep to these rules, and one draw needn't show every extreme that they name: `span_lengths`: each row's 4 lengths sum to 6144; the largest is exactly 3072.
All inputs are finite; a program needn't handle non-finite values.
Results may differ from the reference program's by a relative error of at most 0.014.
Values may be sent and summed in bfloat16 or wider, within the bound.
No kernel may reach another device: no remote copies, remote signals or barrier semaphores. Data moves between devices by JAX's collectives and lax.ppermute only.
A program may use at most 128 MiB of HBM per device.

```python
import math
import jax
import jax.numpy as jnp
import numpy as np
from jax import lax

D = 5120
HEADS = 24
HEAD_DIM = 128
TOK_DEV = 384
SPANS = 4
STEPS = 4
TOKENS = 6144
HD = 3072
N_CTX = 16
N_MP = 8


def draw_states(key, part):
    key = jax.random.fold_in(key, 1)
    return jnp.clip(jax.random.normal(key, (2, TOKENS, D), jnp.float32), -6.0, 6.0).astype(jnp.bfloat16)


def draw_noise(key, part):
    key = jax.random.fold_in(key, 2)
    return jnp.clip(jax.random.normal(key, (2, TOKENS, D), jnp.float32), -6.0, 6.0).astype(jnp.bfloat16)


def draw_in_weights(key, part):
    key = jax.random.fold_in(key, 3)
    base = jnp.clip(jax.random.normal(key, (2, D, 3, HD), jnp.float32), -6.0, 6.0)
    return (base * (2.0 * D ** (-0.5))).astype(jnp.bfloat16)


def set_ends(result, key, low, top_value):
    shape = result.shape
    index_at = [jax.random.randint(jax.random.fold_in(key, axis), (), 0, shape[axis]) for axis in range(len(shape))]
    result = result.at[tuple(index_at)].set(low)
    longest = shape.index(max(shape))
    index_at[longest] = (index_at[longest] + 1) % shape[longest]
    return result.at[tuple(index_at)].set(top_value)


def level_of(stream_key, extent, cuts, smallest, high):
    loudness, own = 1.0, jax.random.fold_in(stream_key, 6)
    for dim, blocks in cuts:
        draws = jnp.exp(jax.random.uniform(jax.random.fold_in(own, dim), (blocks,), jnp.float32, smallest / len(cuts), high / len(cuts)))
        loudness = loudness * jnp.repeat(draws, extent[dim] // blocks).reshape([-1 if axis == dim else 1 for axis in range(len(extent))])
    return loudness


def profile(number_of, total, reach, lean):
    portions = [(1 << 20) // math.isqrt(grade ** lean) + 1 for grade in range(2, number_of + 1)]
    surplus, counts = total - reach - (number_of - 1), [1] * (number_of - 1)
    while surplus > 0:
        movable = [i for i in range(number_of - 1) if counts[i] < reach]
        whole, budget = sum([portions[i] for i in movable]), surplus
        for i in movable:
            addition = min(reach - counts[i], max(1, budget * portions[i] // whole), surplus)
            counts[i] = counts[i] + addition
            surplus = surplus - addition
    return np.array([reach] + counts)


def ragged_sizes(own_key, number_of, total, limit, lean):
    if number_of == 2:
        one = jax.random.randint(own_key, (), max(1, total - limit), min(limit, total - 1) + 1)
        return jnp.stack([one, total - one])
    sizes = jnp.asarray(profile(number_of, total, limit, lean), jnp.int32)
    pairs = (number_of - 1) // 2
    giver, receiver = sizes[1:1 + 2 * pairs:2], sizes[2:2 + 2 * pairs:2]
    margin = jnp.minimum(giver - 1, limit - receiver)
    moved = jax.random.randint(jax.random.fold_in(own_key, 1), (pairs,), 0, 1 << 20) % (margin + 1)
    sizes = sizes.at[1:1 + 2 * pairs:2].set(giver - moved).at[2:2 + 2 * pairs:2].set(receiver + moved)
    return sizes[jax.random.permutation(jax.random.fold_in(own_key, 2), number_of)]


def gaussian(key, shape, scale, bound, pieces=(), held_as=jnp.bfloat16):
    level = level_of(key, shape, pieces, -0.22, 0.18) if pieces else 1.0
    values = jax.random.normal(key, shape, jnp.float32) * scale * level
    return jnp.minimum(jnp.maximum(values, -bound), bound).astype(held_as)


def setup_inputs(seed: int = 0) -> dict:
    splits = jax.random.split(jax.random.key(seed), 8)
    states = draw_states(jax.random.fold_in(splits[7], 71), 0)
    noise = draw_noise(jax.random.fold_in(splits[7], 71), 0)
    span_lengths = jax.vmap(lambda own: ragged_sizes(own, SPANS, TOKENS, TOKENS // 2, 2))(jax.random.split(splits[2], 2)).reshape((2, SPANS)).astype(jnp.int32)
    step_index = set_ends(jax.random.randint(splits[3], (2, SPANS), 0, STEPS), jax.random.fold_in(splits[3], 1), 0, STEPS - 1).astype(jnp.int32)
    gain = jnp.clip(1.0 + 0.18 * jax.random.normal(splits[4], (2, D), jnp.float32), 0.1, 1.9)
    in_weights = draw_in_weights(jax.random.fold_in(splits[7], 71), 0)
    out_weights = gaussian(splits[6], (2, HD, D), HD ** -0.5, 0.109375, ((0, 2), (1, 8)))
    return dict(states=states, noise=noise, span_lengths=span_lengths, step_index=step_index, gain=gain, in_weights=in_weights, out_weights=out_weights)


def span_ids(positions, lengths):
    ends = jnp.cumsum(lengths).astype(jnp.int32)
    return lax.optimization_barrier(jnp.sum((positions[:, None] >= ends[None, :]).astype(jnp.int32), axis=1)).astype(jnp.int32)

def row_times(spans, steps):
    hits = spans[:, None] == jnp.arange(SPANS, dtype=jnp.int32)[None, :]
    picked = jnp.where(hits, (steps[None, :] + 1).astype(jnp.float32), jnp.float32(0.0))
    return lax.optimization_barrier(jnp.sum(picked, axis=1)) / STEPS

def one_group(state, noise, lengths, steps, gain, in_weights, out_weights, causal):
    positions = jnp.arange(TOKENS, dtype=jnp.int32)
    spans = span_ids(positions, lengths)
    times = row_times(spans, steps)[:, None]
    mixed = ((1.0 - times) * state.astype(jnp.float32) + times * noise.astype(jnp.float32)).astype(jnp.bfloat16)
    wide = mixed.astype(jnp.float32)
    mean_square = lax.optimization_barrier(jnp.mean(wide * wide, axis=1, keepdims=True))
    inverse_root = lax.rsqrt(mean_square + 1e-06)
    normed = (wide * inverse_root * gain[None, :]).astype(jnp.bfloat16)
    projected = jnp.dot(normed, in_weights.reshape(D, 3 * HD), preferred_element_type=jnp.float32).astype(jnp.bfloat16)
    projected = projected.reshape(TOKENS, 3, HEADS, HEAD_DIM)
    query = projected[:, 0]
    keys_wide = projected[:, 1].astype(jnp.float32)
    values_wide = projected[:, 2].astype(jnp.float32)

    def block(item):
        query_block, query_spans = item
        scores = jnp.einsum('bhd,shd->hbs', query_block.astype(jnp.float32), keys_wide) * HEAD_DIM ** (-0.5)
        allowed = spans[None, :] <= query_spans[:, None]
        if not causal:
            allowed = jnp.ones_like(allowed)
        scores = jnp.where(allowed[None], scores, -1e+30)
        highest = lax.optimization_barrier(jnp.max(scores, axis=2, keepdims=True))
        weights = jnp.where(allowed[None], jnp.exp(scores - highest), 0.0)
        summed = lax.optimization_barrier(jnp.sum(weights, axis=2))
        rounded = lax.optimization_barrier(weights.astype(jnp.bfloat16))
        output = jnp.einsum('hbs,shd->hbd', rounded.astype(jnp.float32), values_wide)
        return jnp.transpose(output / summed[..., None], (1, 0, 2)).astype(jnp.bfloat16)
    attended = lax.map(block, (query.reshape(N_CTX, TOK_DEV, HEADS, HEAD_DIM), spans.reshape(N_CTX, TOK_DEV)))
    attended = attended.reshape(TOKENS, HD)
    width = HD // N_MP
    velocity = jnp.zeros((TOKENS, D), jnp.float32)
    for group_part in range(N_MP):
        term = jnp.dot(attended[:, group_part * width:(group_part + 1) * width], out_weights[group_part * width:(group_part + 1) * width], preferred_element_type=jnp.float32)
        rounded = lax.optimization_barrier(term.astype(jnp.bfloat16))
        velocity = velocity + rounded.astype(jnp.float32)
    estimate = wide - times * velocity
    if causal:
        return estimate.astype(jnp.bfloat16)
    return (state.astype(jnp.float32) - estimate).astype(jnp.bfloat16)

def reference(states, noise, span_lengths, step_index, gain, in_weights, out_weights):
    student = one_group(states[0], noise[0], span_lengths[0], step_index[0], gain[0], in_weights[0], out_weights[0], True)
    teacher = one_group(states[1], noise[1], span_lengths[1], step_index[1], gain[1], in_weights[1], out_weights[1], False)
    return jnp.stack([teacher, student])
```

```python
import jax
import jax.numpy as jnp
from jax import lax
from jax.sharding import PartitionSpec as P

HEAD_DIM = 128
STEPS = 4


def swapped(block, axis, stride):
    count = lax.axis_size(axis)
    route = []
    for low in range(count):
        high = low | 1 << stride
        if high != low and high < count:
            route += [(low, high), (high, low)]
    return lax.ppermute(block, axis, route)


def crossed(block):
    return lax.ppermute(block, ("a", "c"), [(0, 0), (1, 2), (2, 1), (3, 3)])


def span_ids(positions, lengths):
    ends = jnp.cumsum(lengths)
    return jnp.sum((positions[:, None] >= ends[None, :]).astype(jnp.int32), axis=1)


def local(states, noise, span_lengths, step_index, gain, in_weights, out_weights):
    tokens_here = states.shape[1]
    group = lax.axis_index("grp")
    lengths = span_lengths[0]
    here = jnp.arange(tokens_here, dtype=jnp.int32)
    spans_home = span_ids(lax.axis_index(("z", "a")) * tokens_here + here, lengths)
    spans = span_ids(lax.axis_index(("z", "c")) * tokens_here + here, lengths)
    hits = spans_home[:, None] == jnp.arange(lengths.shape[0], dtype=jnp.int32)[None, :]
    picked = jnp.where(hits, (step_index[0][None, :] + 1).astype(jnp.float32), jnp.float32(0.0))
    times = (jnp.sum(picked, axis=1) / STEPS)[:, None]
    state = states[0].astype(jnp.float32)
    mixed = ((1.0 - times) * state + times * noise[0].astype(jnp.float32)).astype(jnp.bfloat16)
    gathered = lax.all_gather(crossed(mixed), ("y", "a"), axis=1, tiled=True)
    wide = gathered.astype(jnp.float32)
    mean_square = jnp.mean(wide * wide, axis=1, keepdims=True)
    inverse_root = lax.rsqrt(mean_square + 1e-06)
    normed = (wide * inverse_root * gain[0][None, :]).astype(jnp.bfloat16)
    local_rows = crossed(in_weights[0])
    full_rows = lax.all_gather(local_rows, ("z", "c"), axis=0, tiled=True)
    projected = jnp.einsum("rd,dkh->rkh", normed, full_rows, preferred_element_type=jnp.float32)
    projected = projected.astype(jnp.bfloat16)
    heads = projected.shape[2] // HEAD_DIM
    query = projected[:, 0].reshape(tokens_here, heads, HEAD_DIM)
    keys = projected[:, 1].reshape(tokens_here, heads, HEAD_DIM)
    values = projected[:, 2].reshape(tokens_here, heads, HEAD_DIM)
    highest = jnp.full((heads, tokens_here), -1e30, jnp.float32)
    key_piece = lax.all_gather(keys, ("z", "c"), axis=0, tiled=True)
    value_piece = lax.all_gather(values, ("z", "c"), axis=0, tiled=True)
    count = key_piece.shape[0]
    key_spans = span_ids(jnp.arange(count, dtype=jnp.int32), lengths)
    allowed = (key_spans[None, :] <= spans[:, None]) | (group == 1)
    scores = jnp.einsum(
        "rhd,nhd->hrn", query, key_piece, preferred_element_type=jnp.float32
    ) * HEAD_DIM ** (-0.5)
    scores = jnp.where(allowed[None], scores, -1e30)
    new_high = jnp.maximum(highest, jnp.max(scores, axis=2))
    weights = jnp.where(allowed[None], jnp.exp(scores - new_high[..., None]), 0.0)
    summed = jnp.sum(weights, axis=2)
    output = jnp.einsum(
        "hrn,nhd->hrd",
        weights.astype(jnp.bfloat16),
        value_piece,
        preferred_element_type=jnp.float32,
    )
    highest, summed, output = (new_high, summed, output)
    attended = (
        jnp.transpose(output / summed[..., None], (1, 0, 2))
        .reshape(tokens_here, heads * HEAD_DIM)
        .astype(jnp.bfloat16)
    )
    attended = crossed(attended)
    partial_terms = jnp.dot(attended, out_weights[0], preferred_element_type=jnp.float32)
    velocity = lax.psum_scatter(
        partial_terms.astype(jnp.bfloat16), ("y", "c"), scatter_dimension=1, tiled=True
    ).astype(jnp.float32)
    estimate = mixed.astype(jnp.float32) - times * velocity
    result = jnp.where(group == 0, estimate, state - estimate).astype(jnp.bfloat16)
    arrived = swapped(result, "grp", 0)
    return arrived[None]


def solution(mesh):
    fine = jax.sharding.Mesh(mesh.devices.reshape(2, 8, 2, 4, 2), ("grp", "z", "a", "y", "c"))
    tokens, features = ("z", "a"), ("y", "c")
    return jax.shard_map(
        local,
        mesh=fine,
        in_specs=(
            P("grp", tokens, features),
            P("grp", tokens, features),
            P("grp", None),
            P("grp", None),
            P("grp", None),
            P("grp", tokens, None, features),
            P("grp", features, None),
        ),
        out_specs=P("grp", tokens, features),
        check_vma=False,
    )
```

```python
import functools

import jax
import jax.numpy as jnp
from jax import lax
from jax.experimental import pallas as pl
from jax.experimental.pallas import tpu as pltpu
from jax.sharding import PartitionSpec as P

HEAD_DIM = 128
STEPS = 4
LOW = -1e30
SCALE2 = HEAD_DIM ** (-0.5) * 1.4426950408889634


def crossed(block):
    return lax.ppermute(block, ("a", "c"), [(0, 0), (1, 2), (2, 1), (3, 3)])


def shifted(block, axis, hop):
    count = lax.axis_size(axis)
    return lax.ppermute(block, axis, [(i, (i - hop) % count) for i in range(count)])


def span_ends(lengths):
    return jnp.cumsum(lengths)


def flash_kernel(n_blocks, first, last, base_ref, limit_ref, q_ref, *refs):
    keys = refs[:n_blocks]
    values = refs[n_blocks:2 * n_blocks]
    rest = refs[2 * n_blocks:]
    if not first:
        m_in, l_in, acc_in = rest[:3]
        rest = rest[3:]
    heads = q_ref.shape[1] // HEAD_DIM
    limit = limit_ref[...]
    for head in range(heads):
        cols = slice(head * HEAD_DIM, (head + 1) * HEAD_DIM)
        query = q_ref[:, cols]
        scores = []
        for block in range(n_blocks):
            score = lax.dot_general(
                query, keys[block][:, cols], (((1,), (1,)), ((), ())),
                preferred_element_type=jnp.float32,
            )
            place = lax.broadcasted_iota(jnp.int32, score.shape, 1) + base_ref[block]
            scores.append(jnp.where(place < limit, score, LOW))
        high = functools.reduce(
            jnp.maximum, [jnp.max(score, axis=1, keepdims=True) for score in scores]
        )
        if not first:
            before = m_in[:, cols][:, :1]
            high = jnp.maximum(high, before)
        shift = high * SCALE2
        total, output = 0.0, 0.0
        for block in range(n_blocks):
            weight = jnp.exp2(scores[block] * SCALE2 - shift)
            total = total + jnp.sum(weight, axis=1, keepdims=True)
            output = output + jnp.dot(
                weight.astype(jnp.bfloat16), values[block][:, cols],
                preferred_element_type=jnp.float32,
            )
        if not first:
            shrink = jnp.exp2((before - high) * SCALE2)
            total = total + l_in[:, cols][:, :1] * shrink
            output = output + acc_in[:, cols] * shrink
        if last:
            rest[0][:, cols] = (output / total).astype(rest[0].dtype)
        else:
            rest[0][:, cols] = jnp.broadcast_to(high, output.shape)
            rest[1][:, cols] = jnp.broadcast_to(total, output.shape)
            rest[2][:, cols] = output


def flash(bases, limit, query, blocks, state, last):
    rows, width = query.shape
    n_blocks = len(blocks)
    whole = pl.BlockSpec(query.shape, lambda i: (0, 0))
    count = blocks[0][0][0].shape[0]

    def part(item):
        return pl.BlockSpec((count, width), lambda i: (0, item[1]))

    in_specs = [
        pl.BlockSpec(memory_space=pltpu.SMEM),
        pl.BlockSpec(limit.shape, lambda i: (0, 0)),
        whole,
    ]
    in_specs += [part(key) for key, _ in blocks] + [part(value) for _, value in blocks]
    operands = [bases, limit, query]
    operands += [key[0] for key, _ in blocks] + [value[0] for _, value in blocks]
    if state is not None:
        in_specs += [whole] * 3
        operands += list(state)
    if last:
        out_shape = [jax.ShapeDtypeStruct(query.shape, jnp.bfloat16)]
    else:
        out_shape = [jax.ShapeDtypeStruct(query.shape, jnp.float32)] * 3
    work = rows * count * n_blocks * width
    return pl.pallas_call(
        functools.partial(flash_kernel, n_blocks, state is None, last),
        grid=(1,),
        in_specs=in_specs,
        out_specs=[whole] * len(out_shape),
        out_shape=out_shape,
        compiler_params=pltpu.CompilerParams(vmem_limit_bytes=32 * 1024 * 1024),
        cost_estimate=pl.CostEstimate(
            flops=4 * work,
            bytes_accessed=4 * n_blocks * count * width + 12 * rows * width,
            transcendentals=work // HEAD_DIM,
        ),
    )(*operands)


def project_kernel(sizes, place_ref, *refs):
    tokens, feats, n_rows = sizes
    items, weights = refs[:10], refs[10:19]
    given_ref, kept_ref, act, wts, item_sems, weight_sems = refs[19:]
    z, a, y, c = (place_ref[i] for i in range(4))
    kinds = wts.shape[0]
    width = wts.shape[2]
    copies = []
    for t in range(2):
        top = jnp.where(a == c, t, 1 - t) * tokens
        spots = ((0, 0, tokens), (1, 0, tokens), (3, 0, tokens), (2, 0, tokens // 2), (2, tokens // 2, tokens // 2))
        for n, (hop, low, count) in enumerate(spots):
            row = pl.multiple_of(top + low, tokens // 2)
            col = pl.multiple_of(lax.rem(y + hop, 4) * feats, feats)
            copies.append(pltpu.make_async_copy(
                items[5 * t + n], act.at[pl.ds(row, count), pl.ds(col, feats)], item_sems.at[5 * t + n]
            ))
    spots = [(hop, 0, n_rows) for hop in (0, 1, 7, 2, 6, 3, 5)]
    spots += [(4, 0, n_rows // 2), (4, n_rows // 2, n_rows // 2)]
    loads = []
    for kind in range(kinds):
        group = []
        for n, (hop, low, count) in enumerate(spots):
            row = pl.multiple_of(lax.rem(z + hop, 8) * n_rows + low, n_rows // 2)
            group.append(pltpu.make_async_copy(
                weights[n].at[kind], wts.at[kind, pl.ds(row, count)], weight_sems.at[kind, n]
            ))
        loads.append(group)
    for copy in copies:
        copy.start()
    for group in loads:
        for copy in group:
            copy.start()
    for copy in copies:
        copy.wait()
    for kind in range(kinds):
        for copy in loads[kind]:
            copy.wait()
        cols = slice(kind * width, (kind + 1) * width)
        given_ref[:, cols] = jnp.dot(
            act[tokens:, :], wts[kind], preferred_element_type=jnp.float32
        ).astype(given_ref.dtype)
        kept_ref[:, cols] = jnp.dot(act[:tokens, :], wts[kind], preferred_element_type=jnp.float32)


def project(place, items, weights):
    tokens, feats = items[0].shape
    kinds, n_rows, width = weights[0].shape
    anywhere = pl.BlockSpec(memory_space=pl.ANY)
    return pl.pallas_call(
        functools.partial(project_kernel, (tokens, feats, n_rows)),
        in_specs=[pl.BlockSpec(memory_space=pltpu.SMEM)] + [anywhere] * 19,
        out_specs=[pl.BlockSpec(memory_space=pltpu.VMEM)] * 2,
        out_shape=[
            jax.ShapeDtypeStruct((tokens, kinds * width), jnp.bfloat16),
            jax.ShapeDtypeStruct((tokens, kinds * width), jnp.float32),
        ],
        scratch_shapes=[
            pltpu.VMEM((2 * tokens, 4 * feats), jnp.bfloat16),
            pltpu.VMEM((kinds, 8 * n_rows, width), jnp.bfloat16),
            pltpu.SemaphoreType.DMA((10,)),
            pltpu.SemaphoreType.DMA((kinds, 9)),
        ],
        compiler_params=pltpu.CompilerParams(vmem_limit_bytes=32 * 1024 * 1024),
        cost_estimate=pl.CostEstimate(
            flops=2 * 2 * tokens * 8 * n_rows * kinds * width,
            bytes_accessed=2 * (2 * tokens * 4 * feats + kinds * width * 8 * n_rows) + 6 * tokens * kinds * width,
            transcendentals=0,
        ),
    )(place, *items, *weights)


def out_kernel(adds, index_ref, left_ref, *refs):
    weights, rest = refs[:4], refs[4:]
    for hop in range(4):
        value = jnp.dot(left_ref[...], weights[hop][...], preferred_element_type=jnp.float32)
        if adds:
            value = value + rest[0][hop].astype(jnp.float32)
            rest[1 + hop][...] = value.astype(rest[1 + hop].dtype)
        else:
            rest[0][hop] = value.astype(rest[0].dtype)


def out_project(index, left, right, feats, came=None):
    tokens, depth = left.shape

    def columns(hop):
        return pl.BlockSpec((depth, feats), lambda i, where: (0, where[hop]))

    flat = pl.BlockSpec((tokens, feats), lambda i, where: (0, 0))
    deep = pl.BlockSpec((4, tokens, feats), lambda i, where: (0, 0, 0))
    in_specs = [pl.BlockSpec(left.shape, lambda i, where: (0, 0))] + [columns(hop) for hop in range(4)]
    operands = [index, left] + [right] * 4
    if came is None:
        out_shape, out_specs = jax.ShapeDtypeStruct((4, tokens, feats), jnp.bfloat16), deep
    else:
        in_specs.append(deep)
        operands.append(came)
        out_shape = [jax.ShapeDtypeStruct((tokens, feats), jnp.bfloat16 if hop else jnp.float32) for hop in range(4)]
        out_specs = [flat] * 4
    return pl.pallas_call(
        functools.partial(out_kernel, came is not None),
        grid_spec=pltpu.PrefetchScalarGridSpec(
            num_scalar_prefetch=1, grid=(1,), in_specs=in_specs, out_specs=out_specs
        ),
        out_shape=out_shape,
        compiler_params=pltpu.CompilerParams(vmem_limit_bytes=32 * 1024 * 1024),
        cost_estimate=pl.CostEstimate(
            flops=2 * tokens * depth * 4 * feats,
            bytes_accessed=2 * 4 * feats * (depth + 2 * tokens),
            transcendentals=0,
        ),
    )(*operands)


def tied(*values):
    return lax.optimization_barrier(values)


def both_ways(ahead, behind, axis):
    return shifted(ahead, axis, 1), shifted(behind, axis, -1)


def local(states, noise, span_lengths, step_index, gain, in_weights, out_weights):
    tokens_here, feats = states.shape[1:]
    group = lax.axis_index("grp")
    z, a, y, c = (lax.axis_index(name) for name in ("z", "a", "y", "c"))
    lengths = span_lengths[0]
    ends = span_ends(lengths)
    here = jnp.arange(tokens_here, dtype=jnp.int32)

    rows = crossed(jnp.transpose(in_weights[0], (1, 0, 2)))

    positions = (z * 2 + a) * tokens_here + here
    spans = jnp.sum((positions[:, None] >= ends[None, :]).astype(jnp.int32), axis=1)
    hits = spans[:, None] == jnp.arange(lengths.shape[0], dtype=jnp.int32)[None, :]
    picked = jnp.where(hits, (step_index[0][None, :] + 1).astype(jnp.float32), jnp.float32(0.0))
    times = (jnp.sum(picked, axis=1) / STEPS)[:, None]
    state = states[0].astype(jnp.float32)
    mixed = ((1.0 - times) * state + times * noise[0].astype(jnp.float32)).astype(jnp.bfloat16)
    wide = mixed.astype(jnp.float32)
    squares = lax.psum(jnp.sum(wide * wide, axis=1), ("y", "c"))
    own_gain = lax.dynamic_index_in_dim(gain[0].reshape(8, feats), y * 2 + c, 0, keepdims=True)
    scaled = (wide * own_gain).astype(jnp.bfloat16)

    half = feats // 2
    kept = jnp.where(c == 0, scaled[:, :half], scaled[:, half:])
    given = jnp.where(c == 0, scaled[:, half:], scaled[:, :half])
    taken = shifted(given, "c", 1)
    mine = jnp.concatenate([jnp.where(c == 0, kept, taken), jnp.where(c == 0, taken, kept)], axis=1)
    mine_out, rows = tied(mine, rows)
    other = shifted(mine_out, "a", 1)

    def around_y(block):
        ahead, behind = both_ways(block, block, "y")
        middle = block.shape[0] // 2
        far = both_ways(ahead[:middle], behind[middle:], "y")
        return [block, ahead, behind, *far]

    n_rows = rows.shape[1]
    weights = [rows]
    ahead, behind = rows, rows
    for _ in range(3):
        ahead, behind = both_ways(ahead, behind, "z")
        weights += [ahead, behind]
    weights += both_ways(ahead[:, :n_rows // 2], behind[:, n_rows // 2:], "z")

    items = around_y(mine) + around_y(other)
    place = jnp.stack([z, a, y, c]).astype(jnp.int32)
    given, kept = project(place, items, weights)
    inverse_root = crossed(lax.rsqrt(squares / (feats * 8) + 1e-06))[:, None]
    came = shifted(given, "c", 1)
    projected = ((kept + came.astype(jnp.float32)) * inverse_root).astype(jnp.bfloat16)
    cols = projected.shape[1] // 3
    query, pairs = projected[:, :cols], projected[:, cols:]

    places = (z * 2 + c) * tokens_here + here
    limit = jnp.min(
        jnp.where(ends[None, :] > places[:, None], ends[None, :], ends[-1]), axis=1
    )
    limit = jnp.where(group == 1, ends[-1], limit).astype(jnp.int32)[:, None]

    def attend(hops, got, stat):
        blocks, bases = [], []
        for hop, pair in zip(hops, got):
            swapped = [shifted(part, "c", 1) for part in pair]
            if len(pair) == 1:
                blocks += [((pair[0], 0), (pair[0], 1)), ((swapped[0], 0), (swapped[0], 1))]
            else:
                blocks += [((pair[0], 0), (pair[1], 0)), ((swapped[0], 0), (swapped[1], 0))]
            start = ((z + hop) % 8) * 2
            bases += [(start + c) * tokens_here, (start + 1 - c) * tokens_here]
        return flash(jnp.stack(bases), limit, query, blocks, stat, hops == (4,))

    ahead, behind = both_ways(pairs, pairs, "z")
    stat = attend((0,), ((pairs,),), None)
    for hop in (1, 2):
        ahead, behind, *stat = tied(ahead, behind, *stat)
        onward = both_ways(ahead, behind, "z")
        stat = attend((hop, -hop), ((ahead,), (behind,)), stat)
        ahead, behind = onward
    ahead, behind, *stat = tied(ahead, behind, *stat)
    onward = both_ways(ahead[:, :cols], behind[:, cols:], "z")
    stat = attend((3, -3), ((ahead,), (behind,)), stat)
    attended = crossed(attend((4,), (onward,), stat)[0])

    hops = jnp.arange(4, dtype=jnp.int32)
    index = ((y + hops) % 4) * 2
    sent = out_project(index + 1 - c, attended, out_weights[0], feats)
    held = out_project(index + c, attended, out_weights[0], feats, shifted(sent, "c", 1))
    velocity = held[0]
    for hop in (1, 3, 2):
        velocity = velocity + shifted(held[hop], "y", -hop).astype(jnp.float32)
    estimate = mixed.astype(jnp.float32) - times * velocity
    result = jnp.where(group == 0, estimate, state - estimate).astype(jnp.bfloat16)
    return shifted(result, "grp", 1)[None]


def solution(mesh):
    fine = jax.sharding.Mesh(mesh.devices.reshape(2, 8, 2, 4, 2), ("grp", "z", "a", "y", "c"))
    tokens, features = ("z", "a"), ("y", "c")
    return jax.shard_map(
        local,
        mesh=fine,
        in_specs=(
            P("grp", tokens, features),
            P("grp", tokens, features),
            P("grp", None),
            P("grp", None),
            P("grp", None),
            P("grp", tokens, None, features),
            P("grp", features, None),
        ),
        out_specs=P("grp", tokens, features),
        check_vma=False,
    )
```

```python
import functools

import jax
import jax.numpy as jnp
from jax import lax
from jax.experimental import pallas as pl
from jax.experimental.pallas import tpu as pltpu
from jax.sharding import PartitionSpec as P

HEAD_DIM = 128
STEPS = 4
LOW = -1e30
SCALE2 = HEAD_DIM ** (-0.5) * 1.4426950408889634


def crossed(block):
    return lax.ppermute(block, ("a", "c"), [(0, 0), (1, 2), (2, 1), (3, 3)])


def shifted(block, axis, hop):
    count = lax.axis_size(axis)
    return lax.ppermute(block, axis, [(i, (i - hop) % count) for i in range(count)])


def swapped(block):
    return shifted(block, "c", 1)


def both_ways(ahead, behind, axis):
    return shifted(ahead, axis, 1), shifted(behind, axis, -1)


def tied(*values):
    return lax.optimization_barrier(values)


def params():
    return pltpu.CompilerParams(vmem_limit_bytes=32 * 1024 * 1024)


def in_vmem():
    return pl.BlockSpec(memory_space=pltpu.VMEM)


def lay_kernel(order_ref, x_ref, gain_ref, out_ref, square_ref):
    wide = x_ref[0].astype(jnp.float32)
    out_ref[...] = (wide * gain_ref[0]).astype(out_ref.dtype)
    square = jnp.sum(wide * wide, axis=1, keepdims=True)

    @pl.when(pl.program_id(0) == 0)
    def _():
        square_ref[...] = square

    @pl.when(pl.program_id(0) > 0)
    def _():
        square_ref[...] += square


def lay(x, gain, row):
    blocks, tokens, feats = x.shape
    return pl.pallas_call(
        lay_kernel,
        grid=(blocks,),
        in_specs=[
            pl.BlockSpec(memory_space=pltpu.SMEM),
            pl.BlockSpec((1, tokens, feats), lambda i: (i, 0, 0)),
            pl.BlockSpec((1, 1, feats), lambda i: (i, 0, 0)),
        ],
        out_specs=[
            pl.BlockSpec((tokens, feats), lambda i: (0, i)),
            pl.BlockSpec((tokens, 1), lambda i: (0, 0)),
        ],
        out_shape=[
            jax.ShapeDtypeStruct((tokens, blocks * feats), jnp.bfloat16),
            jax.ShapeDtypeStruct((tokens, 1), jnp.float32),
        ],
        compiler_params=params(),
        cost_estimate=pl.CostEstimate(
            flops=3 * x.size, bytes_accessed=4 * x.size, transcendentals=0
        ),
    )(row, x, gain)


def early_kernel(place_ref, mine_ref, other_ref, *refs):
    weights, (out_ref, wts, sems) = refs[:-3], refs[-3:]
    z, a = place_ref[0], place_ref[1]
    kinds, total, width = wts.shape
    tokens = mine_ref.shape[0]
    count = weights[0].shape[1]
    loads = []
    for kind in range(kinds):
        group = []
        for n, hop in enumerate((0, 1, 7, 2, 6, 3, 5)):
            for part in range(2):
                block = lax.rem(z + hop, 8) * 2 + (a if part == 0 else 1 - a)
                group.append(pltpu.make_async_copy(
                    weights[2 * n + part].at[kind],
                    wts.at[kind, pl.ds(pl.multiple_of(block * count, count), count)],
                    sems.at[kind, 2 * n + part],
                ))
        loads.append(group)
    for group in loads:
        for copy in group:
            copy.start()
    hole = pl.ds(pl.multiple_of(lax.rem(z + 4, 8) * 2 * count, 2 * count), 2 * count)
    for kind in range(kinds):
        wts[kind, hole, :] = jnp.zeros((2 * count, width), wts.dtype)
    for kind in range(kinds):
        for copy in loads[kind]:
            copy.wait()
        cols = slice(kind * width, (kind + 1) * width)
        out_ref[0, :, cols] = jnp.dot(mine_ref[...], wts[kind], preferred_element_type=jnp.float32)
        out_ref[1, :, cols] = jnp.dot(other_ref[...], wts[kind], preferred_element_type=jnp.float32)


def late_kernel(place_ref, part_ref, mine_ref, other_ref, first_ref, second_ref,
                given_ref, kept_ref, wts, act, sems):
    z, a, c = place_ref[0], place_ref[1], place_ref[2]
    kinds, _, width = wts.shape
    feats = act.shape[2]
    count = first_ref.shape[1]
    far = lax.rem(z + 4, 8)
    window = pl.ds(pl.multiple_of(far // 2 * feats, feats), feats)
    low = lax.rem(far, 2) * 2 * count
    copies = [
        pltpu.make_async_copy(mine_ref.at[:, window], act.at[0], sems.at[0]),
        pltpu.make_async_copy(other_ref.at[:, window], act.at[1], sems.at[1]),
    ]
    for n, (ref, spot) in enumerate(((first_ref, a), (second_ref, 1 - a))):
        row = pl.multiple_of(low + spot * count, count)
        copies.append(pltpu.make_async_copy(ref, wts.at[:, pl.ds(row, count)], sems.at[2 + n]))
    for copy in copies:
        copy.start()
    rest = pl.multiple_of(2 * count - low, 2 * count)
    for kind in range(kinds):
        wts[kind, pl.ds(rest, 2 * count), :] = jnp.zeros((2 * count, width), wts.dtype)
    for copy in copies:
        copy.wait()
    home = jnp.where(a == c, 0, 1)
    for kind in range(kinds):
        cols = slice(kind * width, (kind + 1) * width)
        value = part_ref[1 - home, :, cols] + jnp.dot(
            act[1 - home], wts[kind], preferred_element_type=jnp.float32
        )
        given_ref[:, cols] = value.astype(given_ref.dtype)
    for kind in range(kinds):
        cols = slice(kind * width, (kind + 1) * width)
        kept_ref[:, cols] = part_ref[home, :, cols] + jnp.dot(
            act[home], wts[kind], preferred_element_type=jnp.float32
        )


def project_early(place, mine, other, weights):
    tokens, feats = mine.shape
    kinds, count, width = weights[0].shape
    return pl.pallas_call(
        early_kernel,
        in_specs=[pl.BlockSpec(memory_space=pltpu.SMEM)] + [in_vmem()] * 2
        + [pl.BlockSpec(memory_space=pl.ANY)] * 14,
        out_specs=in_vmem(),
        out_shape=jax.ShapeDtypeStruct((2, tokens, kinds * width), jnp.float32),
        scratch_shapes=[
            pltpu.VMEM((kinds, feats, width), jnp.bfloat16),
            pltpu.SemaphoreType.DMA((kinds, 14)),
        ],
        compiler_params=params(),
        cost_estimate=pl.CostEstimate(
            flops=4 * tokens * feats * kinds * width,
            bytes_accessed=2 * (2 * tokens * feats + kinds * width * feats) + 8 * tokens * kinds * width,
            transcendentals=0,
        ),
    )(place, mine, other, *weights)


def project_late(place, part, mine, other, first, second):
    tokens = mine.shape[0]
    kinds, count, width = first.shape
    anywhere = pl.BlockSpec(memory_space=pl.ANY)
    return pl.pallas_call(
        late_kernel,
        in_specs=[pl.BlockSpec(memory_space=pltpu.SMEM), in_vmem()] + [anywhere] * 4,
        out_specs=[in_vmem()] * 2,
        out_shape=[
            jax.ShapeDtypeStruct((tokens, kinds * width), jnp.bfloat16),
            jax.ShapeDtypeStruct((tokens, kinds * width), jnp.float32),
        ],
        scratch_shapes=[
            pltpu.VMEM((kinds, 4 * count, width), jnp.bfloat16),
            pltpu.VMEM((2, tokens, 4 * count), jnp.bfloat16),
            pltpu.SemaphoreType.DMA((4,)),
        ],
        compiler_params=params(),
        cost_estimate=pl.CostEstimate(
            flops=16 * tokens * count * kinds * width,
            bytes_accessed=14 * tokens * kinds * width,
            transcendentals=0,
        ),
    )(place, part, mine, other, first, second)


def finish_kernel(kept_ref, came_ref, scale_ref, *outs):
    width = outs[0].shape[1]
    for n, out in enumerate(outs):
        cols = slice(n * width, (n + 1) * width)
        value = (kept_ref[:, cols] + came_ref[:, cols].astype(jnp.float32)) * scale_ref[...]
        out[...] = value.astype(out.dtype)


def finish(kept, came, scale):
    tokens, width = kept.shape
    return pl.pallas_call(
        finish_kernel,
        in_specs=[in_vmem()] * 3,
        out_specs=[in_vmem()] * 3,
        out_shape=[jax.ShapeDtypeStruct((tokens, width // 3), jnp.bfloat16)] * 3,
        compiler_params=params(),
        cost_estimate=pl.CostEstimate(
            flops=2 * kept.size, bytes_accessed=8 * kept.size, transcendentals=0
        ),
    )(kept, came, scale)


def flash_kernel(n_blocks, first, last, base_ref, limit_ref, *refs):
    queries, refs = refs[:2], refs[2:]
    keys, values, rest = refs[:n_blocks], refs[n_blocks:2 * n_blocks], refs[2 * n_blocks:]
    if not first:
        acc_in, stat_in = rest[:2]
        rest = rest[2:]
    rows, width = queries[0].shape
    heads = width // HEAD_DIM
    for side in range(2):
        span = slice(side * rows, (side + 1) * rows)
        limit = limit_ref[span, :]
        for head in range(heads):
            cols = slice(head * HEAD_DIM, (head + 1) * HEAD_DIM)
            query = queries[side][:, cols]
            scores = []
            for block in range(n_blocks):
                score = lax.dot_general(
                    query, keys[block][:, cols], (((1,), (1,)), ((), ())),
                    preferred_element_type=jnp.float32,
                )
                place = lax.broadcasted_iota(jnp.int32, score.shape, 1)
                scores.append(jnp.where(place < limit - base_ref[block], score, LOW))
            high = functools.reduce(
                jnp.maximum, [jnp.max(score, axis=1, keepdims=True) for score in scores]
            )
            if not first:
                before = stat_in[span, head:head + 1]
                high = jnp.maximum(high, before)
            shift = high * SCALE2
            total, output = 0.0, 0.0
            for block in range(n_blocks):
                weight = jnp.exp2(scores[block] * SCALE2 - shift)
                total = total + jnp.sum(weight, axis=1, keepdims=True)
                output = output + jnp.dot(
                    weight.astype(jnp.bfloat16), values[block][:, cols],
                    preferred_element_type=jnp.float32,
                )
            if not first:
                shrink = jnp.exp2((before - high) * SCALE2)
                total = total + stat_in[span, heads + head:heads + head + 1] * shrink
                output = output + acc_in[span, cols] * shrink
            if last:
                spots = (slice(width + head, width + head + 1),
                         slice(width + heads + head, width + heads + head + 1))
                rest[side][:, cols] = output
                rest[side][:, spots[0]] = high
                rest[side][:, spots[1]] = total
            else:
                rest[0][span, cols] = output
                rest[1][span, head:head + 1] = high
                rest[1][span, heads + head:heads + head + 1] = total


def flash(bases, limit, queries, blocks, stat, last):
    rows, width = queries[0].shape
    n_blocks = len(blocks)
    count = blocks[0][0].shape[0]
    operands = [bases, limit, *queries]
    operands += [key for key, _ in blocks] + [value for _, value in blocks]
    operands += [] if stat is None else list(stat)
    if last:
        out_shape = [jax.ShapeDtypeStruct((rows, width + 128), jnp.float32)] * 2
    else:
        out_shape = [
            jax.ShapeDtypeStruct((2 * rows, width), jnp.float32),
            jax.ShapeDtypeStruct((2 * rows, 128), jnp.float32),
        ]
    work = 2 * rows * count * n_blocks * width
    return pl.pallas_call(
        functools.partial(flash_kernel, n_blocks, stat is None, last),
        in_specs=[pl.BlockSpec(memory_space=pltpu.SMEM)] + [in_vmem()] * (len(operands) - 1),
        out_specs=[in_vmem()] * 2,
        out_shape=out_shape,
        compiler_params=params(),
        cost_estimate=pl.CostEstimate(
            flops=4 * work,
            bytes_accessed=4 * n_blocks * count * width + 20 * rows * width,
            transcendentals=work // HEAD_DIM,
        ),
    )(*operands)


def merge_kernel(one_ref, two_ref, out_ref):
    width = out_ref.shape[1]
    heads = width // HEAD_DIM
    for head in range(heads):
        cols = slice(head * HEAD_DIM, (head + 1) * HEAD_DIM)
        top = slice(width + head, width + head + 1)
        low = slice(width + heads + head, width + heads + head + 1)
        high = jnp.maximum(one_ref[:, top], two_ref[:, top])
        one = jnp.exp2((one_ref[:, top] - high) * SCALE2)
        two = jnp.exp2((two_ref[:, top] - high) * SCALE2)
        total = one_ref[:, low] * one + two_ref[:, low] * two
        value = (one_ref[:, cols] * one + two_ref[:, cols] * two) / total
        out_ref[:, cols] = value.astype(out_ref.dtype)


def merge(one, two):
    rows, width = one.shape
    return pl.pallas_call(
        merge_kernel,
        in_specs=[in_vmem()] * 2,
        out_specs=in_vmem(),
        out_shape=jax.ShapeDtypeStruct((rows, width - 128), jnp.bfloat16),
        compiler_params=params(),
        cost_estimate=pl.CostEstimate(flops=4 * one.size, bytes_accessed=10 * one.size, transcendentals=0),
    )(one, two)


def out_kernel(hops, adds, index_ref, left_ref, *refs):
    weights, rest = refs[:hops], refs[hops:]
    for hop in range(hops):
        value = jnp.dot(left_ref[...], weights[hop][...], preferred_element_type=jnp.float32)
        if adds:
            value = value + rest[hop][...].astype(jnp.float32)
            rest[hops + hop][...] = value.astype(rest[hops + hop].dtype)
        else:
            rest[hop][...] = value.astype(rest[hop].dtype)


def out_project(index, left, right, feats, hops, came=(), held=jnp.bfloat16):
    tokens, depth = left.shape

    def columns(hop):
        return pl.BlockSpec((depth, feats), lambda i, where: (0, where[hop]))

    flat = pl.BlockSpec((tokens, feats), lambda i, where: (0, 0))
    return pl.pallas_call(
        functools.partial(out_kernel, hops, bool(came)),
        grid_spec=pltpu.PrefetchScalarGridSpec(
            num_scalar_prefetch=1,
            grid=(1,),
            in_specs=[pl.BlockSpec(left.shape, lambda i, where: (0, 0))]
            + [columns(hop) for hop in range(hops)] + [flat] * len(came),
            out_specs=[flat] * hops,
        ),
        out_shape=[jax.ShapeDtypeStruct((tokens, feats), held)] * hops,
        compiler_params=params(),
        cost_estimate=pl.CostEstimate(
            flops=2 * tokens * depth * hops * feats,
            bytes_accessed=2 * hops * feats * (depth + 2 * tokens),
            transcendentals=0,
        ),
    )(index, left, *[right] * hops, *came)


def local(states, noise, span_lengths, step_index, gain, in_weights, out_weights):
    tokens_here, feats = states.shape[1:]
    group = lax.axis_index("grp")
    z, a, y, c = (lax.axis_index(name) for name in ("z", "a", "y", "c"))
    home = a == c
    lengths = span_lengths[0]
    ends = jnp.cumsum(lengths)
    here = jnp.arange(tokens_here, dtype=jnp.int32)
    place = jnp.stack([z, a, c]).astype(jnp.int32)

    rows = jnp.transpose(in_weights[0], (1, 0, 2))
    count = rows.shape[1] // 2
    same = jnp.where(c == 0, rows[:, :count], rows[:, count:])
    opposite = jnp.where(c == 0, rows[:, count:], rows[:, :count])
    first = jnp.where(home, same, swapped(opposite))
    second = jnp.where(
        home,
        lax.ppermute(same, ("a", "c"), [(1, 3), (2, 0)]),
        lax.ppermute(opposite, ("a", "c"), [(1, 2), (2, 1)]),
    )

    positions = (z * 2 + a) * tokens_here + here
    spans = jnp.sum((positions[:, None] >= ends[None, :]).astype(jnp.int32), axis=1)
    hits = spans[:, None] == jnp.arange(lengths.shape[0], dtype=jnp.int32)[None, :]
    picked = jnp.where(hits, (step_index[0][None, :] + 1).astype(jnp.float32), jnp.float32(0.0))
    times = (jnp.sum(picked, axis=1) / STEPS)[:, None]
    state = states[0].astype(jnp.float32)
    mixed = ((1.0 - times) * state + times * noise[0].astype(jnp.float32)).astype(jnp.bfloat16)

    quarters = [mixed[:, i * count:(i + 1) * count] for i in range(4)]
    kept = jnp.concatenate([jnp.where(c == 0, quarters[2 * i], quarters[2 * i + 1]) for i in range(2)], axis=1)
    given = jnp.concatenate([jnp.where(c == 0, quarters[2 * i + 1], quarters[2 * i]) for i in range(2)], axis=1)
    taken = swapped(given)
    mine = jnp.concatenate([jnp.where(c == 0, kept, taken), jnp.where(c == 0, taken, kept)], axis=1)
    other = shifted(tied(mine, second)[0], "a", 1)
    own_gain = gain[0].reshape(8, 2, 2, count)
    own_gain = jnp.where(c == 0, own_gain[:, :, 0], own_gain[:, :, 1]).reshape(4, 1, feats)
    laid_mine, squares_mine = lay(lax.all_gather(mine, "y"), own_gain, place)
    laid_other, squares_other = lay(lax.all_gather(other, "y"), own_gain, place)
    squares = jnp.where(home, squares_mine, squares_other)
    squares = squares + swapped(jnp.where(home, squares_other, squares_mine))
    inverse_root = lax.rsqrt(squares / (feats * 8) + 1e-06)

    early = [first, second]
    chunks = [(first, first), (second, second)]
    for _ in range(3):
        chunks = [both_ways(*chunk, "z") for chunk in chunks]
        early += [chunks[0][0], chunks[1][0], chunks[0][1], chunks[1][1]]
    first, second = both_ways(chunks[0][0], chunks[1][1], "z")
    part = project_early(place, laid_mine, laid_other, early)
    given, kept = project_late(place, part, laid_mine, laid_other, first, second)
    query, key, value = finish(kept, swapped(given), inverse_root)

    queries = (query, swapped(query))
    places = jnp.concatenate([(z * 2 + c) * tokens_here + here, (z * 2 + 1 - c) * tokens_here + here])
    limit = jnp.min(
        jnp.where(ends[None, :] > places[:, None], ends[None, :], ends[-1]), axis=1
    )
    limit = jnp.where(group == 1, ends[-1], limit).astype(jnp.int32)[:, None]

    def attend(hops, blocks, stat):
        bases = [(((z + hop) % 8) * 2 + c) * tokens_here for hop in hops]
        return flash(jnp.stack(bases), limit, queries, blocks, stat, hops == (4,))

    chunks = [(key, key), (value, value)]
    onward = [both_ways(*chunk, "z") for chunk in chunks]
    stat = attend((0,), [(key, value)], None)
    for hop in (1, 2, 3):
        (keys, values), stat = lax.optimization_barrier((onward, stat))
        if hop < 3:
            onward = [both_ways(*keys, "z"), both_ways(*values, "z")]
        else:
            onward = both_ways(keys[0], values[1], "z")
        stat = attend((hop, -hop), [(keys[0], values[0]), (keys[1], values[1])], stat)
    onward, stat = lax.optimization_barrier((onward, stat))
    ours, theirs = attend((4,), [onward], stat)
    attended = crossed(merge(ours, swapped(theirs)))

    hops = (2, 1, 3, 0)
    index = ((y + jnp.array(hops, jnp.int32)) % 4) * 2
    sent = out_project(index + 1 - c, attended, out_weights[0], feats, 4)
    velocity = 0.0
    for n, hop in enumerate(hops):
        came = swapped(sent[n])
        held = out_project(
            index[n:n + 1] + c, attended, out_weights[0], feats, 1, (came,),
            jnp.bfloat16 if hop else jnp.float32,
        )[0]
        if hop:
            held = shifted(held, "y", -hop).astype(jnp.float32)
        velocity = velocity + held
    estimate = mixed.astype(jnp.float32) - times * velocity
    result = jnp.where(group == 0, estimate, state - estimate).astype(jnp.bfloat16)
    return shifted(result, "grp", 1)[None]


def solution(mesh):
    fine = jax.sharding.Mesh(mesh.devices.reshape(2, 8, 2, 4, 2), ("grp", "z", "a", "y", "c"))
    tokens, features = ("z", "a"), ("y", "c")
    return jax.shard_map(
        local,
        mesh=fine,
        in_specs=(
            P("grp", tokens, features),
            P("grp", tokens, features),
            P("grp", None),
            P("grp", None),
            P("grp", None),
            P("grp", tokens, None, features),
            P("grp", features, None),
        ),
        out_specs=P("grp", tokens, features),
        check_vma=False,
    )
```

```python
import functools

import jax
import jax.numpy as jnp
from jax import lax
from jax.experimental import pallas as pl
from jax.experimental.pallas import tpu as pltpu
from jax.sharding import PartitionSpec as P

HEAD_DIM = 128
STEPS = 4
LOW = -1e30
SCALE2 = HEAD_DIM ** (-0.5) * 1.4426950408889634


def crossed(block):
    return lax.ppermute(block, ("a", "c"), [(0, 0), (1, 2), (2, 1), (3, 3)])


def shifted(block, axis, hop):
    count = lax.axis_size(axis)
    return lax.ppermute(block, axis, [(i, (i - hop) % count) for i in range(count)])


def swapped(block):
    return shifted(block, "c", 1)


def both_ways(ahead, behind, axis):
    return shifted(ahead, axis, 1), shifted(behind, axis, -1)


def tied(*values):
    return lax.optimization_barrier(values)


def params():
    return pltpu.CompilerParams(vmem_limit_bytes=32 * 1024 * 1024)


def in_vmem():
    return pl.BlockSpec(memory_space=pltpu.VMEM)


def lay_kernel(blocks, order_ref, gain_ref, *refs):
    x_refs, out_ref, square_ref = refs[:-2], refs[-2], refs[-1]
    step = pl.program_id(0)
    for n, x_ref in enumerate(x_refs):

        @pl.when(step == n if len(x_refs) > 1 else step >= 0)
        def _():
            wide = x_ref[...].reshape(out_ref.shape).astype(jnp.float32)
            out_ref[...] = (wide * gain_ref[0]).astype(out_ref.dtype)
            square = jnp.sum(wide * wide, axis=1, keepdims=True)
            square_ref[...] = jnp.where(step == 0, square, square_ref[...] + square)


def lay(xs, gain, order):
    blocks = gain.shape[0]
    tokens, feats = xs[0].shape[-2:]
    if len(xs) == 1:
        specs = [pl.BlockSpec((1, tokens, feats), lambda i, where: (i, 0, 0))]
    else:
        specs = [pl.BlockSpec((tokens, feats), lambda i, where: (0, 0))] * blocks
    return pl.pallas_call(
        functools.partial(lay_kernel, blocks),
        grid_spec=pltpu.PrefetchScalarGridSpec(
            num_scalar_prefetch=1,
            grid=(blocks,),
            in_specs=[pl.BlockSpec((1, 1, feats), lambda i, where: (where[i], 0, 0))] + specs,
            out_specs=[
                pl.BlockSpec((tokens, feats), lambda i, where: (0, where[i])),
                pl.BlockSpec((tokens, 1), lambda i, where: (0, 0)),
            ],
        ),
        out_shape=[
            jax.ShapeDtypeStruct((tokens, blocks * feats), jnp.bfloat16),
            jax.ShapeDtypeStruct((tokens, 1), jnp.float32),
        ],
        compiler_params=params(),
        cost_estimate=pl.CostEstimate(
            flops=3 * blocks * tokens * feats, bytes_accessed=4 * blocks * tokens * feats, transcendentals=0
        ),
    )(order, gain, *xs)


def early_kernel(place_ref, mine_ref, other_ref, *refs):
    weights, (out_ref, wts, sems) = refs[:-3], refs[-3:]
    z, a = place_ref[0], place_ref[1]
    kinds, total, width = wts.shape
    tokens = mine_ref.shape[0]
    count = weights[0].shape[1]
    loads = []
    for kind in range(kinds):
        group = []
        for n, hop in enumerate((0, 1, 7, 2, 6, 3, 5)):
            for part in range(2):
                block = lax.rem(z + hop, 8) * 2 + (a if part == 0 else 1 - a)
                group.append(pltpu.make_async_copy(
                    weights[2 * n + part].at[kind],
                    wts.at[kind, pl.ds(pl.multiple_of(block * count, count), count)],
                    sems.at[kind, 2 * n + part],
                ))
        loads.append(group)
    for group in loads:
        for copy in group:
            copy.start()
    hole = pl.ds(pl.multiple_of(lax.rem(z + 4, 8) * 2 * count, 2 * count), 2 * count)
    for kind in range(kinds):
        wts[kind, hole, :] = jnp.zeros((2 * count, width), wts.dtype)
    for kind in range(kinds):
        for copy in loads[kind]:
            copy.wait()
        cols = slice(kind * width, (kind + 1) * width)
        out_ref[0, :, cols] = jnp.dot(mine_ref[...], wts[kind], preferred_element_type=jnp.float32)
        out_ref[1, :, cols] = jnp.dot(other_ref[...], wts[kind], preferred_element_type=jnp.float32)


def late_kernel(place_ref, part_ref, mine_ref, other_ref, first_ref, second_ref,
                given_ref, kept_ref, wts, act, sems):
    z, a, c = place_ref[0], place_ref[1], place_ref[2]
    kinds, _, width = wts.shape
    feats = act.shape[2]
    count = first_ref.shape[1]
    far = lax.rem(z + 4, 8)
    window = pl.ds(pl.multiple_of(far // 2 * feats, feats), feats)
    low = lax.rem(far, 2) * 2 * count
    copies = [
        pltpu.make_async_copy(mine_ref.at[:, window], act.at[0], sems.at[0]),
        pltpu.make_async_copy(other_ref.at[:, window], act.at[1], sems.at[1]),
    ]
    for n, (ref, spot) in enumerate(((first_ref, a), (second_ref, 1 - a))):
        row = pl.multiple_of(low + spot * count, count)
        copies.append(pltpu.make_async_copy(ref, wts.at[:, pl.ds(row, count)], sems.at[2 + n]))
    for copy in copies:
        copy.start()
    rest = pl.multiple_of(2 * count - low, 2 * count)
    for kind in range(kinds):
        wts[kind, pl.ds(rest, 2 * count), :] = jnp.zeros((2 * count, width), wts.dtype)
    for copy in copies:
        copy.wait()
    home = jnp.where(a == c, 0, 1)
    for kind in range(kinds):
        cols = slice(kind * width, (kind + 1) * width)
        value = part_ref[1 - home, :, cols] + jnp.dot(
            act[1 - home], wts[kind], preferred_element_type=jnp.float32
        )
        given_ref[:, cols] = value.astype(given_ref.dtype)
    for kind in range(kinds):
        cols = slice(kind * width, (kind + 1) * width)
        kept_ref[:, cols] = part_ref[home, :, cols] + jnp.dot(
            act[home], wts[kind], preferred_element_type=jnp.float32
        )


def project_early(place, mine, other, weights):
    tokens, feats = mine.shape
    kinds, count, width = weights[0].shape
    return pl.pallas_call(
        early_kernel,
        in_specs=[pl.BlockSpec(memory_space=pltpu.SMEM)] + [in_vmem()] * 2
        + [pl.BlockSpec(memory_space=pl.ANY)] * 14,
        out_specs=in_vmem(),
        out_shape=jax.ShapeDtypeStruct((2, tokens, kinds * width), jnp.float32),
        scratch_shapes=[
            pltpu.VMEM((kinds, feats, width), jnp.bfloat16),
            pltpu.SemaphoreType.DMA((kinds, 14)),
        ],
        compiler_params=params(),
        cost_estimate=pl.CostEstimate(
            flops=4 * tokens * feats * kinds * width,
            bytes_accessed=2 * (2 * tokens * feats + kinds * width * feats) + 8 * tokens * kinds * width,
            transcendentals=0,
        ),
    )(place, mine, other, *weights)


def project_late(place, part, mine, other, first, second):
    tokens = mine.shape[0]
    kinds, count, width = first.shape
    anywhere = pl.BlockSpec(memory_space=pl.ANY)
    return pl.pallas_call(
        late_kernel,
        in_specs=[pl.BlockSpec(memory_space=pltpu.SMEM), in_vmem()] + [anywhere] * 4,
        out_specs=[in_vmem()] * 2,
        out_shape=[
            jax.ShapeDtypeStruct((tokens, kinds * width), jnp.bfloat16),
            jax.ShapeDtypeStruct((tokens, kinds * width), jnp.float32),
        ],
        scratch_shapes=[
            pltpu.VMEM((kinds, 4 * count, width), jnp.bfloat16),
            pltpu.VMEM((2, tokens, 4 * count), jnp.bfloat16),
            pltpu.SemaphoreType.DMA((4,)),
        ],
        compiler_params=params(),
        cost_estimate=pl.CostEstimate(
            flops=16 * tokens * count * kinds * width,
            bytes_accessed=14 * tokens * kinds * width,
            transcendentals=0,
        ),
    )(place, part, mine, other, first, second)


def finish_kernel(kept_ref, came_ref, scale_ref, *outs):
    for n, out in enumerate(outs):

        @pl.when(pl.program_id(0) == n)
        def _():
            value = (kept_ref[...] + came_ref[...].astype(jnp.float32)) * scale_ref[...]
            out[...] = value.astype(out.dtype)


def finish(kept, came, scale):
    tokens, width = kept.shape
    part = pl.BlockSpec((tokens, width // 3), lambda i: (0, i))
    whole = pl.BlockSpec((tokens, width // 3), lambda i: (0, 0))
    return pl.pallas_call(
        finish_kernel,
        grid=(3,),
        in_specs=[part, part, pl.BlockSpec((tokens, 1), lambda i: (0, 0))],
        out_specs=[whole] * 3,
        out_shape=[jax.ShapeDtypeStruct((tokens, width // 3), jnp.bfloat16)] * 3,
        compiler_params=params(),
        cost_estimate=pl.CostEstimate(
            flops=2 * kept.size, bytes_accessed=8 * kept.size, transcendentals=0
        ),
    )(kept, came, scale)


def flash_kernel(n_blocks, first, last, base_ref, limit_ref, *refs):
    queries, refs = refs[:2], refs[2:]
    keys, values, rest = refs[:n_blocks], refs[n_blocks:2 * n_blocks], refs[2 * n_blocks:]
    if not first:
        acc_in, stat_in = rest[:2]
        rest = rest[2:]
    rows, width = queries[0].shape
    heads = width // HEAD_DIM
    for side in range(2):
        span = slice(side * rows, (side + 1) * rows)
        limit = limit_ref[span, :]
        for head in range(heads):
            cols = slice(head * HEAD_DIM, (head + 1) * HEAD_DIM)
            query = queries[side][:, cols]
            scores = []
            for block in range(n_blocks):
                score = lax.dot_general(
                    query, keys[block][:, cols], (((1,), (1,)), ((), ())),
                    preferred_element_type=jnp.float32,
                )
                place = lax.broadcasted_iota(jnp.int32, score.shape, 1)
                scores.append(jnp.where(place < limit - base_ref[block], score, LOW))
            high = functools.reduce(
                jnp.maximum, [jnp.max(score, axis=1, keepdims=True) for score in scores]
            )
            if not first:
                before = stat_in[span, head:head + 1]
                high = jnp.maximum(high, before)
            shift = high * SCALE2
            total, output = 0.0, 0.0
            for block in range(n_blocks):
                weight = jnp.exp2(scores[block] * SCALE2 - shift)
                total = total + jnp.sum(weight, axis=1, keepdims=True)
                output = output + jnp.dot(
                    weight.astype(jnp.bfloat16), values[block][:, cols],
                    preferred_element_type=jnp.float32,
                )
            if not first:
                shrink = jnp.exp2((before - high) * SCALE2)
                total = total + stat_in[span, heads + head:heads + head + 1] * shrink
                output = output + acc_in[span, cols] * shrink
            if last:
                spots = (slice(width + head, width + head + 1),
                         slice(width + heads + head, width + heads + head + 1))
                rest[side][:, cols] = output
                rest[side][:, spots[0]] = high
                rest[side][:, spots[1]] = total
            else:
                rest[0][span, cols] = output
                rest[1][span, head:head + 1] = high
                rest[1][span, heads + head:heads + head + 1] = total


def flash(bases, limit, queries, blocks, stat, last):
    rows, width = queries[0].shape
    n_blocks = len(blocks)
    count = blocks[0][0].shape[0]
    operands = [bases, limit, *queries]
    operands += [key for key, _ in blocks] + [value for _, value in blocks]
    operands += [] if stat is None else list(stat)
    if last:
        out_shape = [jax.ShapeDtypeStruct((rows, width + 128), jnp.float32)] * 2
    else:
        out_shape = [
            jax.ShapeDtypeStruct((2 * rows, width), jnp.float32),
            jax.ShapeDtypeStruct((2 * rows, 128), jnp.float32),
        ]
    work = 2 * rows * count * n_blocks * width
    return pl.pallas_call(
        functools.partial(flash_kernel, n_blocks, stat is None, last),
        in_specs=[pl.BlockSpec(memory_space=pltpu.SMEM)] + [in_vmem()] * (len(operands) - 1),
        out_specs=[in_vmem()] * 2,
        out_shape=out_shape,
        compiler_params=params(),
        cost_estimate=pl.CostEstimate(
            flops=4 * work,
            bytes_accessed=4 * n_blocks * count * width + 20 * rows * width,
            transcendentals=work // HEAD_DIM,
        ),
    )(*operands)


def merge_kernel(one_ref, two_ref, out_ref):
    width = out_ref.shape[1]
    heads = width // HEAD_DIM
    for head in range(heads):
        cols = slice(head * HEAD_DIM, (head + 1) * HEAD_DIM)
        top = slice(width + head, width + head + 1)
        low = slice(width + heads + head, width + heads + head + 1)
        high = jnp.maximum(one_ref[:, top], two_ref[:, top])
        one = jnp.exp2((one_ref[:, top] - high) * SCALE2)
        two = jnp.exp2((two_ref[:, top] - high) * SCALE2)
        total = one_ref[:, low] * one + two_ref[:, low] * two
        value = (one_ref[:, cols] * one + two_ref[:, cols] * two) / total
        out_ref[:, cols] = value.astype(out_ref.dtype)


def merge(one, two):
    rows, width = one.shape
    return pl.pallas_call(
        merge_kernel,
        in_specs=[in_vmem()] * 2,
        out_specs=in_vmem(),
        out_shape=jax.ShapeDtypeStruct((rows, width - 128), jnp.bfloat16),
        compiler_params=params(),
        cost_estimate=pl.CostEstimate(flops=4 * one.size, bytes_accessed=10 * one.size, transcendentals=0),
    )(one, two)


def result_kernel(n_blocks, teacher_ref, times_ref, mixed_ref, state_ref, *refs):
    lefts, rights, out_ref = refs[:n_blocks], refs[n_blocks:-1], refs[-1]
    velocity = 0.0
    for n in range(n_blocks):
        right = rights[n // 2][n % 2] if len(rights) < n_blocks else rights[n][...]
        velocity = velocity + jnp.dot(lefts[n][...], right, preferred_element_type=jnp.float32)
    estimate = mixed_ref[...].astype(jnp.float32) - times_ref[...] * velocity
    value = jnp.where(teacher_ref[0] == 1, state_ref[...].astype(jnp.float32) - estimate, estimate)
    out_ref[...] = value.astype(out_ref.dtype)


def result_of(teacher, times, mixed, state, lefts, rights):
    tokens, feats = mixed.shape
    depth = lefts[0].shape[1]
    return pl.pallas_call(
        functools.partial(result_kernel, len(lefts)),
        in_specs=[pl.BlockSpec(memory_space=pltpu.SMEM)] + [in_vmem()] * (3 + len(lefts) + len(rights)),
        out_specs=in_vmem(),
        out_shape=jax.ShapeDtypeStruct((tokens, feats), jnp.bfloat16),
        compiler_params=params(),
        cost_estimate=pl.CostEstimate(
            flops=2 * tokens * depth * len(lefts) * feats,
            bytes_accessed=2 * len(lefts) * depth * (tokens + feats) + 6 * tokens * feats,
            transcendentals=0,
        ),
    )(teacher, times, mixed, state, *lefts, *rights)


def local(states, noise, span_lengths, step_index, gain, in_weights, out_weights):
    tokens_here, feats = states.shape[1:]
    group = lax.axis_index("grp")
    z, a, y, c = (lax.axis_index(name) for name in ("z", "a", "y", "c"))
    home = a == c
    lengths = span_lengths[0]
    ends = jnp.cumsum(lengths)
    here = jnp.arange(tokens_here, dtype=jnp.int32)
    place = jnp.stack([z, a, c]).astype(jnp.int32)

    rows = jnp.transpose(in_weights[0], (1, 0, 2))
    count = rows.shape[1] // 2
    same = jnp.where(c == 0, rows[:, :count], rows[:, count:])
    opposite = jnp.where(c == 0, rows[:, count:], rows[:, :count])
    first = jnp.where(home, same, swapped(opposite))
    near = lax.ppermute(same, ("a", "c"), [(1, 3), (2, 0)])
    across = lax.ppermute(opposite, ("a", "c"), [(1, 2), (2, 1)])

    positions = (z * 2 + a) * tokens_here + here
    spans = jnp.sum((positions[:, None] >= ends[None, :]).astype(jnp.int32), axis=1)
    hits = spans[:, None] == jnp.arange(lengths.shape[0], dtype=jnp.int32)[None, :]
    picked = jnp.where(hits, (step_index[0][None, :] + 1).astype(jnp.float32), jnp.float32(0.0))
    times = (jnp.sum(picked, axis=1) / STEPS)[:, None]
    state = states[0].astype(jnp.float32)
    mixed = ((1.0 - times) * state + times * noise[0].astype(jnp.float32)).astype(jnp.bfloat16)

    quarters = [mixed[:, i * count:(i + 1) * count] for i in range(4)]
    kept = jnp.concatenate([jnp.where(c == 0, quarters[2 * i], quarters[2 * i + 1]) for i in range(2)], axis=1)
    given = jnp.concatenate([jnp.where(c == 0, quarters[2 * i + 1], quarters[2 * i]) for i in range(2)], axis=1)
    taken = swapped(given)
    mine = jnp.concatenate([jnp.where(c == 0, kept, taken), jnp.where(c == 0, taken, kept)], axis=1)
    gathered = lax.all_gather(mine, "y")
    other = shifted(mine, "a", 1)
    own_gain = gain[0].reshape(8, 2, 2, count)
    own_gain = jnp.where(c == 0, own_gain[:, :, 0], own_gain[:, :, 1]).reshape(4, 1, feats)

    chunks = [both_ways(first, first, "z"), None]
    *chunks[0], near, across, other = tied(*chunks[0], near, across, other)
    second = jnp.where(home, near, across)
    chunks[1] = both_ways(second, second, "z")
    early = [first, second, chunks[0][0], chunks[1][0], chunks[0][1], chunks[1][1]]
    for _ in range(2):
        chunks = [both_ways(*chunk, "z") for chunk in chunks]
        early += [chunks[0][0], chunks[1][0], chunks[0][1], chunks[1][1]]
    first, second = both_ways(chunks[0][0], chunks[1][1], "z")

    along = jnp.arange(4, dtype=jnp.int32)
    others = [other] + [shifted(other, "y", hop) for hop in (1, 2, 3)]
    laid_mine, squares_mine = lay([gathered], own_gain, along)
    laid_other, squares_other = lay(others, own_gain, (y + along) % 4)
    squares = jnp.where(home, squares_mine, squares_other)
    squares = squares + swapped(jnp.where(home, squares_other, squares_mine))
    inverse_root = lax.rsqrt(squares / (feats * 8) + 1e-06)

    columns = out_weights[0].reshape(out_weights.shape[1], 4, 2 * feats)

    def block_for(hop):
        return lax.dynamic_index_in_dim(columns, (y - hop) % 4, 1, keepdims=False)

    moved = [block_for(0)]
    laid_other, ready = tied(laid_other, block_for(1))
    moved.append(shifted(ready, "y", 1))

    part = project_early(place, laid_mine, laid_other, early)
    part, inverse_root = tied(part, inverse_root)
    given, kept = project_late(place, part, laid_mine, laid_other, first, second)
    query, key, value = finish(kept, swapped(given), inverse_root)

    queries = (query, swapped(query))
    places = jnp.concatenate([(z * 2 + c) * tokens_here + here, (z * 2 + 1 - c) * tokens_here + here])
    limit = jnp.min(
        jnp.where(ends[None, :] > places[:, None], ends[None, :], ends[-1]), axis=1
    )
    limit = jnp.where(group == 1, ends[-1], limit).astype(jnp.int32)[:, None]

    def attend(hops, blocks, stat):
        bases = [(((z + hop) % 8) * 2 + c) * tokens_here for hop in hops]
        return flash(jnp.stack(bases), limit, queries, blocks, stat, hops == (4,))

    keys, values = both_ways(key, key, "z"), both_ways(value, value, "z")
    stat = attend((0,), [(key, value)], None)
    for hop in (1, 2, 3):
        keys, stat_one = lax.optimization_barrier((keys, stat))
        values, stat = lax.optimization_barrier((values, stat_one))
        if hop > 1:
            moved[-1], ready, _ = tied(moved[-1], block_for(hop), keys[0])
            moved.append(shifted(ready, "y", hop))
        if hop < 3:
            next_keys, next_values = both_ways(*keys, "z"), both_ways(*values, "z")
        else:
            last_key, last_value = shifted(keys[0], "z", 1), shifted(values[1], "z", -1)
        stat = attend((hop, -hop), [(keys[0], values[0]), (keys[1], values[1])], stat)
        keys, values = next_keys, next_values
    last_key, last_value, *stat = tied(last_key, last_value, *stat)
    ours, theirs = attend((4,), [(last_key, last_value)], stat)
    attended = crossed(merge(ours, swapped(theirs)))

    halves = [(block[:, :feats], block[:, feats:]) for block in moved]
    held = [jnp.where(c == 0, *half) for half in halves]
    came = swapped(jnp.stack([jnp.where(c == 0, *half[::-1]) for half in halves]))
    rights = [held[0], came[0], held[1], came[1], held[2], came[2], held[3], came[3]]
    lefts = []
    for hop in range(4):
        block = shifted(attended, "y", hop) if hop else attended
        lefts += [block, swapped(block)]
    teacher = jnp.full((1,), group, jnp.int32)
    result = result_of(teacher, times, mixed, states[0], lefts, rights)
    return shifted(result, "grp", 1)[None]


def solution(mesh):
    fine = jax.sharding.Mesh(mesh.devices.reshape(2, 8, 2, 4, 2), ("grp", "z", "a", "y", "c"))
    tokens, features = ("z", "a"), ("y", "c")
    return jax.shard_map(
        local,
        mesh=fine,
        in_specs=(
            P("grp", tokens, features),
            P("grp", tokens, features),
            P("grp", None),
            P("grp", None),
            P("grp", None),
            P("grp", tokens, None, features),
            P("grp", features, None),
        ),
        out_specs=P("grp", tokens, features),
        check_vma=False,
    )
```

```python
import functools

import jax
import jax.numpy as jnp
from jax import lax
from jax.experimental import pallas as pl
from jax.experimental.pallas import tpu as pltpu
from jax.sharding import PartitionSpec as P

HEAD_DIM = 128
STEPS = 4
LOW = -1e30
SCALE2 = HEAD_DIM ** (-0.5) * 1.4426950408889634


def crossed(block):
    return lax.ppermute(block, ("a", "c"), [(0, 0), (1, 2), (2, 1), (3, 3)])


def shifted(block, axis, hop):
    count = lax.axis_size(axis)
    return lax.ppermute(block, axis, [(i, (i - hop) % count) for i in range(count)])


def swapped(block):
    return shifted(block, "c", 1)


def both_ways(ahead, behind, axis):
    return shifted(ahead, axis, 1), shifted(behind, axis, -1)


def tied(*values):
    return lax.optimization_barrier(values)


def params():
    return pltpu.CompilerParams(vmem_limit_bytes=56 * 1024 * 1024)


def in_vmem():
    return pl.BlockSpec(memory_space=pltpu.VMEM)


def lay_kernel(blocks, order_ref, gain_ref, *refs):
    x_refs, out_ref, square_ref = refs[:-2], refs[-2], refs[-1]
    step = pl.program_id(0)
    for n, x_ref in enumerate(x_refs):

        @pl.when(step == n if len(x_refs) > 1 else step >= 0)
        def _():
            wide = x_ref[...].reshape(out_ref.shape).astype(jnp.float32)
            out_ref[...] = (wide * gain_ref[0]).astype(out_ref.dtype)
            square = jnp.sum(wide * wide, axis=1, keepdims=True)
            square_ref[...] = jnp.where(step == 0, square, square_ref[...] + square)


def lay(xs, gain, order):
    blocks = gain.shape[0]
    tokens, feats = xs[0].shape[-2:]
    if len(xs) == 1:
        specs = [pl.BlockSpec((1, tokens, feats), lambda i, where: (i, 0, 0))]
    else:
        specs = [pl.BlockSpec((tokens, feats), lambda i, where: (0, 0))] * blocks
    return pl.pallas_call(
        functools.partial(lay_kernel, blocks),
        grid_spec=pltpu.PrefetchScalarGridSpec(
            num_scalar_prefetch=1,
            grid=(blocks,),
            in_specs=[pl.BlockSpec((1, 1, feats), lambda i, where: (where[i], 0, 0))] + specs,
            out_specs=[
                pl.BlockSpec((tokens, feats), lambda i, where: (0, where[i])),
                pl.BlockSpec((tokens, 1), lambda i, where: (0, 0)),
            ],
        ),
        out_shape=[
            jax.ShapeDtypeStruct((tokens, blocks * feats), jnp.bfloat16),
            jax.ShapeDtypeStruct((tokens, 1), jnp.float32),
        ],
        compiler_params=params(),
        cost_estimate=pl.CostEstimate(
            flops=3 * blocks * tokens * feats, bytes_accessed=4 * blocks * tokens * feats, transcendentals=0
        ),
    )(order, gain, *xs)


def early_kernel(place_ref, mine_ref, other_ref, *refs):
    weights, (out_ref, wts, sems) = refs[:-3], refs[-3:]
    z, a = place_ref[0], place_ref[1]
    kinds, total, width = wts.shape
    tokens = mine_ref.shape[0]
    count = weights[0].shape[1]
    loads = []
    for kind in range(kinds):
        group = []
        for n, hop in enumerate((0, 1, 7, 2, 6, 3, 5)):
            for part in range(2):
                block = lax.rem(z + hop, 8) * 2 + (a if part == 0 else 1 - a)
                group.append(pltpu.make_async_copy(
                    weights[2 * n + part].at[kind],
                    wts.at[kind, pl.ds(pl.multiple_of(block * count, count), count)],
                    sems.at[kind, 2 * n + part],
                ))
        loads.append(group)
    for group in loads:
        for copy in group:
            copy.start()
    hole = pl.ds(pl.multiple_of(lax.rem(z + 4, 8) * 2 * count, 2 * count), 2 * count)
    for kind in range(kinds):
        wts[kind, hole, :] = jnp.zeros((2 * count, width), wts.dtype)
    for group in loads:
        for copy in group:
            copy.wait()

    @pl.loop(0, kinds)
    def _(kind):
        cols = pl.ds(pl.multiple_of(kind * width, width), width)
        right = wts[kind]
        out_ref[0, :, cols] = jnp.dot(mine_ref[...], right, preferred_element_type=jnp.float32)
        out_ref[1, :, cols] = jnp.dot(other_ref[...], right, preferred_element_type=jnp.float32)


def late_kernel(place_ref, part_ref, mine_ref, other_ref, first_ref, second_ref,
                given_ref, kept_ref, wts, act, sems):
    z, a, c = place_ref[0], place_ref[1], place_ref[2]
    kinds, _, width = wts.shape
    feats = act.shape[2]
    count = first_ref.shape[1]
    far = lax.rem(z + 4, 8)
    window = pl.ds(pl.multiple_of(far // 2 * feats, feats), feats)
    low = lax.rem(far, 2) * 2 * count
    copies = [
        pltpu.make_async_copy(mine_ref.at[:, window], act.at[0], sems.at[0]),
        pltpu.make_async_copy(other_ref.at[:, window], act.at[1], sems.at[1]),
    ]
    for n, (ref, spot) in enumerate(((first_ref, a), (second_ref, 1 - a))):
        row = pl.multiple_of(low + spot * count, count)
        copies.append(pltpu.make_async_copy(ref, wts.at[:, pl.ds(row, count)], sems.at[2 + n]))
    for copy in copies:
        copy.start()
    rest = pl.multiple_of(2 * count - low, 2 * count)
    for kind in range(kinds):
        wts[kind, pl.ds(rest, 2 * count), :] = jnp.zeros((2 * count, width), wts.dtype)
    for copy in copies:
        copy.wait()
    home = jnp.where(a == c, 0, 1)

    @pl.loop(0, kinds)
    def _(kind):
        cols = pl.ds(pl.multiple_of(kind * width, width), width)
        right = wts[kind]
        value = part_ref[1 - home, :, cols] + jnp.dot(
            act[1 - home], right, preferred_element_type=jnp.float32
        )
        given_ref[:, cols] = value.astype(given_ref.dtype)
        kept_ref[:, cols] = part_ref[home, :, cols] + jnp.dot(
            act[home], right, preferred_element_type=jnp.float32
        )


def project_early(place, mine, other, weights):
    tokens, feats = mine.shape
    kinds, count, width = weights[0].shape
    return pl.pallas_call(
        early_kernel,
        in_specs=[pl.BlockSpec(memory_space=pltpu.SMEM)] + [in_vmem()] * 2
        + [pl.BlockSpec(memory_space=pl.ANY)] * 14,
        out_specs=in_vmem(),
        out_shape=jax.ShapeDtypeStruct((2, tokens, kinds * width), jnp.float32),
        scratch_shapes=[
            pltpu.VMEM((kinds, feats, width), jnp.bfloat16),
            pltpu.SemaphoreType.DMA((kinds, 14)),
        ],
        compiler_params=params(),
        cost_estimate=pl.CostEstimate(
            flops=4 * tokens * feats * kinds * width,
            bytes_accessed=2 * (2 * tokens * feats + kinds * width * feats) + 8 * tokens * kinds * width,
            transcendentals=0,
        ),
    )(place, mine, other, *weights)


def project_late(place, part, mine, other, first, second):
    tokens = mine.shape[0]
    kinds, count, width = first.shape
    anywhere = pl.BlockSpec(memory_space=pl.ANY)
    return pl.pallas_call(
        late_kernel,
        in_specs=[pl.BlockSpec(memory_space=pltpu.SMEM), in_vmem()] + [anywhere] * 4,
        out_specs=[in_vmem()] * 2,
        out_shape=[
            jax.ShapeDtypeStruct((tokens, kinds * width), jnp.bfloat16),
            jax.ShapeDtypeStruct((tokens, kinds * width), jnp.float32),
        ],
        scratch_shapes=[
            pltpu.VMEM((kinds, 4 * count, width), jnp.bfloat16),
            pltpu.VMEM((2, tokens, 4 * count), jnp.bfloat16),
            pltpu.SemaphoreType.DMA((4,)),
        ],
        compiler_params=params(),
        cost_estimate=pl.CostEstimate(
            flops=16 * tokens * count * kinds * width,
            bytes_accessed=14 * tokens * kinds * width,
            transcendentals=0,
        ),
    )(place, part, mine, other, first, second)


def finish_kernel(kept_ref, came_ref, scale_ref, query_ref, pairs_ref):
    value = (kept_ref[...] + came_ref[...].astype(jnp.float32)) * scale_ref[...]
    value = value.astype(query_ref.dtype)

    @pl.when(pl.program_id(0) == 0)
    def _():
        query_ref[...] = value

    @pl.when(pl.program_id(0) > 0)
    def _():
        pairs_ref[...] = value


def finish(kept, came, scale):
    tokens, width = kept.shape[0], kept.shape[1] // 3
    part = pl.BlockSpec((tokens, width), lambda i: (0, i))
    return pl.pallas_call(
        finish_kernel,
        grid=(3,),
        in_specs=[part, part, pl.BlockSpec((tokens, 1), lambda i: (0, 0))],
        out_specs=[
            pl.BlockSpec((tokens, width), lambda i: (0, 0)),
            pl.BlockSpec((tokens, width), lambda i: (0, jnp.maximum(i - 1, 0))),
        ],
        out_shape=[
            jax.ShapeDtypeStruct((tokens, width), jnp.bfloat16),
            jax.ShapeDtypeStruct((tokens, 2 * width), jnp.bfloat16),
        ],
        compiler_params=params(),
        cost_estimate=pl.CostEstimate(
            flops=2 * kept.size, bytes_accessed=8 * kept.size, transcendentals=0
        ),
    )(kept, came, scale)


def flash_kernel(n_blocks, first, last, base_ref, limit_ref, *refs):
    side = pl.program_id(1)
    query = jnp.where(side == 0, refs[0][...], refs[1][...])
    refs = refs[2:]
    keys, values, rest = refs[:n_blocks], refs[n_blocks:2 * n_blocks], refs[2 * n_blocks:]
    if not first:
        acc_in, stat_in = rest[:2]
        rest = rest[2:]
    limit = limit_ref[...]
    scores = []
    for block in range(n_blocks):
        score = lax.dot_general(
            query, keys[block][...], (((1,), (1,)), ((), ())),
            preferred_element_type=jnp.float32,
        )
        place = lax.broadcasted_iota(jnp.int32, score.shape, 1)
        scores.append(jnp.where(place < limit - base_ref[block], score, LOW))
    high = functools.reduce(
        jnp.maximum, [jnp.max(score, axis=1, keepdims=True) for score in scores]
    )
    if not first:
        before = stat_in[:, :1]
        high = jnp.maximum(high, before)
    shift = high * SCALE2
    total, output = 0.0, 0.0
    for block in range(n_blocks):
        weight = jnp.exp2(scores[block] * SCALE2 - shift)
        total = total + jnp.sum(weight, axis=1, keepdims=True)
        output = output + jnp.dot(
            weight.astype(jnp.bfloat16), values[block][...], preferred_element_type=jnp.float32
        )
    if not first:
        shrink = jnp.exp2((before - high) * SCALE2)
        total = total + stat_in[:, HEAD_DIM // 2:HEAD_DIM // 2 + 1] * shrink
        output = output + acc_in[...] * shrink
    lane = lax.broadcasted_iota(jnp.int32, output.shape, 1)
    stat = jnp.where(lane < HEAD_DIM // 2, high, total)
    if last:
        for spot in range(2):

            @pl.when(side == spot)
            def _():
                rest[2 * spot][...] = output
                rest[2 * spot + 1][...] = stat
    else:
        rest[0][...] = output
        rest[1][...] = stat


def flash(bases, limit, queries, blocks, stat, last):
    rows, width = queries[0].shape
    n_blocks, heads = len(blocks), width // HEAD_DIM
    count = blocks[0][0][0].shape[0]

    def part(item):
        return pl.BlockSpec((count, HEAD_DIM), lambda h, i: (0, item[1] + h))

    flat = pl.BlockSpec((rows, HEAD_DIM), lambda h, i: (0, h))
    deep = pl.BlockSpec((rows, HEAD_DIM), lambda h, i: (i, h))
    in_specs = [
        pl.BlockSpec(memory_space=pltpu.SMEM),
        pl.BlockSpec((rows, 1), lambda h, i: (i, 0)),
        flat,
        flat,
    ]
    in_specs += [part(key) for key, _ in blocks] + [part(value) for _, value in blocks]
    operands = [bases, limit, *queries]
    operands += [key[0] for key, _ in blocks] + [value[0] for _, value in blocks]
    if stat is not None:
        in_specs += [deep] * 2
        operands += list(stat)
    sides = 1 if last else 2
    work = 2 * rows * count * n_blocks * width
    return pl.pallas_call(
        functools.partial(flash_kernel, n_blocks, stat is None, last),
        grid=(heads, 2),
        in_specs=in_specs,
        out_specs=[flat] * 4 if last else [deep] * 2,
        out_shape=[jax.ShapeDtypeStruct((sides * rows, width), jnp.float32)] * (4 // sides),
        compiler_params=params(),
        cost_estimate=pl.CostEstimate(
            flops=4 * work,
            bytes_accessed=4 * n_blocks * count * width + 32 * rows * width,
            transcendentals=work // HEAD_DIM,
        ),
    )(*operands)


def merge_kernel(one_ref, one_stat, two_ref, two_stat, out_ref):
    half = HEAD_DIM // 2
    high = jnp.maximum(one_stat[:, :1], two_stat[:, :1])
    one = jnp.exp2((one_stat[:, :1] - high) * SCALE2)
    two = jnp.exp2((two_stat[:, :1] - high) * SCALE2)
    total = one_stat[:, half:half + 1] * one + two_stat[:, half:half + 1] * two
    out_ref[...] = ((one_ref[...] * one + two_ref[...] * two) / total).astype(out_ref.dtype)


def merge(one, one_stat, two, two_stat):
    rows, width = one.shape
    part = pl.BlockSpec((rows, HEAD_DIM), lambda h: (0, h))
    return pl.pallas_call(
        merge_kernel,
        grid=(width // HEAD_DIM,),
        in_specs=[part] * 4,
        out_specs=part,
        out_shape=jax.ShapeDtypeStruct((rows, width), jnp.bfloat16),
        compiler_params=params(),
        cost_estimate=pl.CostEstimate(flops=4 * one.size, bytes_accessed=18 * one.size, transcendentals=0),
    )(one, one_stat, two, two_stat)


def result_kernel(n_blocks, teacher_ref, times_ref, mixed_ref, state_ref, *refs):
    lefts, rights, out_ref = refs[:n_blocks], refs[n_blocks:-1], refs[-1]
    velocity = 0.0
    for n in range(n_blocks):
        velocity = velocity + jnp.dot(lefts[n][...], rights[n][...], preferred_element_type=jnp.float32)
    estimate = mixed_ref[...].astype(jnp.float32) - times_ref[...] * velocity
    value = jnp.where(teacher_ref[0] == 1, state_ref[...].astype(jnp.float32) - estimate, estimate)
    out_ref[...] = value.astype(out_ref.dtype)


def result_of(teacher, times, mixed, state, lefts, rights):
    tokens, feats = mixed.shape
    depth = lefts[0].shape[1]
    return pl.pallas_call(
        functools.partial(result_kernel, len(lefts)),
        in_specs=[pl.BlockSpec(memory_space=pltpu.SMEM)] + [in_vmem()] * (3 + len(lefts) + len(rights)),
        out_specs=in_vmem(),
        out_shape=jax.ShapeDtypeStruct((tokens, feats), jnp.bfloat16),
        compiler_params=params(),
        cost_estimate=pl.CostEstimate(
            flops=2 * tokens * depth * len(lefts) * feats,
            bytes_accessed=2 * len(lefts) * depth * (tokens + feats) + 6 * tokens * feats,
            transcendentals=0,
        ),
    )(teacher, times, mixed, state, *lefts, *rights)


def local(states, noise, span_lengths, step_index, gain, in_weights, out_weights):
    tokens_here, feats = states.shape[1:]
    group = lax.axis_index("grp")
    z, a, y, c = (lax.axis_index(name) for name in ("z", "a", "y", "c"))
    home = a == c
    lengths = span_lengths[0]
    ends = jnp.cumsum(lengths)
    here = jnp.arange(tokens_here, dtype=jnp.int32)
    place = jnp.stack([z, a, c]).astype(jnp.int32)

    rows = jnp.transpose(in_weights[0], (1, 0, 2))
    count = rows.shape[1] // 2
    same = jnp.where(c == 0, rows[:, :count], rows[:, count:])
    opposite = jnp.where(c == 0, rows[:, count:], rows[:, :count])
    first = jnp.where(home, same, swapped(opposite))
    near = lax.ppermute(same, ("a", "c"), [(1, 3), (2, 0)])
    across = lax.ppermute(opposite, ("a", "c"), [(1, 2), (2, 1)])

    positions = (z * 2 + a) * tokens_here + here
    spans = jnp.sum((positions[:, None] >= ends[None, :]).astype(jnp.int32), axis=1)
    hits = spans[:, None] == jnp.arange(lengths.shape[0], dtype=jnp.int32)[None, :]
    picked = jnp.where(hits, (step_index[0][None, :] + 1).astype(jnp.float32), jnp.float32(0.0))
    times = (jnp.sum(picked, axis=1) / STEPS)[:, None]
    state = states[0].astype(jnp.float32)
    mixed = ((1.0 - times) * state + times * noise[0].astype(jnp.float32)).astype(jnp.bfloat16)

    quarters = [mixed[:, i * count:(i + 1) * count] for i in range(4)]
    kept = jnp.concatenate([jnp.where(c == 0, quarters[2 * i], quarters[2 * i + 1]) for i in range(2)], axis=1)
    given = jnp.concatenate([jnp.where(c == 0, quarters[2 * i + 1], quarters[2 * i]) for i in range(2)], axis=1)
    taken = swapped(given)
    mine = jnp.concatenate([jnp.where(c == 0, kept, taken), jnp.where(c == 0, taken, kept)], axis=1)
    gathered = lax.all_gather(mine, "y")
    other = shifted(mine, "a", 1)
    own_gain = gain[0].reshape(8, 2, 2, count)
    own_gain = jnp.where(c == 0, own_gain[:, :, 0], own_gain[:, :, 1]).reshape(4, 1, feats)

    chunks = [both_ways(first, first, "z"), None]
    *chunks[0], near, across = tied(*chunks[0], near, across)
    second = jnp.where(home, near, across)
    chunks[1] = both_ways(second, second, "z")
    early = [first, second, chunks[0][0], chunks[1][0], chunks[0][1], chunks[1][1]]
    for _ in range(2):
        chunks = [both_ways(*chunk, "z") for chunk in chunks]
        early += [chunks[0][0], chunks[1][0], chunks[0][1], chunks[1][1]]
    first, second = both_ways(chunks[0][0], chunks[1][1], "z")

    along = jnp.arange(4, dtype=jnp.int32)
    others = [other] + [shifted(other, "y", hop) for hop in (1, 2, 3)]
    laid_mine, squares_mine = lay([gathered], own_gain, along)
    laid_other, squares_other = lay(others, own_gain, (y + along) % 4)
    squares = jnp.where(home, squares_mine, squares_other)
    squares = squares + swapped(jnp.where(home, squares_other, squares_mine))
    inverse_root = lax.rsqrt(squares / (feats * 8) + 1e-06)

    part = project_early(place, laid_mine, laid_other, early)
    part, inverse_root = tied(part, inverse_root)
    given, kept = project_late(place, part, laid_mine, laid_other, first, second)
    cols = given.shape[1] // 3
    query, pairs = finish(kept, swapped(given), inverse_root)

    def block_for(hop):
        return lax.dynamic_slice_in_dim(out_weights[0], (y - hop) % 4 * 2 * feats, 2 * feats, axis=1)

    ready = [block_for(hop) for hop in range(4)]
    *ready, _ = tied(*ready, pairs)
    moved = [ready[0]] + [shifted(ready[hop], "y", hop) for hop in (1, 2, 3)]

    queries = (query, swapped(query))
    places = jnp.concatenate([(z * 2 + c) * tokens_here + here, (z * 2 + 1 - c) * tokens_here + here])
    limit = jnp.min(
        jnp.where(ends[None, :] > places[:, None], ends[None, :], ends[-1]), axis=1
    )
    limit = jnp.where(group == 1, ends[-1], limit).astype(jnp.int32)[:, None]

    def attend(hops, blocks, stat):
        bases = [(((z + hop) % 8) * 2 + c) * tokens_here for hop in hops]
        return flash(jnp.stack(bases), limit, queries, blocks, stat, hops == (4,))

    ahead, behind = both_ways(pairs, pairs, "z")
    wide_heads = cols // HEAD_DIM
    stat = attend((0,), [((pairs, 0), (pairs, wide_heads))], None)
    for hop in (1, 2, 3):
        ahead, behind, *stat = tied(ahead, behind, *stat)
        if hop < 3:
            onward = both_ways(ahead, behind, "z")
        else:
            onward = both_ways(ahead[:, :cols], behind[:, cols:], "z")
        blocks = [((pair, 0), (pair, wide_heads)) for pair in (ahead, behind)]
        stat = attend((hop, -hop), blocks, stat)
        ahead, behind = onward
    ahead, behind, *stat = tied(ahead, behind, *stat)
    one, one_stat, two, two_stat = attend((4,), [((ahead, 0), (behind, 0))], stat)
    attended = crossed(merge(one, one_stat, swapped(two), swapped(two_stat)))

    halves = [(block[:, :feats], block[:, feats:]) for block in moved]
    held = [jnp.where(c == 0, *half) for half in halves]
    came = swapped(jnp.stack([jnp.where(c == 0, *half[::-1]) for half in halves]))
    rights = [held[0], came[0], held[1], came[1], held[2], came[2], held[3], came[3]]
    lefts = []
    for hop in range(4):
        block = shifted(attended, "y", hop) if hop else attended
        lefts += [block, swapped(block)]
    teacher = jnp.full((1,), group, jnp.int32)
    result = result_of(teacher, times, mixed, states[0], lefts, rights)
    return shifted(result, "grp", 1)[None]


def solution(mesh):
    fine = jax.sharding.Mesh(mesh.devices.reshape(2, 8, 2, 4, 2), ("grp", "z", "a", "y", "c"))
    tokens, features = ("z", "a"), ("y", "c")
    return jax.shard_map(
        local,
        mesh=fine,
        in_specs=(
            P("grp", tokens, features),
            P("grp", tokens, features),
            P("grp", None),
            P("grp", None),
            P("grp", None),
            P("grp", tokens, None, features),
            P("grp", features, None),
        ),
        out_specs=P("grp", tokens, features),
        check_vma=False,
    )
```

```python
import functools

import jax
import jax.numpy as jnp
from jax import lax
from jax.experimental import pallas as pl
from jax.experimental.pallas import tpu as pltpu
from jax.sharding import PartitionSpec as P

HEAD_DIM = 128
STEPS = 4
LOW = -1e30
SCALE2 = HEAD_DIM ** (-0.5) * 1.4426950408889634


def crossed(block):
    return lax.ppermute(block, ("a", "c"), [(0, 0), (1, 2), (2, 1), (3, 3)])


def shifted(block, axis, hop):
    count = lax.axis_size(axis)
    return lax.ppermute(block, axis, [(i, (i - hop) % count) for i in range(count)])


def swapped(block):
    return shifted(block, "c", 1)


def both_ways(ahead, behind, axis):
    return shifted(ahead, axis, 1), shifted(behind, axis, -1)


def tied(*values):
    return lax.optimization_barrier(values)


def params():
    return pltpu.CompilerParams(vmem_limit_bytes=32 * 1024 * 1024)


def in_vmem():
    return pl.BlockSpec(memory_space=pltpu.VMEM)


def lay_kernel(order_ref, gain_ref, *refs):
    x_refs, out_ref, square_ref = refs[:-2], refs[-2], refs[-1]
    step = pl.program_id(0)
    half = out_ref.shape[2]
    for n, x_ref in enumerate(x_refs):

        @pl.when(step == n)
        def _():
            wide = x_ref[...].astype(jnp.float32)
            scaled = (wide * gain_ref[0]).astype(out_ref.dtype)
            out_ref[0] = scaled[:, :half]
            out_ref[1] = scaled[:, half:]
            square = jnp.sum(wide * wide, axis=1, keepdims=True)
            square_ref[...] = jnp.where(step == 0, square, square_ref[...] + square)


def lay(xs, gain, order):
    blocks = gain.shape[0]
    tokens, feats = xs[0].shape
    return pl.pallas_call(
        lay_kernel,
        grid_spec=pltpu.PrefetchScalarGridSpec(
            num_scalar_prefetch=1,
            grid=(blocks,),
            in_specs=[pl.BlockSpec((1, 1, feats), lambda i, where: (where[i], 0, 0))]
            + [pl.BlockSpec((tokens, feats), lambda i, where: (0, 0))] * blocks,
            out_specs=[
                pl.BlockSpec((2, tokens, feats // 2), lambda i, where: (where[i], 0, 0)),
                pl.BlockSpec((tokens, 1), lambda i, where: (0, 0)),
            ],
        ),
        out_shape=[
            jax.ShapeDtypeStruct((2 * blocks, tokens, feats // 2), jnp.bfloat16),
            jax.ShapeDtypeStruct((tokens, 1), jnp.float32),
        ],
        compiler_params=params(),
        cost_estimate=pl.CostEstimate(
            flops=3 * blocks * tokens * feats, bytes_accessed=4 * blocks * tokens * feats, transcendentals=0
        ),
    )(order, gain, *xs)


def project_kernel(parts, first, last, where_ref, home_ref, *refs):
    blocks = len(parts)
    acts, refs = refs[:2 * blocks], refs[2 * blocks:]
    weights = []
    for count in parts:
        weights.append(refs[:count])
        refs = refs[count:]
    if not first:
        part_ref, refs = refs[0], refs[1:]
    kinds, _, width = weights[0][0].shape
    home = home_ref[0]
    for side in range(2):
        for kind in range(kinds):
            cols = slice(kind * width, (kind + 1) * width)
            value = 0.0
            for n in range(blocks):
                mine, other = acts[2 * n][0], acts[2 * n + 1][0]
                if last:
                    left = jnp.where(home == side, mine, other)
                else:
                    left = (mine, other)[side]
                right = jnp.concatenate([ref[kind] for ref in weights[n]], axis=0)
                value = value + jnp.dot(left, right, preferred_element_type=jnp.float32)
            if last:
                value = value + part_ref[jnp.where(home == side, 0, 1), :, cols]
                refs[side][:, cols] = value.astype(refs[side].dtype)
            else:
                if not first:
                    value = value + part_ref[side, :, cols]
                refs[0][side, :, cols] = value


def project(where, home, mine, other, weights, part, last):
    tokens, depth = mine.shape[1:]
    kinds, _, width = weights[0][0].shape
    blocks = len(weights)

    def chosen(n):
        return pl.BlockSpec((1, tokens, depth), lambda i, where, home: (where[n], 0, 0))

    def whole(shape):
        return pl.BlockSpec(shape, lambda i, where, home: (0,) * len(shape))

    flat, deep = (tokens, kinds * width), (2, tokens, kinds * width)
    operands, in_specs = [], []
    for n in range(blocks):
        operands += [mine, other]
        in_specs += [chosen(n)] * 2
    for group in weights:
        operands += group
        in_specs += [whole(array.shape) for array in group]
    if part is not None:
        operands.append(part)
        in_specs.append(whole(deep))
    if last:
        out_specs = [whole(flat)] * 2
        out_shape = [jax.ShapeDtypeStruct(flat, jnp.bfloat16), jax.ShapeDtypeStruct(flat, jnp.float32)]
    else:
        out_specs, out_shape = whole(deep), jax.ShapeDtypeStruct(deep, jnp.float32)
    return pl.pallas_call(
        functools.partial(project_kernel, [len(group) for group in weights], part is None, last),
        grid_spec=pltpu.PrefetchScalarGridSpec(
            num_scalar_prefetch=2, grid=(1,), in_specs=in_specs, out_specs=out_specs
        ),
        out_shape=out_shape,
        compiler_params=params(),
        cost_estimate=pl.CostEstimate(
            flops=4 * tokens * depth * blocks * kinds * width,
            bytes_accessed=2 * blocks * depth * (2 * tokens + kinds * width) + 16 * tokens * kinds * width,
            transcendentals=0,
        ),
    )(where, home, *operands)


def finish_kernel(kept_ref, came_ref, scale_ref, query_ref, pairs_ref):
    value = (kept_ref[...] + came_ref[...].astype(jnp.float32)) * scale_ref[...]
    value = value.astype(query_ref.dtype)

    @pl.when(pl.program_id(0) == 0)
    def _():
        query_ref[...] = value

    @pl.when(pl.program_id(0) > 0)
    def _():
        pairs_ref[...] = value


def finish(kept, came, scale):
    tokens, width = kept.shape[0], kept.shape[1] // 3
    part = pl.BlockSpec((tokens, width), lambda i: (0, i))
    return pl.pallas_call(
        finish_kernel,
        grid=(3,),
        in_specs=[part, part, pl.BlockSpec((tokens, 1), lambda i: (0, 0))],
        out_specs=[
            pl.BlockSpec((tokens, width), lambda i: (0, 0)),
            pl.BlockSpec((tokens, width), lambda i: (0, jnp.maximum(i - 1, 0))),
        ],
        out_shape=[
            jax.ShapeDtypeStruct((tokens, width), jnp.bfloat16),
            jax.ShapeDtypeStruct((tokens, 2 * width), jnp.bfloat16),
        ],
        compiler_params=params(),
        cost_estimate=pl.CostEstimate(
            flops=2 * kept.size, bytes_accessed=8 * kept.size, transcendentals=0
        ),
    )(kept, came, scale)


def flash_kernel(spots, first, last, base_ref, limit_ref, *refs):
    n_blocks = len(spots)
    queries, refs = refs[:2], refs[2:]
    n_arrays = 1 + max(max(spot[0], spot[2]) for spot in spots)
    arrays, rest = refs[:n_arrays], refs[n_arrays:]
    if not first:
        acc_in, stat_in = rest[:2]
        rest = rest[2:]
    rows, width = queries[0].shape
    heads = width // HEAD_DIM
    for side in range(2):
        span = slice(side * rows, (side + 1) * rows)
        limit = limit_ref[span, :]
        for head in range(heads):
            cols = slice(head * HEAD_DIM, (head + 1) * HEAD_DIM)
            query = queries[side][:, cols]
            scores = []
            for block, (array, start, _, _) in enumerate(spots):
                start = start + head * HEAD_DIM
                score = lax.dot_general(
                    query, arrays[array][:, start:start + HEAD_DIM], (((1,), (1,)), ((), ())),
                    preferred_element_type=jnp.float32,
                )
                place = lax.broadcasted_iota(jnp.int32, score.shape, 1)
                scores.append(jnp.where(place < limit - base_ref[block], score, LOW))
            high = functools.reduce(
                jnp.maximum, [jnp.max(score, axis=1, keepdims=True) for score in scores]
            )
            if not first:
                before = stat_in[span, head:head + 1]
                high = jnp.maximum(high, before)
            shift = high * SCALE2
            total, output = 0.0, 0.0
            for block, (_, _, array, start) in enumerate(spots):
                start = start + head * HEAD_DIM
                weight = jnp.exp2(scores[block] * SCALE2 - shift)
                total = total + jnp.sum(weight, axis=1, keepdims=True)
                output = output + jnp.dot(
                    weight.astype(jnp.bfloat16), arrays[array][:, start:start + HEAD_DIM],
                    preferred_element_type=jnp.float32,
                )
            if not first:
                shrink = jnp.exp2((before - high) * SCALE2)
                total = total + stat_in[span, heads + head:heads + head + 1] * shrink
                output = output + acc_in[span, cols] * shrink
            acc_out, stat_out = rest[2 * side:2 * side + 2] if last else rest
            place = slice(0, rows) if last else span
            acc_out[place, cols] = output
            stat_out[place, head:head + 1] = high
            stat_out[place, heads + head:heads + head + 1] = total


def flash(bases, limit, queries, blocks, stat, last):
    rows, width = queries[0].shape
    count = blocks[0][0].shape[0]
    arrays, spots = [], []
    for key, key_start, value, value_start in blocks:
        spot = []
        for array, start in ((key, key_start), (value, value_start)):
            known = [n for n, seen in enumerate(arrays) if seen is array]
            if not known:
                known = [len(arrays)]
                arrays.append(array)
            spot += [known[0], start]
        spots.append(tuple(spot))
    operands = [bases, limit, *queries, *arrays]
    operands += [] if stat is None else list(stat)
    sides = 1 if last else 2
    shapes = [
        jax.ShapeDtypeStruct((sides * rows, width), jnp.float32),
        jax.ShapeDtypeStruct((sides * rows, 128), jnp.float32),
    ]
    work = 2 * rows * count * len(blocks) * width
    return pl.pallas_call(
        functools.partial(flash_kernel, tuple(spots), stat is None, last),
        in_specs=[pl.BlockSpec(memory_space=pltpu.SMEM)] + [in_vmem()] * (len(operands) - 1),
        out_specs=[in_vmem()] * (2 * (3 - sides)),
        out_shape=shapes * (3 - sides),
        compiler_params=params(),
        cost_estimate=pl.CostEstimate(
            flops=4 * work,
            bytes_accessed=4 * len(blocks) * count * width + 20 * rows * width,
            transcendentals=work // HEAD_DIM,
        ),
    )(*operands)


def merge_kernel(one_ref, one_stat, two_ref, two_stat, out_ref):
    heads = out_ref.shape[1] // HEAD_DIM
    for head in range(heads):
        cols = slice(head * HEAD_DIM, (head + 1) * HEAD_DIM)
        top, low = slice(head, head + 1), slice(heads + head, heads + head + 1)
        high = jnp.maximum(one_stat[:, top], two_stat[:, top])
        one = jnp.exp2((one_stat[:, top] - high) * SCALE2)
        two = jnp.exp2((two_stat[:, top] - high) * SCALE2)
        total = one_stat[:, low] * one + two_stat[:, low] * two
        value = (one_ref[:, cols] * one + two_ref[:, cols] * two) / total
        out_ref[:, cols] = value.astype(out_ref.dtype)


def merge(one, one_stat, two, two_stat):
    return pl.pallas_call(
        merge_kernel,
        in_specs=[in_vmem()] * 4,
        out_specs=in_vmem(),
        out_shape=jax.ShapeDtypeStruct(one.shape, jnp.bfloat16),
        compiler_params=params(),
        cost_estimate=pl.CostEstimate(flops=4 * one.size, bytes_accessed=10 * one.size, transcendentals=0),
    )(one, one_stat, two, two_stat)


def result_kernel(n_blocks, teacher_ref, times_ref, mixed_ref, state_ref, *refs):
    lefts, rights, out_ref = refs[:n_blocks], refs[n_blocks:-1], refs[-1]
    velocity = 0.0
    for left, right in zip(lefts, rights):
        velocity = velocity + jnp.dot(left[...], right[...], preferred_element_type=jnp.float32)
    estimate = mixed_ref[...].astype(jnp.float32) - times_ref[...] * velocity
    value = jnp.where(teacher_ref[0] == 1, state_ref[...].astype(jnp.float32) - estimate, estimate)
    out_ref[...] = value.astype(out_ref.dtype)


def result_of(teacher, times, mixed, state, lefts, rights):
    tokens, feats = mixed.shape
    depth = lefts[0].shape[1]
    return pl.pallas_call(
        functools.partial(result_kernel, len(lefts)),
        in_specs=[pl.BlockSpec(memory_space=pltpu.SMEM)] + [in_vmem()] * (3 + len(lefts) + len(rights)),
        out_specs=in_vmem(),
        out_shape=jax.ShapeDtypeStruct((tokens, feats), jnp.bfloat16),
        compiler_params=params(),
        cost_estimate=pl.CostEstimate(
            flops=2 * tokens * depth * len(lefts) * feats,
            bytes_accessed=2 * len(lefts) * depth * (tokens + feats) + 6 * tokens * feats,
            transcendentals=0,
        ),
    )(teacher, times, mixed, state, *lefts, *rights)


def local(states, noise, span_lengths, step_index, gain, in_weights, out_weights):
    tokens_here, feats = states.shape[1:]
    group = lax.axis_index("grp")
    z, a, y, c = (lax.axis_index(name) for name in ("z", "a", "y", "c"))
    lengths = span_lengths[0]
    ends = jnp.cumsum(lengths)
    here = jnp.arange(tokens_here, dtype=jnp.int32)

    rows = crossed(jnp.transpose(in_weights[0], (1, 0, 2)))
    half = rows.shape[1]

    positions = (z * 2 + a) * tokens_here + here
    spans = jnp.sum((positions[:, None] >= ends[None, :]).astype(jnp.int32), axis=1)
    hits = spans[:, None] == jnp.arange(lengths.shape[0], dtype=jnp.int32)[None, :]
    picked = jnp.where(hits, (step_index[0][None, :] + 1).astype(jnp.float32), jnp.float32(0.0))
    times = (jnp.sum(picked, axis=1) / STEPS)[:, None]
    state = states[0].astype(jnp.float32)
    mixed = ((1.0 - times) * state + times * noise[0].astype(jnp.float32)).astype(jnp.bfloat16)

    kept = jnp.where(c == 0, mixed[:, :half], mixed[:, half:])
    given = jnp.where(c == 0, mixed[:, half:], mixed[:, :half])
    taken = swapped(given)
    mine = jnp.concatenate([jnp.where(c == 0, kept, taken), jnp.where(c == 0, taken, kept)], axis=1)
    own_gain = gain[0].reshape(8, 2, half)
    own_gain = jnp.where(c == 0, own_gain[:, 0], own_gain[:, 1]).reshape(4, 1, feats)

    other = shifted(tied(mine, rows)[0], "a", 1)
    near = both_ways(rows, rows, "z")
    mine_y = [mine, shifted(mine, "y", 1), None, shifted(mine, "y", -1)]
    mine_y[2] = shifted(tied(mine, mine_y[1], mine_y[3])[0], "y", 2)
    mine_y[1], mine_y[3], other, *near = tied(mine_y[1], mine_y[3], other, *near)
    middle = both_ways(*near, "z")
    other_y = [other, shifted(other, "y", 1), None, shifted(other, "y", -1)]
    other_y[2] = shifted(tied(other, other_y[1], other_y[3], mine_y[2])[0], "y", 2)
    mine_y[2], other_y[1], other_y[3], *middle = tied(mine_y[2], other_y[1], other_y[3], *middle)
    distant = both_ways(*middle, "z")

    def columns_for(hop, core):
        return lax.dynamic_slice_in_dim(out_weights[0], ((y - hop) % 4 * 2 + core) * feats, feats, axis=1)

    def moved(hop, *after):
        own, partners, *_ = tied(columns_for(hop, c), columns_for(hop, 1 - c), *after)
        return shifted(own, "y", hop), shifted(partners, "y", hop)

    right = {0: (columns_for(0, c), columns_for(0, 1 - c))}
    right[1] = moved(1, other_y[2])

    along = jnp.arange(4, dtype=jnp.int32)
    order = (y + along) % 4
    laid = []
    squares = []
    for blocks in (mine_y, other_y):
        block, square = lay(blocks, own_gain, order)
        laid.append(block)
        squares.append(square)
    home = a == c
    square = jnp.where(home, squares[0], squares[1])
    square = square + swapped(jnp.where(home, squares[1], squares[0]))
    inverse_root = lax.rsqrt(square / (feats * 8) + 1e-06)
    at_home = jnp.full((1,), jnp.where(home, 1, 0), jnp.int32)

    def project_hops(hops, weights, part, last=False):
        where = jnp.stack([(z + hop) % 8 for hop in hops]).astype(jnp.int32)
        return project(where, at_home, *laid, weights, part, last)

    part = project_hops((0,), [(rows,)], None)
    part = project_hops((1, -1), [(near[0],), (near[1],)], part)
    part = project_hops((2, -2), [(middle[0],), (middle[1],)], part)
    part, inverse_root, *distant = tied(part, inverse_root, *distant)
    last = both_ways(distant[0][:, :half // 2], distant[1][:, half // 2:], "z")
    right[3] = moved(3, *right[1])
    part = project_hops((3, -3), [(distant[0],), (distant[1],)], part)
    part, *last = tied(part, *last)
    given, kept = project_hops((4,), [tuple(last)], part, True)
    cols = given.shape[1] // 3
    query, pairs = finish(kept, swapped(given), inverse_root)

    queries = (query, swapped(query))
    places = jnp.concatenate([(z * 2 + c) * tokens_here + here, (z * 2 + 1 - c) * tokens_here + here])
    limit = jnp.min(
        jnp.where(ends[None, :] > places[:, None], ends[None, :], ends[-1]), axis=1
    )
    limit = jnp.where(group == 1, ends[-1], limit).astype(jnp.int32)[:, None]

    def attend(hops, blocks, stat):
        bases = [(((z + hop) % 8) * 2 + c) * tokens_here for hop in hops]
        return flash(jnp.stack(bases), limit, queries, blocks, stat, hops == (4,))

    ahead, behind = both_ways(pairs, pairs, "z")
    right[2] = moved(2, *right[3], pairs)
    stat = attend((0,), [(pairs, 0, pairs, cols)], None)
    for hop in (1, 2, 3):
        ahead, behind, *stat = tied(ahead, behind, *stat)
        if hop < 3:
            onward = both_ways(ahead, behind, "z")
        else:
            onward = both_ways(ahead[:, :cols], behind[:, cols:], "z")
        stat = attend((hop, -hop), [(ahead, 0, ahead, cols), (behind, 0, behind, cols)], stat)
        ahead, behind = onward
    ahead, behind, *stat = tied(ahead, behind, *stat)
    one, one_stat, two, two_stat = attend((4,), [(ahead, 0, behind, 0)], stat)
    attended = crossed(merge(one, one_stat, swapped(two), swapped(two_stat)))

    lefts, rights = [], []
    for hop in range(4):
        block = shifted(attended, "y", hop) if hop else attended
        lefts += [block, swapped(block)]
        rights += [right[hop][0], swapped(right[hop][1])]
    teacher = jnp.full((1,), group, jnp.int32)
    result = result_of(teacher, times, mixed, states[0], lefts, rights)
    return shifted(result, "grp", 1)[None]


def solution(mesh):
    fine = jax.sharding.Mesh(mesh.devices.reshape(2, 8, 2, 4, 2), ("grp", "z", "a", "y", "c"))
    tokens, features = ("z", "a"), ("y", "c")
    return jax.shard_map(
        local,
        mesh=fine,
        in_specs=(
            P("grp", tokens, features),
            P("grp", tokens, features),
            P("grp", None),
            P("grp", None),
            P("grp", None),
            P("grp", tokens, None, features),
            P("grp", features, None),
        ),
        out_specs=P("grp", tokens, features),
        check_vma=False,
    )
```

```python
import functools

import jax
import jax.numpy as jnp
from jax import lax
from jax.experimental import pallas as pl
from jax.experimental.pallas import tpu as pltpu
from jax.sharding import PartitionSpec as P

HEAD_DIM = 128
STEPS = 4
LOW = -1e30
SCALE2 = HEAD_DIM ** (-0.5) * 1.4426950408889634


def crossed(block):
    return lax.ppermute(block, ("a", "c"), [(0, 0), (1, 2), (2, 1), (3, 3)])


def shifted(block, axis, hop):
    count = lax.axis_size(axis)
    return lax.ppermute(block, axis, [(i, (i - hop) % count) for i in range(count)])


def swapped(block):
    return shifted(block, "c", 1)


def both_ways(ahead, behind, axis):
    return shifted(ahead, axis, 1), shifted(behind, axis, -1)


def tied(*values):
    return lax.optimization_barrier(values)


def params():
    return pltpu.CompilerParams(vmem_limit_bytes=32 * 1024 * 1024)


def in_vmem():
    return pl.BlockSpec(memory_space=pltpu.VMEM)


def lay_kernel(order_ref, gain_ref, *refs):
    x_refs, out_ref, square_ref = refs[:-2], refs[-2], refs[-1]
    step = pl.program_id(0)
    half = out_ref.shape[2]
    for n, x_ref in enumerate(x_refs):

        @pl.when(step == n)
        def _():
            wide = x_ref[...].astype(jnp.float32)
            scaled = (wide * gain_ref[0]).astype(out_ref.dtype)
            out_ref[0] = scaled[:, :half]
            out_ref[1] = scaled[:, half:]
            square = jnp.sum(wide * wide, axis=1, keepdims=True)
            square_ref[...] = jnp.where(step == 0, square, square_ref[...] + square)


def lay(xs, gain, order):
    blocks = gain.shape[0]
    tokens, feats = xs[0].shape
    return pl.pallas_call(
        lay_kernel,
        grid_spec=pltpu.PrefetchScalarGridSpec(
            num_scalar_prefetch=1,
            grid=(blocks,),
            in_specs=[pl.BlockSpec((1, 1, feats), lambda i, where: (where[i], 0, 0))]
            + [pl.BlockSpec((tokens, feats), lambda i, where: (0, 0))] * blocks,
            out_specs=[
                pl.BlockSpec((2, tokens, feats // 2), lambda i, where: (where[i], 0, 0)),
                pl.BlockSpec((tokens, 1), lambda i, where: (0, 0)),
            ],
        ),
        out_shape=[
            jax.ShapeDtypeStruct((2 * blocks, tokens, feats // 2), jnp.bfloat16),
            jax.ShapeDtypeStruct((tokens, 1), jnp.float32),
        ],
        compiler_params=params(),
        cost_estimate=pl.CostEstimate(
            flops=3 * blocks * tokens * feats, bytes_accessed=4 * blocks * tokens * feats, transcendentals=0
        ),
    )(order, gain, *xs)


def project_kernel(parts, first, last, where_ref, home_ref, *refs):
    blocks = len(parts)
    acts, refs = refs[:2 * blocks], refs[2 * blocks:]
    weights = []
    for count in parts:
        weights.append(refs[:count])
        refs = refs[count:]
    if not first:
        part_ref, refs = refs[0], refs[1:]
    kinds, _, width = weights[0][0].shape
    home = home_ref[0]
    for side in range(2):
        for kind in range(kinds):
            cols = slice(kind * width, (kind + 1) * width)
            value = 0.0
            for n in range(blocks):
                mine, other = acts[2 * n][0], acts[2 * n + 1][0]
                if last:
                    left = jnp.where(home == side, mine, other)
                else:
                    left = (mine, other)[side]
                right = jnp.concatenate([ref[kind] for ref in weights[n]], axis=0)
                value = value + jnp.dot(left, right, preferred_element_type=jnp.float32)
            if last:
                value = value + part_ref[jnp.where(home == side, 0, 1), :, cols]
                refs[side][:, cols] = value.astype(refs[side].dtype)
            else:
                if not first:
                    value = value + part_ref[side, :, cols]
                refs[0][side, :, cols] = value


def project(where, home, mine, other, weights, part, last):
    tokens, depth = mine.shape[1:]
    kinds, _, width = weights[0][0].shape
    blocks = len(weights)

    def chosen(n):
        return pl.BlockSpec((1, tokens, depth), lambda i, where, home: (where[n], 0, 0))

    def whole(shape):
        return pl.BlockSpec(shape, lambda i, where, home: (0,) * len(shape))

    flat, deep = (tokens, kinds * width), (2, tokens, kinds * width)
    operands, in_specs = [], []
    for n in range(blocks):
        operands += [mine, other]
        in_specs += [chosen(n)] * 2
    for group in weights:
        operands += group
        in_specs += [whole(array.shape) for array in group]
    if part is not None:
        operands.append(part)
        in_specs.append(whole(deep))
    if last:
        out_specs = [whole(flat)] * 2
        out_shape = [jax.ShapeDtypeStruct(flat, jnp.bfloat16), jax.ShapeDtypeStruct(flat, jnp.float32)]
    else:
        out_specs, out_shape = whole(deep), jax.ShapeDtypeStruct(deep, jnp.float32)
    return pl.pallas_call(
        functools.partial(project_kernel, [len(group) for group in weights], part is None, last),
        grid_spec=pltpu.PrefetchScalarGridSpec(
            num_scalar_prefetch=2, grid=(1,), in_specs=in_specs, out_specs=out_specs
        ),
        out_shape=out_shape,
        compiler_params=params(),
        cost_estimate=pl.CostEstimate(
            flops=4 * tokens * depth * blocks * kinds * width,
            bytes_accessed=2 * blocks * depth * (2 * tokens + kinds * width) + 16 * tokens * kinds * width,
            transcendentals=0,
        ),
    )(where, home, *operands)


def finish_kernel(kept_ref, came_ref, scale_ref, query_ref, pairs_ref):
    value = (kept_ref[...] + came_ref[...].astype(jnp.float32)) * scale_ref[...]
    value = value.astype(query_ref.dtype)

    @pl.when(pl.program_id(0) == 0)
    def _():
        query_ref[...] = value

    @pl.when(pl.program_id(0) > 0)
    def _():
        pairs_ref[...] = value


def finish(kept, came, scale):
    tokens, width = kept.shape[0], kept.shape[1] // 3
    part = pl.BlockSpec((tokens, width), lambda i: (0, i))
    return pl.pallas_call(
        finish_kernel,
        grid=(3,),
        in_specs=[part, part, pl.BlockSpec((tokens, 1), lambda i: (0, 0))],
        out_specs=[
            pl.BlockSpec((tokens, width), lambda i: (0, 0)),
            pl.BlockSpec((tokens, width), lambda i: (0, jnp.maximum(i - 1, 0))),
        ],
        out_shape=[
            jax.ShapeDtypeStruct((tokens, width), jnp.bfloat16),
            jax.ShapeDtypeStruct((tokens, 2 * width), jnp.bfloat16),
        ],
        compiler_params=params(),
        cost_estimate=pl.CostEstimate(
            flops=2 * kept.size, bytes_accessed=8 * kept.size, transcendentals=0
        ),
    )(kept, came, scale)


def flash_kernel(spots, first, last, base_ref, limit_ref, *refs):
    n_blocks = len(spots)
    queries, refs = refs[:2], refs[2:]
    n_arrays = 1 + max(max(spot[0], spot[2]) for spot in spots)
    arrays, rest = refs[:n_arrays], refs[n_arrays:]
    if not first:
        acc_in, stat_in = rest[:2]
        rest = rest[2:]
    rows, width = queries[0].shape
    heads = width // HEAD_DIM
    for side in range(2):
        span = slice(side * rows, (side + 1) * rows)
        limit = limit_ref[span, :]
        for head in range(heads):
            cols = slice(head * HEAD_DIM, (head + 1) * HEAD_DIM)
            query = queries[side][:, cols]
            scores = []
            for block, (array, start, _, _) in enumerate(spots):
                start = start + head * HEAD_DIM
                score = lax.dot_general(
                    query, arrays[array][:, start:start + HEAD_DIM], (((1,), (1,)), ((), ())),
                    preferred_element_type=jnp.float32,
                )
                place = lax.broadcasted_iota(jnp.int32, score.shape, 1)
                scores.append(jnp.where(place < limit - base_ref[block], score, LOW))
            high = functools.reduce(
                jnp.maximum, [jnp.max(score, axis=1, keepdims=True) for score in scores]
            )
            if not first:
                before = stat_in[span, head:head + 1]
                high = jnp.maximum(high, before)
            shift = high * SCALE2
            total, output = 0.0, 0.0
            for block, (_, _, array, start) in enumerate(spots):
                start = start + head * HEAD_DIM
                weight = jnp.exp2(scores[block] * SCALE2 - shift)
                total = total + jnp.sum(weight, axis=1, keepdims=True)
                output = output + jnp.dot(
                    weight.astype(jnp.bfloat16), arrays[array][:, start:start + HEAD_DIM],
                    preferred_element_type=jnp.float32,
                )
            if not first:
                shrink = jnp.exp2((before - high) * SCALE2)
                total = total + stat_in[span, heads + head:heads + head + 1] * shrink
                output = output + acc_in[span, cols] * shrink
            acc_out, stat_out = rest[2 * side:2 * side + 2] if last else rest
            place = slice(0, rows) if last else span
            acc_out[place, cols] = output
            stat_out[place, head:head + 1] = high
            stat_out[place, heads + head:heads + head + 1] = total


def flash(bases, limit, queries, blocks, stat, last):
    rows, width = queries[0].shape
    count = blocks[0][0].shape[0]
    arrays, spots = [], []
    for key, key_start, value, value_start in blocks:
        spot = []
        for array, start in ((key, key_start), (value, value_start)):
            known = [n for n, seen in enumerate(arrays) if seen is array]
            if not known:
                known = [len(arrays)]
                arrays.append(array)
            spot += [known[0], start]
        spots.append(tuple(spot))
    operands = [bases, limit, *queries, *arrays]
    operands += [] if stat is None else list(stat)
    sides = 1 if last else 2
    shapes = [
        jax.ShapeDtypeStruct((sides * rows, width), jnp.float32),
        jax.ShapeDtypeStruct((sides * rows, 128), jnp.float32),
    ]
    work = 2 * rows * count * len(blocks) * width
    return pl.pallas_call(
        functools.partial(flash_kernel, tuple(spots), stat is None, last),
        in_specs=[pl.BlockSpec(memory_space=pltpu.SMEM)] + [in_vmem()] * (len(operands) - 1),
        out_specs=[in_vmem()] * (2 * (3 - sides)),
        out_shape=shapes * (3 - sides),
        compiler_params=params(),
        cost_estimate=pl.CostEstimate(
            flops=4 * work,
            bytes_accessed=4 * len(blocks) * count * width + 20 * rows * width,
            transcendentals=work // HEAD_DIM,
        ),
    )(*operands)


def merge_kernel(one_ref, one_stat, two_ref, two_stat, out_ref):
    heads = out_ref.shape[1] // HEAD_DIM
    for head in range(heads):
        cols = slice(head * HEAD_DIM, (head + 1) * HEAD_DIM)
        top, low = slice(head, head + 1), slice(heads + head, heads + head + 1)
        high = jnp.maximum(one_stat[:, top], two_stat[:, top])
        one = jnp.exp2((one_stat[:, top] - high) * SCALE2)
        two = jnp.exp2((two_stat[:, top] - high) * SCALE2)
        total = one_stat[:, low] * one + two_stat[:, low] * two
        value = (one_ref[:, cols] * one + two_ref[:, cols] * two) / total
        out_ref[:, cols] = value.astype(out_ref.dtype)


def merge(one, one_stat, two, two_stat):
    return pl.pallas_call(
        merge_kernel,
        in_specs=[in_vmem()] * 4,
        out_specs=in_vmem(),
        out_shape=jax.ShapeDtypeStruct(one.shape, jnp.bfloat16),
        compiler_params=params(),
        cost_estimate=pl.CostEstimate(flops=4 * one.size, bytes_accessed=10 * one.size, transcendentals=0),
    )(one, one_stat, two, two_stat)


def result_kernel(n_blocks, index_ref, times_ref, mixed_ref, state_ref, *refs):
    lefts, rights, out_ref = refs[:n_blocks], refs[n_blocks:-1], refs[-1]
    velocity = 0.0
    for left, right in zip(lefts, rights):
        velocity = velocity + jnp.dot(left[...], right[...], preferred_element_type=jnp.float32)
    estimate = mixed_ref[...].astype(jnp.float32) - times_ref[...] * velocity
    value = jnp.where(index_ref[0] == 1, state_ref[...].astype(jnp.float32) - estimate, estimate)
    out_ref[...] = value.astype(out_ref.dtype)


def result_of(index, times, mixed, state, lefts, rights):
    tokens, feats = mixed.shape
    depth = lefts[0].shape[1]

    def whole(array):
        return pl.BlockSpec(array.shape, lambda i, index: (0, 0))

    def columns(n):
        return pl.BlockSpec((depth, feats), lambda i, index: (0, index[n]))

    return pl.pallas_call(
        functools.partial(result_kernel, len(lefts)),
        grid_spec=pltpu.PrefetchScalarGridSpec(
            num_scalar_prefetch=1,
            grid=(1,),
            in_specs=[whole(array) for array in (times, mixed, state, *lefts)]
            + [columns(1)] + [columns(2)] * (len(rights) - 1),
            out_specs=whole(mixed),
        ),
        out_shape=jax.ShapeDtypeStruct((tokens, feats), jnp.bfloat16),
        compiler_params=params(),
        cost_estimate=pl.CostEstimate(
            flops=2 * tokens * depth * len(lefts) * feats,
            bytes_accessed=2 * len(lefts) * depth * (tokens + feats) + 6 * tokens * feats,
            transcendentals=0,
        ),
    )(index, times, mixed, state, *lefts, *rights)


def local(states, noise, span_lengths, step_index, gain, in_weights, out_weights):
    tokens_here, feats = states.shape[1:]
    group = lax.axis_index("grp")
    z, a, y, c = (lax.axis_index(name) for name in ("z", "a", "y", "c"))
    lengths = span_lengths[0]
    ends = jnp.cumsum(lengths)
    here = jnp.arange(tokens_here, dtype=jnp.int32)

    rows = crossed(jnp.transpose(in_weights[0], (1, 0, 2)))
    half = rows.shape[1]

    positions = (z * 2 + a) * tokens_here + here
    spans = jnp.sum((positions[:, None] >= ends[None, :]).astype(jnp.int32), axis=1)
    hits = spans[:, None] == jnp.arange(lengths.shape[0], dtype=jnp.int32)[None, :]
    picked = jnp.where(hits, (step_index[0][None, :] + 1).astype(jnp.float32), jnp.float32(0.0))
    times = (jnp.sum(picked, axis=1) / STEPS)[:, None]
    state = states[0].astype(jnp.float32)
    mixed = ((1.0 - times) * state + times * noise[0].astype(jnp.float32)).astype(jnp.bfloat16)

    kept = jnp.where(c == 0, mixed[:, :half], mixed[:, half:])
    given = jnp.where(c == 0, mixed[:, half:], mixed[:, :half])
    taken = swapped(given)
    mine = jnp.concatenate([jnp.where(c == 0, kept, taken), jnp.where(c == 0, taken, kept)], axis=1)
    own_gain = gain[0].reshape(8, 2, half)
    own_gain = jnp.where(c == 0, own_gain[:, 0], own_gain[:, 1]).reshape(4, 1, feats)

    other = shifted(tied(mine, rows)[0], "a", 1)
    near = both_ways(rows, rows, "z")
    mine_y = [mine, shifted(mine, "y", 1), None, shifted(mine, "y", -1)]
    mine_y[2] = shifted(tied(mine, mine_y[1], mine_y[3])[0], "y", 2)
    mine_y[1], mine_y[3], *near = tied(mine_y[1], mine_y[3], *near)
    middle = both_ways(*near, "z")
    other_y = [other, shifted(other, "y", 1), None, shifted(other, "y", -1)]
    other_y[2] = shifted(tied(other, other_y[1], other_y[3], mine_y[2])[0], "y", 2)
    mine_y[2], other_y[1], other_y[3], *middle = tied(mine_y[2], other_y[1], other_y[3], *middle)
    distant = both_ways(*middle, "z")

    def block_for(hop):
        return lax.dynamic_slice_in_dim(out_weights[0], (y - hop) % 4 * 2 * feats, 2 * feats, axis=1)

    near_out = tied(block_for(1), block_for(3), other_y[2])
    near_out = (shifted(near_out[0], "y", 1), shifted(near_out[1], "y", 3))

    along = jnp.arange(4, dtype=jnp.int32)
    order = (y + along) % 4
    laid = []
    squares = []
    for blocks in (mine_y, other_y):
        block, square = lay(blocks, own_gain, order)
        laid.append(block)
        squares.append(square)
    home = a == c
    square = jnp.where(home, squares[0], squares[1])
    square = square + swapped(jnp.where(home, squares[1], squares[0]))
    inverse_root = lax.rsqrt(square / (feats * 8) + 1e-06)
    at_home = jnp.full((1,), jnp.where(home, 1, 0), jnp.int32)

    def project_hops(hops, weights, part, last=False):
        where = jnp.stack([(z + hop) % 8 for hop in hops]).astype(jnp.int32)
        return project(where, at_home, *laid, weights, part, last)

    part = project_hops((0,), [(rows,)], None)
    part = project_hops((1, -1), [(near[0],), (near[1],)], part)
    part, inverse_root, *distant = tied(part, inverse_root, *distant)
    part = project_hops((2, -2), [(middle[0],), (middle[1],)], part)
    last = both_ways(distant[0][:, :half // 2], distant[1][:, half // 2:], "z")
    part = project_hops((3, -3), [(distant[0],), (distant[1],)], part)
    part, *last, one_out, three_out = tied(part, *last, *near_out)
    given, kept = project_hops((4,), [tuple(last)], part, True)
    cols = given.shape[1] // 3
    query, pairs = finish(kept, swapped(given), inverse_root)

    queries = (query, swapped(query))
    places = jnp.concatenate([(z * 2 + c) * tokens_here + here, (z * 2 + 1 - c) * tokens_here + here])
    limit = jnp.min(
        jnp.where(ends[None, :] > places[:, None], ends[None, :], ends[-1]), axis=1
    )
    limit = jnp.where(group == 1, ends[-1], limit).astype(jnp.int32)[:, None]

    def attend(hops, blocks, stat):
        bases = [(((z + hop) % 8) * 2 + c) * tokens_here for hop in hops]
        return flash(jnp.stack(bases), limit, queries, blocks, stat, hops == (4,))

    ahead, behind = both_ways(pairs, pairs, "z")
    two_out = shifted(tied(block_for(2), pairs, one_out)[0], "y", 2)
    stat = attend((0,), [(pairs, 0, pairs, cols)], None)
    for hop in (1, 2, 3):
        ahead, behind, *stat = tied(ahead, behind, *stat)
        if hop == 3:
            two_out, one_out, three_out, ahead, behind = tied(two_out, one_out, three_out, ahead, behind)
            outs = [block_for(0), one_out, two_out, three_out]
            partners = [swapped(block) for block in outs]
        if hop < 3:
            onward = both_ways(ahead, behind, "z")
        else:
            onward = both_ways(ahead[:, :cols], behind[:, cols:], "z")
        stat = attend((hop, -hop), [(ahead, 0, ahead, cols), (behind, 0, behind, cols)], stat)
        ahead, behind = onward
    ahead, behind, *rest = tied(ahead, behind, *stat, *partners)
    stat, partners = rest[:2], rest[2:]
    one, one_stat, two, two_stat = attend((4,), [(ahead, 0, behind, 0)], stat)
    attended = crossed(merge(one, one_stat, swapped(two), swapped(two_stat)))

    lefts, rights = [], []
    for hop in range(4):
        block = shifted(attended, "y", hop) if hop else attended
        lefts += [block, swapped(block)]
        rights += [outs[hop] if hop else out_weights[0], partners[hop]]
    index = jnp.stack([group, y * 2 + c, c]).astype(jnp.int32)
    result = result_of(index, times, mixed, states[0], lefts, rights)
    return shifted(result, "grp", 1)[None]


def solution(mesh):
    fine = jax.sharding.Mesh(mesh.devices.reshape(2, 8, 2, 4, 2), ("grp", "z", "a", "y", "c"))
    tokens, features = ("z", "a"), ("y", "c")
    return jax.shard_map(
        local,
        mesh=fine,
        in_specs=(
            P("grp", tokens, features),
            P("grp", tokens, features),
            P("grp", None),
            P("grp", None),
            P("grp", None),
            P("grp", tokens, None, features),
            P("grp", features, None),
        ),
        out_specs=P("grp", tokens, features),
        check_vma=False,
    )
```

```python
import functools

import jax
import jax.numpy as jnp
from jax import lax
from jax.experimental import pallas as pl
from jax.experimental.pallas import tpu as pltpu
from jax.sharding import PartitionSpec as P

HEAD_DIM = 128
STEPS = 4
LOW = -1e30
SCALE2 = HEAD_DIM ** (-0.5) * 1.4426950408889634


def crossed(block):
    return lax.ppermute(block, ("a", "c"), [(0, 0), (1, 2), (2, 1), (3, 3)])


def shifted(block, axis, hop):
    count = lax.axis_size(axis)
    return lax.ppermute(block, axis, [(i, (i - hop) % count) for i in range(count)])


def crossed_along(block, hop):
    route = []
    for a in range(2):
        for y in range(4):
            for c in range(2):
                route.append(((a * 4 + y) * 2 + c, (c * 4 + (y - hop) % 4) * 2 + a))
    return lax.ppermute(block, ("a", "y", "c"), route)


def swapped(block):
    return shifted(block, "c", 1)


def both_ways(ahead, behind, axis):
    return shifted(ahead, axis, 1), shifted(behind, axis, -1)


def tied(*values):
    return lax.optimization_barrier(values)


def params():
    return pltpu.CompilerParams(vmem_limit_bytes=32 * 1024 * 1024)


def in_vmem():
    return pl.BlockSpec(memory_space=pltpu.VMEM)


def lay_kernel(order_ref, gain_ref, *refs):
    x_refs, out_ref, square_ref = refs[:-2], refs[-2], refs[-1]
    step = pl.program_id(0)
    half = out_ref.shape[2]
    for n, x_ref in enumerate(x_refs):

        @pl.when(step == n)
        def _():
            wide = x_ref[...].astype(jnp.float32)
            scaled = (wide * gain_ref[0]).astype(out_ref.dtype)
            out_ref[0] = scaled[:, :half]
            out_ref[1] = scaled[:, half:]
            square = jnp.sum(wide * wide, axis=1, keepdims=True)
            square_ref[...] = jnp.where(step == 0, square, square_ref[...] + square)


def lay(xs, gain, order):
    blocks = gain.shape[0]
    tokens, feats = xs[0].shape
    return pl.pallas_call(
        lay_kernel,
        grid_spec=pltpu.PrefetchScalarGridSpec(
            num_scalar_prefetch=1,
            grid=(blocks,),
            in_specs=[pl.BlockSpec((1, 1, feats), lambda i, where: (where[i], 0, 0))]
            + [pl.BlockSpec((tokens, feats), lambda i, where: (0, 0))] * blocks,
            out_specs=[
                pl.BlockSpec((2, tokens, feats // 2), lambda i, where: (where[i], 0, 0)),
                pl.BlockSpec((tokens, 1), lambda i, where: (0, 0)),
            ],
        ),
        out_shape=[
            jax.ShapeDtypeStruct((2 * blocks, tokens, feats // 2), jnp.bfloat16),
            jax.ShapeDtypeStruct((tokens, 1), jnp.float32),
        ],
        compiler_params=params(),
        cost_estimate=pl.CostEstimate(
            flops=3 * blocks * tokens * feats, bytes_accessed=4 * blocks * tokens * feats, transcendentals=0
        ),
    )(order, gain, *xs)


def project_kernel(parts, first, last, where_ref, home_ref, *refs):
    blocks = len(parts)
    acts, refs = refs[:2 * blocks], refs[2 * blocks:]
    weights = []
    for count in parts:
        weights.append(refs[:count])
        refs = refs[count:]
    if not first:
        part_ref, refs = refs[0], refs[1:]
    kinds, _, width = weights[0][0].shape
    home = home_ref[0]
    for side in range(2) if last is None else (last,):
        for kind in range(kinds):
            cols = slice(kind * width, (kind + 1) * width)
            value = 0.0
            for n in range(blocks):
                mine, other = acts[2 * n][0], acts[2 * n + 1][0]
                if last is not None:
                    left = jnp.where(home == side, mine, other)
                else:
                    left = (mine, other)[side]
                right = jnp.concatenate([ref[kind] for ref in weights[n]], axis=0)
                value = value + jnp.dot(left, right, preferred_element_type=jnp.float32)
            if last is not None:
                value = value + part_ref[jnp.where(home == side, 0, 1), :, cols]
                refs[0][:, cols] = value.astype(refs[0].dtype)
            else:
                if not first:
                    value = value + part_ref[side, :, cols]
                refs[0][side, :, cols] = value


def project(where, home, mine, other, weights, part, last):
    tokens, depth = mine.shape[1:]
    kinds, _, width = weights[0][0].shape
    blocks = len(weights)

    def chosen(n):
        return pl.BlockSpec((1, tokens, depth), lambda i, where, home: (where[n], 0, 0))

    def whole(shape):
        return pl.BlockSpec(shape, lambda i, where, home: (0,) * len(shape))

    flat, deep = (tokens, kinds * width), (2, tokens, kinds * width)
    operands, in_specs = [], []
    for n in range(blocks):
        operands += [mine, other]
        in_specs += [chosen(n)] * 2
    for group in weights:
        operands += group
        in_specs += [whole(array.shape) for array in group]
    if part is not None:
        operands.append(part)
        in_specs.append(whole(deep))
    if last is not None:
        out_specs, out_shape = whole(flat), jax.ShapeDtypeStruct(flat, (jnp.bfloat16, jnp.float32)[last])
    else:
        out_specs, out_shape = whole(deep), jax.ShapeDtypeStruct(deep, jnp.float32)
    return pl.pallas_call(
        functools.partial(project_kernel, [len(group) for group in weights], part is None, last),
        grid_spec=pltpu.PrefetchScalarGridSpec(
            num_scalar_prefetch=2, grid=(1,), in_specs=in_specs, out_specs=out_specs
        ),
        out_shape=out_shape,
        compiler_params=params(),
        cost_estimate=pl.CostEstimate(
            flops=4 * tokens * depth * blocks * kinds * width,
            bytes_accessed=2 * blocks * depth * (2 * tokens + kinds * width) + 16 * tokens * kinds * width,
            transcendentals=0,
        ),
    )(where, home, *operands)


def finish_kernel(kept_ref, came_ref, scale_ref, query_ref, pairs_ref):
    value = (kept_ref[...] + came_ref[...].astype(jnp.float32)) * scale_ref[...]
    value = value.astype(query_ref.dtype)

    @pl.when(pl.program_id(0) == 0)
    def _():
        query_ref[...] = value

    @pl.when(pl.program_id(0) > 0)
    def _():
        pairs_ref[...] = value


def finish(kept, came, scale):
    tokens, width = kept.shape[0], kept.shape[1] // 3
    part = pl.BlockSpec((tokens, width), lambda i: (0, i))
    return pl.pallas_call(
        finish_kernel,
        grid=(3,),
        in_specs=[part, part, pl.BlockSpec((tokens, 1), lambda i: (0, 0))],
        out_specs=[
            pl.BlockSpec((tokens, width), lambda i: (0, 0)),
            pl.BlockSpec((tokens, width), lambda i: (0, jnp.maximum(i - 1, 0))),
        ],
        out_shape=[
            jax.ShapeDtypeStruct((tokens, width), jnp.bfloat16),
            jax.ShapeDtypeStruct((tokens, 2 * width), jnp.bfloat16),
        ],
        compiler_params=params(),
        cost_estimate=pl.CostEstimate(
            flops=2 * kept.size, bytes_accessed=8 * kept.size, transcendentals=0
        ),
    )(kept, came, scale)


def flash_kernel(spots, first, last, base_ref, limit_ref, *refs):
    n_blocks = len(spots)
    queries, refs = refs[:2], refs[2:]
    n_arrays = 1 + max(max(spot[0], spot[2]) for spot in spots)
    arrays, rest = refs[:n_arrays], refs[n_arrays:]
    if not first:
        acc_in, stat_in = rest[:2]
        rest = rest[2:]
    rows, width = queries[0].shape
    heads = width // HEAD_DIM
    for side in range(2):
        span = slice(side * rows, (side + 1) * rows)
        limit = limit_ref[span, :]
        for head in range(heads):
            cols = slice(head * HEAD_DIM, (head + 1) * HEAD_DIM)
            query = queries[side][:, cols]
            scores = []
            for block, (array, start, _, _) in enumerate(spots):
                start = start + head * HEAD_DIM
                score = lax.dot_general(
                    query, arrays[array][:, start:start + HEAD_DIM], (((1,), (1,)), ((), ())),
                    preferred_element_type=jnp.float32,
                )
                place = lax.broadcasted_iota(jnp.int32, score.shape, 1)
                scores.append(jnp.where(place < limit - base_ref[block], score, LOW))
            high = functools.reduce(
                jnp.maximum, [jnp.max(score, axis=1, keepdims=True) for score in scores]
            )
            if not first:
                before = stat_in[span, head:head + 1]
                high = jnp.maximum(high, before)
            shift = high * SCALE2
            total, output = 0.0, 0.0
            for block, (_, _, array, start) in enumerate(spots):
                start = start + head * HEAD_DIM
                weight = jnp.exp2(scores[block] * SCALE2 - shift)
                total = total + jnp.sum(weight, axis=1, keepdims=True)
                output = output + jnp.dot(
                    weight.astype(jnp.bfloat16), arrays[array][:, start:start + HEAD_DIM],
                    preferred_element_type=jnp.float32,
                )
            if not first:
                shrink = jnp.exp2((before - high) * SCALE2)
                total = total + stat_in[span, heads + head:heads + head + 1] * shrink
                output = output + acc_in[span, cols] * shrink
            acc_out, stat_out = rest[2 * side:2 * side + 2] if last else rest
            place = slice(0, rows) if last else span
            acc_out[place, cols] = output
            stat_out[place, head:head + 1] = high
            stat_out[place, heads + head:heads + head + 1] = total


def flash(bases, limit, queries, blocks, stat, last):
    rows, width = queries[0].shape
    count = blocks[0][0].shape[0]
    arrays, spots = [], []
    for key, key_start, value, value_start in blocks:
        spot = []
        for array, start in ((key, key_start), (value, value_start)):
            known = [n for n, seen in enumerate(arrays) if seen is array]
            if not known:
                known = [len(arrays)]
                arrays.append(array)
            spot += [known[0], start]
        spots.append(tuple(spot))
    operands = [bases, limit, *queries, *arrays]
    operands += [] if stat is None else list(stat)
    sides = 1 if last else 2
    shapes = [
        jax.ShapeDtypeStruct((sides * rows, width), jnp.float32),
        jax.ShapeDtypeStruct((sides * rows, 128), jnp.float32),
    ]
    work = 2 * rows * count * len(blocks) * width
    return pl.pallas_call(
        functools.partial(flash_kernel, tuple(spots), stat is None, last),
        in_specs=[pl.BlockSpec(memory_space=pltpu.SMEM)] + [in_vmem()] * (len(operands) - 1),
        out_specs=[in_vmem()] * (2 * (3 - sides)),
        out_shape=shapes * (3 - sides),
        compiler_params=params(),
        cost_estimate=pl.CostEstimate(
            flops=4 * work,
            bytes_accessed=4 * len(blocks) * count * width + 20 * rows * width,
            transcendentals=work // HEAD_DIM,
        ),
    )(*operands)


def merge_kernel(one_ref, one_stat, two_ref, two_stat, out_ref):
    heads = out_ref.shape[1] // HEAD_DIM
    for head in range(heads):
        cols = slice(head * HEAD_DIM, (head + 1) * HEAD_DIM)
        top, low = slice(head, head + 1), slice(heads + head, heads + head + 1)
        high = jnp.maximum(one_stat[:, top], two_stat[:, top])
        one = jnp.exp2((one_stat[:, top] - high) * SCALE2)
        two = jnp.exp2((two_stat[:, top] - high) * SCALE2)
        total = one_stat[:, low] * one + two_stat[:, low] * two
        value = (one_ref[:, cols] * one + two_ref[:, cols] * two) / total
        out_ref[:, cols] = value.astype(out_ref.dtype)


def merge(one, one_stat, two, two_stat):
    return pl.pallas_call(
        merge_kernel,
        in_specs=[in_vmem()] * 4,
        out_specs=in_vmem(),
        out_shape=jax.ShapeDtypeStruct(one.shape, jnp.bfloat16),
        compiler_params=params(),
        cost_estimate=pl.CostEstimate(flops=4 * one.size, bytes_accessed=10 * one.size, transcendentals=0),
    )(one, one_stat, two, two_stat)


def result_kernel(n_blocks, index_ref, times_ref, mixed_ref, state_ref, *refs):
    lefts, rights, out_ref = refs[:n_blocks], refs[n_blocks:-1], refs[-1]
    velocity = 0.0
    for left, right in zip(lefts, rights):
        velocity = velocity + jnp.dot(left[...], right[...], preferred_element_type=jnp.float32)
    estimate = mixed_ref[...].astype(jnp.float32) - times_ref[...] * velocity
    value = jnp.where(index_ref[0] == 1, state_ref[...].astype(jnp.float32) - estimate, estimate)
    out_ref[...] = value.astype(out_ref.dtype)


def result_of(index, times, mixed, state, lefts, rights):
    tokens, feats = mixed.shape
    depth = lefts[0].shape[1]

    def whole(array):
        return pl.BlockSpec(array.shape, lambda i, index: (0, 0))

    columns = pl.BlockSpec((depth, feats), lambda i, index: (0, index[1]))
    return pl.pallas_call(
        functools.partial(result_kernel, len(lefts)),
        grid_spec=pltpu.PrefetchScalarGridSpec(
            num_scalar_prefetch=1,
            grid=(1,),
            in_specs=[whole(array) for array in (times, mixed, state, *lefts)]
            + [columns] * len(rights),
            out_specs=whole(mixed),
        ),
        out_shape=jax.ShapeDtypeStruct((tokens, feats), jnp.bfloat16),
        compiler_params=params(),
        cost_estimate=pl.CostEstimate(
            flops=2 * tokens * depth * len(lefts) * feats,
            bytes_accessed=2 * len(lefts) * depth * (tokens + feats) + 6 * tokens * feats,
            transcendentals=0,
        ),
    )(index, times, mixed, state, *lefts, *rights)


def local(states, noise, span_lengths, step_index, gain, in_weights, out_weights):
    tokens_here, feats = states.shape[1:]
    group = lax.axis_index("grp")
    z, a, y, c = (lax.axis_index(name) for name in ("z", "a", "y", "c"))
    lengths = span_lengths[0]
    ends = jnp.cumsum(lengths)
    here = jnp.arange(tokens_here, dtype=jnp.int32)

    rows = crossed(jnp.transpose(in_weights[0], (1, 0, 2)))
    half = rows.shape[1]

    positions = (z * 2 + a) * tokens_here + here
    spans = jnp.sum((positions[:, None] >= ends[None, :]).astype(jnp.int32), axis=1)
    hits = spans[:, None] == jnp.arange(lengths.shape[0], dtype=jnp.int32)[None, :]
    picked = jnp.where(hits, (step_index[0][None, :] + 1).astype(jnp.float32), jnp.float32(0.0))
    times = (jnp.sum(picked, axis=1) / STEPS)[:, None]
    state = states[0].astype(jnp.float32)
    mixed = ((1.0 - times) * state + times * noise[0].astype(jnp.float32)).astype(jnp.bfloat16)

    kept = jnp.where(c == 0, mixed[:, :half], mixed[:, half:])
    given = jnp.where(c == 0, mixed[:, half:], mixed[:, :half])
    taken = swapped(given)
    mine = jnp.concatenate([jnp.where(c == 0, kept, taken), jnp.where(c == 0, taken, kept)], axis=1)
    own_gain = gain[0].reshape(8, 2, half)
    own_gain = jnp.where(c == 0, own_gain[:, 0], own_gain[:, 1]).reshape(4, 1, feats)

    other = shifted(tied(mine, rows)[0], "a", 1)
    near = both_ways(rows, rows, "z")
    mine_y = [mine, shifted(mine, "y", 1), None, shifted(mine, "y", -1)]
    mine_y[2] = shifted(tied(mine, mine_y[1], mine_y[3])[0], "y", 2)
    mine_y[1], mine_y[3], *near = tied(mine_y[1], mine_y[3], *near)
    middle = both_ways(*near, "z")

    def block_for(hop):
        return lax.dynamic_slice_in_dim(out_weights[0], (y - hop) % 4 * 2 * feats, 2 * feats, axis=1)

    other, *outs = tied(other, *[block_for(hop) for hop in range(4)])
    other_y = [other, shifted(other, "y", 1), None, shifted(other, "y", -1)]
    other_y[2] = shifted(tied(other, other_y[1], other_y[3], mine_y[2])[0], "y", 2)
    mine_y[2], other_y[1], other_y[3], *middle = tied(mine_y[2], other_y[1], other_y[3], *middle)
    distant = both_ways(*middle, "z")

    outs[1], outs[3], _ = tied(outs[1], outs[3], other_y[2])
    near_out = (shifted(outs[1], "y", 1), shifted(outs[3], "y", 3))

    along = jnp.arange(4, dtype=jnp.int32)
    order = (y + along) % 4
    laid = []
    squares = []
    for blocks in (mine_y, other_y):
        block, square = lay(blocks, own_gain, order)
        laid.append(block)
        squares.append(square)
    home = a == c
    square = jnp.where(home, squares[0], squares[1])
    square = square + swapped(jnp.where(home, squares[1], squares[0]))
    inverse_root = lax.rsqrt(square / (feats * 8) + 1e-06)
    at_home = jnp.full((1,), jnp.where(home, 1, 0), jnp.int32)

    def project_hops(hops, weights, part, last=None):
        where = jnp.stack([(z + hop) % 8 for hop in hops]).astype(jnp.int32)
        return project(where, at_home, *laid, weights, part, last)

    part = project_hops((0,), [(rows,)], None)
    part = project_hops((1, -1), [(near[0],), (near[1],)], part)
    part, inverse_root, *distant = tied(part, inverse_root, *distant)
    part = project_hops((2, -2), [(middle[0],), (middle[1],)], part)
    last = both_ways(distant[0][:, :half // 2], distant[1][:, half // 2:], "z")
    part = project_hops((3, -3), [(distant[0],), (distant[1],)], part)
    partners = [swapped(outs[0]), None, None, None]
    part, *last, outs[1], outs[3], partners[0] = tied(part, *last, *near_out, partners[0])
    given = project_hops((4,), [tuple(last)], part, 0)
    came = swapped(given)
    kept = project_hops((4,), [tuple(last)], part, 1)
    cols = given.shape[1] // 3
    query, pairs = finish(kept, came, inverse_root)

    queries = (query, swapped(query))
    places = jnp.concatenate([(z * 2 + c) * tokens_here + here, (z * 2 + 1 - c) * tokens_here + here])
    limit = jnp.min(
        jnp.where(ends[None, :] > places[:, None], ends[None, :], ends[-1]), axis=1
    )
    limit = jnp.where(group == 1, ends[-1], limit).astype(jnp.int32)[:, None]

    def attend(hops, blocks, stat):
        bases = [(((z + hop) % 8) * 2 + c) * tokens_here for hop in hops]
        return flash(jnp.stack(bases), limit, queries, blocks, stat, hops == (4,))

    ahead, behind = both_ways(pairs, pairs, "z")
    outs[2] = shifted(tied(outs[2], pairs, outs[1])[0], "y", 2)
    partners[1] = swapped(outs[1])
    stat = attend((0,), [(pairs, 0, pairs, cols)], None)
    for hop in (1, 2, 3):
        ahead, behind, *stat = tied(ahead, behind, *stat)
        if hop == 2:
            partners[1], outs[2], ahead, behind = tied(partners[1], outs[2], ahead, behind)
            partners[3] = swapped(tied(outs[3], stat[0])[0])
        if hop == 3:
            partners[3], ahead, behind = tied(partners[3], ahead, behind)
            partners[2] = swapped(outs[2])
        if hop < 3:
            onward = both_ways(ahead, behind, "z")
        else:
            onward = both_ways(ahead[:, :cols], behind[:, cols:], "z")
        stat = attend((hop, -hop), [(ahead, 0, ahead, cols), (behind, 0, behind, cols)], stat)
        ahead, behind = onward
    ahead, behind, partners[2], *stat = tied(ahead, behind, partners[2], *stat)
    one, one_stat, two, two_stat = attend((4,), [(ahead, 0, behind, 0)], stat)
    attended = merge(one, one_stat, swapped(two), swapped(two_stat))

    lefts, rights = [], []
    for hop in (2, 1, 3, 0):
        block = crossed_along(attended, hop)
        lefts += [block, swapped(block)]
        rights += [outs[hop], partners[hop]]
    index = jnp.stack([group, c]).astype(jnp.int32)
    result = result_of(index, times, mixed, states[0], lefts, rights)
    return shifted(result, "grp", 1)[None]


def solution(mesh):
    fine = jax.sharding.Mesh(mesh.devices.reshape(2, 8, 2, 4, 2), ("grp", "z", "a", "y", "c"))
    tokens, features = ("z", "a"), ("y", "c")
    return jax.shard_map(
        local,
        mesh=fine,
        in_specs=(
            P("grp", tokens, features),
            P("grp", tokens, features),
            P("grp", None),
            P("grp", None),
            P("grp", None),
            P("grp", tokens, None, features),
            P("grp", features, None),
        ),
        out_specs=P("grp", tokens, features),
        check_vma=False,
    )
```

```python
import functools

import jax
import jax.numpy as jnp
from jax import lax
from jax.experimental import pallas as pl
from jax.experimental.pallas import tpu as pltpu
from jax.sharding import PartitionSpec as P

HEAD_DIM = 128
STEPS = 4
LOW = -1e30
SCALE2 = HEAD_DIM ** (-0.5) * 1.4426950408889634


def crossed(block):
    return lax.ppermute(block, ("a", "c"), [(0, 0), (1, 2), (2, 1), (3, 3)])


def shifted(block, axis, hop):
    count = lax.axis_size(axis)
    return lax.ppermute(block, axis, [(i, (i - hop) % count) for i in range(count)])


def crossed_along(block, hop):
    route = []
    for a in range(2):
        for y in range(4):
            for c in range(2):
                route.append(((a * 4 + y) * 2 + c, (c * 4 + (y - hop) % 4) * 2 + a))
    return lax.ppermute(block, ("a", "y", "c"), route)


def swapped(block):
    return shifted(block, "c", 1)


def both_ways(ahead, behind, axis):
    return shifted(ahead, axis, 1), shifted(behind, axis, -1)


def tied(*values):
    return lax.optimization_barrier(values)


def params():
    return pltpu.CompilerParams(vmem_limit_bytes=32 * 1024 * 1024)


def hint(flops, bytes_accessed, transcendentals):
    return pl.CostEstimate(
        flops=flops // 16, bytes_accessed=bytes_accessed // 16, transcendentals=transcendentals // 16
    )


def in_vmem():
    return pl.BlockSpec(memory_space=pltpu.VMEM)


def lay_kernel(order_ref, gain_ref, *refs):
    x_refs, out_ref, square_ref = refs[:-2], refs[-2], refs[-1]
    step = pl.program_id(0)
    half = out_ref.shape[2]
    for n, x_ref in enumerate(x_refs):

        @pl.when(step == n)
        def _():
            wide = x_ref[...].astype(jnp.float32)
            scaled = (wide * gain_ref[0]).astype(out_ref.dtype)
            out_ref[0] = scaled[:, :half]
            out_ref[1] = scaled[:, half:]
            square = jnp.sum(wide * wide, axis=1, keepdims=True)
            square_ref[...] = jnp.where(step == 0, square, square_ref[...] + square)


def lay(xs, gain, order):
    blocks = gain.shape[0]
    tokens, feats = xs[0].shape
    return pl.pallas_call(
        lay_kernel,
        grid_spec=pltpu.PrefetchScalarGridSpec(
            num_scalar_prefetch=1,
            grid=(blocks,),
            in_specs=[pl.BlockSpec((1, 1, feats), lambda i, where: (where[i], 0, 0))]
            + [pl.BlockSpec((tokens, feats), lambda i, where: (0, 0))] * blocks,
            out_specs=[
                pl.BlockSpec((2, tokens, feats // 2), lambda i, where: (where[i], 0, 0)),
                pl.BlockSpec((tokens, 1), lambda i, where: (0, 0)),
            ],
        ),
        out_shape=[
            jax.ShapeDtypeStruct((2 * blocks, tokens, feats // 2), jnp.bfloat16),
            jax.ShapeDtypeStruct((tokens, 1), jnp.float32),
        ],
        compiler_params=params(),
        cost_estimate=hint(
            flops=3 * blocks * tokens * feats, bytes_accessed=4 * blocks * tokens * feats, transcendentals=0
        ),
    )(order, gain, *xs)


def project_kernel(side, parts, spot_ref, mine_ref, other_ref, *refs):
    weights = []
    for count in parts:
        weights.append(refs[:count])
        refs = refs[count:]
    out_ref = refs[-1]
    kinds, _, width = weights[0][0].shape
    tokens = mine_ref.shape[1]
    for turn, tokens_of in enumerate((0, 1) if side == 2 else (side,)):
        wanted = spot_ref[0] == tokens_of
        for kind in range(kinds):
            cols = slice(kind * width, (kind + 1) * width)
            value = 0.0
            for n, group in enumerate(weights):
                left = jnp.where(wanted, mine_ref[spot_ref[1 + n]], other_ref[spot_ref[1 + n]])
                right = jnp.concatenate([ref[kind] for ref in group], axis=0)
                value = value + jnp.dot(left, right, preferred_element_type=jnp.float32)
            if side == 1:
                value = (value + refs[0][:, cols].astype(jnp.float32)) * refs[1][...]
            out_ref[turn * tokens:(turn + 1) * tokens, cols] = value.astype(out_ref.dtype)


def project(side, spots, mine, other, weights, more=()):
    tokens, depth = mine.shape[1:]
    kinds, _, width = weights[0][0].shape
    operands = [mine, other] + [array for group in weights for array in group] + list(more)
    return pl.pallas_call(
        functools.partial(project_kernel, side, [len(group) for group in weights]),
        in_specs=[pl.BlockSpec(memory_space=pltpu.SMEM)] + [in_vmem()] * len(operands),
        out_specs=in_vmem(),
        out_shape=jax.ShapeDtypeStruct(((1 + side // 2) * tokens, kinds * width), jnp.bfloat16),
        compiler_params=params(),
        cost_estimate=hint(
            flops=2 * tokens * depth * len(weights) * kinds * width,
            bytes_accessed=2 * len(weights) * depth * (2 * tokens + kinds * width) + 4 * tokens * kinds * width,
            transcendentals=0,
        ),
    )(spots, *operands)


def queries_kernel(part_ref, came_ref, own_scale, other_scale, own_ref, other_ref):
    rows = own_ref.shape[0]
    own = part_ref[rows:, :].astype(jnp.float32) + came_ref[:rows, :].astype(jnp.float32)
    other = part_ref[:rows, :].astype(jnp.float32) + came_ref[rows:, :].astype(jnp.float32)
    own_ref[...] = (own * own_scale[...]).astype(own_ref.dtype)
    other_ref[...] = (other * other_scale[...]).astype(other_ref.dtype)


def queries_of(part, came, own_scale, other_scale):
    rows, width = part.shape[0] // 2, part.shape[1]
    return pl.pallas_call(
        queries_kernel,
        in_specs=[in_vmem()] * 4,
        out_specs=[in_vmem()] * 2,
        out_shape=[jax.ShapeDtypeStruct((rows, width), jnp.bfloat16)] * 2,
        compiler_params=params(),
        cost_estimate=hint(flops=3 * part.size, bytes_accessed=6 * part.size, transcendentals=0),
    )(part, came, own_scale, other_scale)


def flash_kernel(spots, first, last, base_ref, limit_ref, *refs):
    n_blocks = len(spots)
    queries, refs = refs[:2], refs[2:]
    n_arrays = 1 + max(max(spot[0], spot[2]) for spot in spots)
    arrays, rest = refs[:n_arrays], refs[n_arrays:]
    if not first:
        acc_in, stat_in = rest[:2]
        rest = rest[2:]
    rows, width = queries[0].shape
    heads = width // HEAD_DIM
    for side in range(2):
        span = slice(side * rows, (side + 1) * rows)
        limit = limit_ref[span, :]
        for head in range(heads):
            cols = slice(head * HEAD_DIM, (head + 1) * HEAD_DIM)
            query = queries[side][:, cols]
            scores = []
            for block, (array, start, _, _) in enumerate(spots):
                start = start + head * HEAD_DIM
                score = lax.dot_general(
                    query, arrays[array][:, start:start + HEAD_DIM], (((1,), (1,)), ((), ())),
                    preferred_element_type=jnp.float32,
                )
                place = lax.broadcasted_iota(jnp.int32, score.shape, 1)
                scores.append(jnp.where(place < limit - base_ref[block], score, LOW))
            high = functools.reduce(
                jnp.maximum, [jnp.max(score, axis=1, keepdims=True) for score in scores]
            )
            if not first:
                before = stat_in[span, head:head + 1]
                high = jnp.maximum(high, before)
            shift = high * SCALE2
            total, output = 0.0, 0.0
            for block, (_, _, array, start) in enumerate(spots):
                start = start + head * HEAD_DIM
                weight = jnp.exp2(scores[block] * SCALE2 - shift)
                total = total + jnp.sum(weight, axis=1, keepdims=True)
                output = output + jnp.dot(
                    weight.astype(jnp.bfloat16), arrays[array][:, start:start + HEAD_DIM],
                    preferred_element_type=jnp.float32,
                )
            if not first:
                shrink = jnp.exp2((before - high) * SCALE2)
                total = total + stat_in[span, heads + head:heads + head + 1] * shrink
                output = output + acc_in[span, cols] * shrink
            acc_out, stat_out = rest[2 * side:2 * side + 2] if last else rest
            place = slice(0, rows) if last else span
            acc_out[place, cols] = output
            stat_out[place, head:head + 1] = high
            stat_out[place, heads + head:heads + head + 1] = total


def flash(bases, limit, queries, blocks, stat, last):
    rows, width = queries[0].shape
    count = blocks[0][0].shape[0]
    arrays, spots = [], []
    for key, key_start, value, value_start in blocks:
        spot = []
        for array, start in ((key, key_start), (value, value_start)):
            known = [n for n, seen in enumerate(arrays) if seen is array]
            if not known:
                known = [len(arrays)]
                arrays.append(array)
            spot += [known[0], start]
        spots.append(tuple(spot))
    operands = [bases, limit, *queries, *arrays]
    operands += [] if stat is None else list(stat)
    sides = 1 if last else 2
    shapes = [
        jax.ShapeDtypeStruct((sides * rows, width), jnp.float32),
        jax.ShapeDtypeStruct((sides * rows, 128), jnp.float32),
    ]
    work = 2 * rows * count * len(blocks) * width
    return pl.pallas_call(
        functools.partial(flash_kernel, tuple(spots), stat is None, last),
        in_specs=[pl.BlockSpec(memory_space=pltpu.SMEM)] + [in_vmem()] * (len(operands) - 1),
        out_specs=[in_vmem()] * (2 * (3 - sides)),
        out_shape=shapes * (3 - sides),
        compiler_params=params(),
        cost_estimate=hint(
            flops=4 * work,
            bytes_accessed=4 * len(blocks) * count * width + 20 * rows * width,
            transcendentals=work // HEAD_DIM,
        ),
    )(*operands)


def merge_kernel(one_ref, one_stat, two_ref, two_stat, out_ref):
    heads = out_ref.shape[1] // HEAD_DIM
    for head in range(heads):
        cols = slice(head * HEAD_DIM, (head + 1) * HEAD_DIM)
        top, low = slice(head, head + 1), slice(heads + head, heads + head + 1)
        high = jnp.maximum(one_stat[:, top], two_stat[:, top])
        one = jnp.exp2((one_stat[:, top] - high) * SCALE2)
        two = jnp.exp2((two_stat[:, top] - high) * SCALE2)
        total = one_stat[:, low] * one + two_stat[:, low] * two
        value = (one_ref[:, cols] * one + two_ref[:, cols] * two) / total
        out_ref[:, cols] = value.astype(out_ref.dtype)


def merge(one, one_stat, two, two_stat):
    return pl.pallas_call(
        merge_kernel,
        in_specs=[in_vmem()] * 4,
        out_specs=in_vmem(),
        out_shape=jax.ShapeDtypeStruct(one.shape, jnp.bfloat16),
        compiler_params=params(),
        cost_estimate=hint(flops=4 * one.size, bytes_accessed=10 * one.size, transcendentals=0),
    )(one, one_stat, two, two_stat)


def result_kernel(n_blocks, teacher_ref, times_ref, mixed_ref, state_ref, *refs):
    lefts, rights, out_ref = refs[:n_blocks], refs[n_blocks:-1], refs[-1]
    velocity = 0.0
    for left, right in zip(lefts, rights):
        velocity = velocity + jnp.dot(left[...], right[...], preferred_element_type=jnp.float32)
    estimate = mixed_ref[...].astype(jnp.float32) - times_ref[...] * velocity
    value = jnp.where(teacher_ref[0] == 1, state_ref[...].astype(jnp.float32) - estimate, estimate)
    out_ref[...] = value.astype(out_ref.dtype)


def result_of(teacher, times, mixed, state, lefts, rights):
    tokens, feats = mixed.shape
    depth = lefts[0].shape[1]
    return pl.pallas_call(
        functools.partial(result_kernel, len(lefts)),
        in_specs=[pl.BlockSpec(memory_space=pltpu.SMEM)] + [in_vmem()] * (3 + len(lefts) + len(rights)),
        out_specs=in_vmem(),
        out_shape=jax.ShapeDtypeStruct((tokens, feats), jnp.bfloat16),
        compiler_params=params(),
        cost_estimate=hint(
            flops=2 * tokens * depth * len(lefts) * feats,
            bytes_accessed=2 * len(lefts) * depth * (tokens + feats) + 6 * tokens * feats,
            transcendentals=0,
        ),
    )(teacher, times, mixed, state, *lefts, *rights)


def local(states, noise, span_lengths, step_index, gain, in_weights, out_weights):
    tokens_here, feats = states.shape[1:]
    group = lax.axis_index("grp")
    z, a, y, c = (lax.axis_index(name) for name in ("z", "a", "y", "c"))
    lengths = span_lengths[0]
    ends = jnp.cumsum(lengths)
    here = jnp.arange(tokens_here, dtype=jnp.int32)

    rows = jnp.transpose(in_weights[0], (1, 0, 2))
    rows_q, rows = rows[:1], crossed(rows[1:])
    half = rows.shape[1]

    positions = (z * 2 + a) * tokens_here + here
    spans = jnp.sum((positions[:, None] >= ends[None, :]).astype(jnp.int32), axis=1)
    hits = spans[:, None] == jnp.arange(lengths.shape[0], dtype=jnp.int32)[None, :]
    picked = jnp.where(hits, (step_index[0][None, :] + 1).astype(jnp.float32), jnp.float32(0.0))
    times = (jnp.sum(picked, axis=1) / STEPS)[:, None]
    state = states[0].astype(jnp.float32)
    mixed = ((1.0 - times) * state + times * noise[0].astype(jnp.float32)).astype(jnp.bfloat16)

    kept = jnp.where(c == 0, mixed[:, :half], mixed[:, half:])
    given = jnp.where(c == 0, mixed[:, half:], mixed[:, :half])
    taken = swapped(given)
    mine = jnp.concatenate([jnp.where(c == 0, kept, taken), jnp.where(c == 0, taken, kept)], axis=1)
    own_gain = gain[0].reshape(8, 2, half)
    own_gain = jnp.where(c == 0, own_gain[:, 0], own_gain[:, 1]).reshape(4, 1, feats)

    other = shifted(tied(mine, rows)[0], "a", 1)
    near = both_ways(rows, rows, "z")
    mine_y = [mine, shifted(mine, "y", 1), None, shifted(mine, "y", -1)]
    mine_y[2] = shifted(tied(mine, mine_y[1], mine_y[3])[0], "y", 2)
    rows_q = crossed(tied(rows_q, mine_y[1])[0])
    mine_y[1], mine_y[3], *near = tied(mine_y[1], mine_y[3], *near)
    middle = both_ways(*near, "z")

    def block_for(hop, core):
        return lax.dynamic_slice_in_dim(out_weights[0], ((y - hop) % 4 * 2 + core) * feats, feats, axis=1)

    other, rows_q, *outs = tied(
        other, rows_q, *[block_for(hop, core) for hop in range(4) for core in (c, 1 - c)]
    )

    def moved(n, *after):
        return shifted(tied(outs[n], *after)[0], "y", n // 2)

    other_y = [other, shifted(other, "y", 1), None, shifted(other, "y", -1)]
    other_y[2] = shifted(tied(other, other_y[1], other_y[3], mine_y[2])[0], "y", 2)
    mine_y[2], other_y[1], other_y[3], *middle = tied(mine_y[2], other_y[1], other_y[3], *middle)
    distant = both_ways(*middle, "z")
    outs[2] = moved(2, other_y[2])

    rows_q, *distant = tied(rows_q, *distant)
    near_q = both_ways(rows_q, rows_q, "z")

    along = jnp.arange(4, dtype=jnp.int32)
    order = (y + along) % 4
    mine_laid, mine_square = lay(mine_y, own_gain, order)
    other_laid, other_square = lay(other_y, own_gain, order)
    home = a == c
    square = jnp.concatenate([mine_square, other_square], axis=0)
    inverse_root = lax.rsqrt((square + swapped(square)) / (feats * 8) + 1e-06)
    around = jnp.array((0, 1, -1, 2, -2, 3, -3, 4), jnp.int32)
    spots = jnp.concatenate([jnp.where(home, 1, 0)[None], (z + around) % 8]).astype(jnp.int32)

    def last_hop(ahead, behind):
        return both_ways(ahead[:, :half // 2], behind[:, half // 2:], "z")

    last = last_hop(*distant)
    outs[1] = swapped(outs[1])
    outs[1], outs[2], inverse_root, mine_laid, other_laid, *near_last = tied(
        outs[1], outs[2], inverse_root, mine_laid, other_laid, *near_q, *last
    )
    outs[3] = moved(3, outs[2])
    near_q, last = near_last[:2], near_last[2:]
    middle_q = both_ways(*near_q, "z")
    scales = inverse_root[:tokens_here], inverse_root[tokens_here:]
    own_scale, other_scale = jnp.where(home, *scales), jnp.where(home, *scales[::-1])
    weights = [(rows,)] + [(block,) for block in (*near, *middle, *distant)] + [tuple(last)]
    given = project(0, spots, mine_laid, other_laid, weights)
    came, *middle_q = tied(swapped(given), *middle_q)
    pairs = project(1, spots, mine_laid, other_laid, weights, (came, own_scale))
    cols = pairs.shape[1] // 2

    places = jnp.concatenate([(z * 2 + c) * tokens_here + here, (z * 2 + 1 - c) * tokens_here + here])
    limit = jnp.min(
        jnp.where(ends[None, :] > places[:, None], ends[None, :], ends[-1]), axis=1
    )
    limit = jnp.where(group == 1, ends[-1], limit).astype(jnp.int32)[:, None]

    def attend(hops, blocks, stat):
        bases = [(((z + hop) % 8) * 2 + c) * tokens_here for hop in hops]
        return flash(jnp.stack(bases), limit, queries, blocks, stat, hops == (4,))

    got = {0: pairs}
    got[1], got[-1] = both_ways(pairs, pairs, "z")
    *middle_q, _ = tied(*middle_q, pairs)
    distant_q = both_ways(*middle_q, "z")
    got[1], got[-1], outs[3], *distant_q = tied(got[1], got[-1], outs[3], *distant_q)
    got[2], got[-2] = both_ways(got[1], got[-1], "z")
    last_q = last_hop(*distant_q)
    outs[6] = moved(6, outs[3])
    weights = [(rows_q,)] + [(block,) for block in (*near_q, *middle_q, *distant_q)] + [tuple(last_q)]
    part = project(2, spots, mine_laid, other_laid, weights)
    came = swapped(part)
    got[2], got[-2], outs[6], came = tied(got[2], got[-2], outs[6], came)
    got[3], got[-3] = both_ways(got[2], got[-2], "z")
    queries = queries_of(part, came, own_scale, other_scale)
    outs[7] = moved(7, outs[6])

    def attend_hops(hops, stat):
        return attend(hops, [(got[hop], 0, got[hop], cols) for hop in hops], stat)

    stat = attend_hops((0, 1, -1), None)
    outs[3] = swapped(tied(outs[3], stat[0])[0])
    got[3], got[-3], outs[3], outs[7], *stat = tied(got[3], got[-3], outs[3], outs[7], *stat)
    ahead, behind = both_ways(got[3][:, :cols], got[-3][:, cols:], "z")
    outs[4] = moved(4, outs[7])
    stat = attend_hops((2, -2, 3, -3), stat)
    outs[7] = swapped(tied(outs[7], stat[0])[0])
    ahead, behind, outs[4], *stat = tied(ahead, behind, outs[4], *stat)
    outs[5] = moved(5, outs[4])
    one, one_stat, two, two_stat = attend((4,), [(ahead, 0, behind, 0)], stat)
    attended = merge(one, one_stat, swapped(two), swapped(two_stat))
    attended, outs[5] = tied(attended, outs[5])
    outs[5] = swapped(outs[5])

    lefts, rights = [], []
    for hop in (2, 1, 3, 0):
        block = crossed_along(attended, hop)
        lefts += [block, swapped(block)]
        rights += [outs[2 * hop], outs[2 * hop + 1]]
    index = jnp.full((1,), group, jnp.int32)
    result = result_of(index, times, mixed, states[0], lefts, rights)
    return shifted(result, "grp", 1)[None]


def solution(mesh):
    fine = jax.sharding.Mesh(mesh.devices.reshape(2, 8, 2, 4, 2), ("grp", "z", "a", "y", "c"))
    tokens, features = ("z", "a"), ("y", "c")
    return jax.shard_map(
        local,
        mesh=fine,
        in_specs=(
            P("grp", tokens, features),
            P("grp", tokens, features),
            P("grp", None),
            P("grp", None),
            P("grp", None),
            P("grp", tokens, None, features),
            P("grp", features, None),
        ),
        out_specs=P("grp", tokens, features),
        check_vma=False,
    )
```

```python
import functools

import jax
import jax.numpy as jnp
from jax import lax
from jax.experimental import pallas as pl
from jax.experimental.pallas import tpu as pltpu
from jax.sharding import PartitionSpec as P

HEAD_DIM = 128
STEPS = 4
LOW = -1e30
SCALE2 = HEAD_DIM ** (-0.5) * 1.4426950408889634


def crossed(block):
    return lax.ppermute(block, ("a", "c"), [(0, 0), (1, 2), (2, 1), (3, 3)])


def shifted(block, axis, hop):
    count = lax.axis_size(axis)
    return lax.ppermute(block, axis, [(i, (i - hop) % count) for i in range(count)])


def crossed_along(block, hop):
    route = []
    for a in range(2):
        for y in range(4):
            for c in range(2):
                route.append(((a * 4 + y) * 2 + c, (c * 4 + (y - hop) % 4) * 2 + a))
    return lax.ppermute(block, ("a", "y", "c"), route)


def swapped(block):
    return shifted(block, "c", 1)


def both_ways(ahead, behind, axis):
    return shifted(ahead, axis, 1), shifted(behind, axis, -1)


def tied(*values):
    return lax.optimization_barrier(values)


def params():
    return pltpu.CompilerParams(vmem_limit_bytes=32 * 1024 * 1024)


def in_vmem():
    return pl.BlockSpec(memory_space=pltpu.VMEM)


def lay_kernel(order_ref, gain_ref, *refs):
    x_refs, out_ref, square_ref = refs[:-2], refs[-2], refs[-1]
    step = pl.program_id(0)
    half = out_ref.shape[2]
    for n, x_ref in enumerate(x_refs):

        @pl.when(step == n)
        def _():
            wide = x_ref[...].astype(jnp.float32)
            scaled = (wide * gain_ref[0]).astype(out_ref.dtype)
            out_ref[0] = scaled[:, :half]
            out_ref[1] = scaled[:, half:]
            square = jnp.sum(wide * wide, axis=1, keepdims=True)
            square_ref[...] = jnp.where(step == 0, square, square_ref[...] + square)


def lay(xs, gain, order):
    blocks = gain.shape[0]
    tokens, feats = xs[0].shape
    return pl.pallas_call(
        lay_kernel,
        grid_spec=pltpu.PrefetchScalarGridSpec(
            num_scalar_prefetch=1,
            grid=(blocks,),
            in_specs=[pl.BlockSpec((1, 1, feats), lambda i, where: (where[i], 0, 0))]
            + [pl.BlockSpec((tokens, feats), lambda i, where: (0, 0))] * blocks,
            out_specs=[
                pl.BlockSpec((2, tokens, feats // 2), lambda i, where: (where[i], 0, 0)),
                pl.BlockSpec((tokens, 1), lambda i, where: (0, 0)),
            ],
        ),
        out_shape=[
            jax.ShapeDtypeStruct((2 * blocks, tokens, feats // 2), jnp.bfloat16),
            jax.ShapeDtypeStruct((tokens, 1), jnp.float32),
        ],
        compiler_params=params(),
        cost_estimate=pl.CostEstimate(
            flops=3 * blocks * tokens * feats, bytes_accessed=4 * blocks * tokens * feats, transcendentals=0
        ),
    )(order, gain, *xs)


def project_kernel(parts, first, last, where_ref, home_ref, *refs):
    blocks = len(parts)
    acts, refs = refs[:2 * blocks], refs[2 * blocks:]
    weights = []
    for count in parts:
        weights.append(refs[:count])
        refs = refs[count:]
    if not first:
        part_ref, refs = refs[0], refs[1:]
    kinds, _, width = weights[0][0].shape
    home = home_ref[0]
    for side in range(2):
        for kind in range(kinds):
            cols = slice(kind * width, (kind + 1) * width)
            value = 0.0
            for n in range(blocks):
                mine, other = acts[2 * n][0], acts[2 * n + 1][0]
                if last:
                    left = jnp.where(home == side, mine, other)
                else:
                    left = (mine, other)[side]
                right = jnp.concatenate([ref[kind] for ref in weights[n]], axis=0)
                value = value + jnp.dot(left, right, preferred_element_type=jnp.float32)
            if last:
                value = value + part_ref[jnp.where(home == side, 0, 1), :, cols]
                refs[side][:, cols] = value.astype(refs[side].dtype)
            else:
                if not first:
                    value = value + part_ref[side, :, cols]
                refs[0][side, :, cols] = value


def project(where, home, mine, other, weights, part, last):
    tokens, depth = mine.shape[1:]
    kinds, _, width = weights[0][0].shape
    blocks = len(weights)

    def chosen(n):
        return pl.BlockSpec((1, tokens, depth), lambda i, where, home: (where[n], 0, 0))

    def whole(shape):
        return pl.BlockSpec(shape, lambda i, where, home: (0,) * len(shape))

    flat, deep = (tokens, kinds * width), (2, tokens, kinds * width)
    operands, in_specs = [], []
    for n in range(blocks):
        operands += [mine, other]
        in_specs += [chosen(n)] * 2
    for group in weights:
        operands += group
        in_specs += [whole(array.shape) for array in group]
    if part is not None:
        operands.append(part)
        in_specs.append(whole(deep))
    if last:
        out_specs = [whole(flat)] * 2
        out_shape = [jax.ShapeDtypeStruct(flat, jnp.bfloat16), jax.ShapeDtypeStruct(flat, jnp.float32)]
    else:
        out_specs, out_shape = whole(deep), jax.ShapeDtypeStruct(deep, jnp.float32)
    return pl.pallas_call(
        functools.partial(project_kernel, [len(group) for group in weights], part is None, last),
        grid_spec=pltpu.PrefetchScalarGridSpec(
            num_scalar_prefetch=2, grid=(1,), in_specs=in_specs, out_specs=out_specs
        ),
        out_shape=out_shape,
        compiler_params=params(),
        cost_estimate=pl.CostEstimate(
            flops=4 * tokens * depth * blocks * kinds * width,
            bytes_accessed=2 * blocks * depth * (2 * tokens + kinds * width) + 16 * tokens * kinds * width,
            transcendentals=0,
        ),
    )(where, home, *operands)


def finish_kernel(kept_ref, came_ref, scale_ref, query_ref, pairs_ref):
    value = (kept_ref[...] + came_ref[...].astype(jnp.float32)) * scale_ref[...]
    value = value.astype(query_ref.dtype)

    @pl.when(pl.program_id(0) == 0)
    def _():
        query_ref[...] = value

    @pl.when(pl.program_id(0) > 0)
    def _():
        pairs_ref[...] = value


def finish(kept, came, scale):
    tokens, width = kept.shape[0], kept.shape[1] // 3
    part = pl.BlockSpec((tokens, width), lambda i: (0, i))
    return pl.pallas_call(
        finish_kernel,
        grid=(3,),
        in_specs=[part, part, pl.BlockSpec((tokens, 1), lambda i: (0, 0))],
        out_specs=[
            pl.BlockSpec((tokens, width), lambda i: (0, 0)),
            pl.BlockSpec((tokens, width), lambda i: (0, jnp.maximum(i - 1, 0))),
        ],
        out_shape=[
            jax.ShapeDtypeStruct((tokens, width), jnp.bfloat16),
            jax.ShapeDtypeStruct((tokens, 2 * width), jnp.bfloat16),
        ],
        compiler_params=params(),
        cost_estimate=pl.CostEstimate(
            flops=2 * kept.size, bytes_accessed=8 * kept.size, transcendentals=0
        ),
    )(kept, came, scale)


def flash_kernel(spots, first, split, base_ref, limit_ref, *refs):
    n_blocks = len(spots)
    queries, refs = refs[:2], refs[2:]
    n_arrays = 1 + max(max(spot[0], spot[2]) for spot in spots)
    arrays, rest = refs[:n_arrays], refs[n_arrays:]
    if not first:
        acc_in, stat_in = rest[:2]
        rest = rest[2:]
    rows, width = queries[0].shape
    heads = width // HEAD_DIM
    for side in range(2):
        span = slice(side * rows, (side + 1) * rows)
        limit = limit_ref[span, :]
        for head in range(heads):
            cols = slice(head * HEAD_DIM, (head + 1) * HEAD_DIM)
            query = queries[side][:, cols]
            scores = []
            for block, (array, start, _, _) in enumerate(spots):
                start = start + head * HEAD_DIM
                score = lax.dot_general(
                    query, arrays[array][:, start:start + HEAD_DIM], (((1,), (1,)), ((), ())),
                    preferred_element_type=jnp.float32,
                )
                place = lax.broadcasted_iota(jnp.int32, score.shape, 1)
                scores.append(jnp.where(place < limit - base_ref[block], score, LOW))
            high = functools.reduce(
                jnp.maximum, [jnp.max(score, axis=1, keepdims=True) for score in scores]
            )
            if not first:
                before = stat_in[span, head:head + 1]
                high = jnp.maximum(high, before)
            shift = high * SCALE2
            total, output = 0.0, 0.0
            for block, (_, _, array, start) in enumerate(spots):
                start = start + head * HEAD_DIM
                weight = jnp.exp2(scores[block] * SCALE2 - shift)
                total = total + jnp.sum(weight, axis=1, keepdims=True)
                output = output + jnp.dot(
                    weight.astype(jnp.bfloat16), arrays[array][:, start:start + HEAD_DIM],
                    preferred_element_type=jnp.float32,
                )
            if not first:
                shrink = jnp.exp2((before - high) * SCALE2)
                total = total + stat_in[span, heads + head:heads + head + 1] * shrink
                output = output + acc_in[span, cols] * shrink
            acc_out, stat_out = rest[2 * side:2 * side + 2] if split else rest
            place = slice(0, rows) if split else span
            acc_out[place, cols] = output
            stat_out[place, head:head + 1] = high
            stat_out[place, heads + head:heads + head + 1] = total


def flash(bases, limit, queries, blocks, stat, split):
    rows, width = queries[0].shape
    count = blocks[0][0].shape[0]
    arrays, spots = [], []
    for key, key_start, value, value_start in blocks:
        spot = []
        for array, start in ((key, key_start), (value, value_start)):
            known = [n for n, seen in enumerate(arrays) if seen is array]
            if not known:
                known = [len(arrays)]
                arrays.append(array)
            spot += [known[0], start]
        spots.append(tuple(spot))
    operands = [bases, limit, *queries, *arrays]
    operands += [] if stat is None else list(stat)
    sides = 1 if split else 2
    shapes = [
        jax.ShapeDtypeStruct((sides * rows, width), jnp.float32),
        jax.ShapeDtypeStruct((sides * rows, 128), jnp.float32),
    ]
    work = 2 * rows * count * len(blocks) * width
    return pl.pallas_call(
        functools.partial(flash_kernel, tuple(spots), stat is None, split),
        in_specs=[pl.BlockSpec(memory_space=pltpu.SMEM)] + [in_vmem()] * (len(operands) - 1),
        out_specs=[in_vmem()] * (2 * (3 - sides)),
        out_shape=shapes * (3 - sides),
        compiler_params=params(),
        cost_estimate=pl.CostEstimate(
            flops=4 * work,
            bytes_accessed=4 * len(blocks) * count * width + 20 * rows * width,
            transcendentals=work // HEAD_DIM,
        ),
    )(*operands)


def merge_kernel(n_parts, *refs):
    parts, stats, out_ref = refs[:n_parts], refs[n_parts:-1], refs[-1]
    heads = out_ref.shape[1] // HEAD_DIM
    for head in range(heads):
        cols = slice(head * HEAD_DIM, (head + 1) * HEAD_DIM)
        top, low = slice(head, head + 1), slice(heads + head, heads + head + 1)
        high = functools.reduce(jnp.maximum, [stat[:, top] for stat in stats])
        output, total = 0.0, 0.0
        for part, stat in zip(parts, stats):
            share = jnp.exp2((stat[:, top] - high) * SCALE2)
            total = total + stat[:, low] * share
            output = output + part[:, cols] * share
        out_ref[:, cols] = (output / total).astype(out_ref.dtype)


def merge(parts, stats):
    return pl.pallas_call(
        functools.partial(merge_kernel, len(parts)),
        in_specs=[in_vmem()] * (2 * len(parts)),
        out_specs=in_vmem(),
        out_shape=jax.ShapeDtypeStruct(parts[0].shape, jnp.bfloat16),
        compiler_params=params(),
        cost_estimate=pl.CostEstimate(
            flops=3 * len(parts) * parts[0].size, bytes_accessed=6 * len(parts) * parts[0].size, transcendentals=0
        ),
    )(*parts, *stats)


def result_kernel(n_blocks, index_ref, times_ref, mixed_ref, state_ref, *refs):
    lefts, rights, out_ref = refs[:n_blocks], refs[n_blocks:-1], refs[-1]
    velocity = 0.0
    for left, right in zip(lefts, rights):
        velocity = velocity + jnp.dot(left[...], right[...], preferred_element_type=jnp.float32)
    estimate = mixed_ref[...].astype(jnp.float32) - times_ref[...] * velocity
    value = jnp.where(index_ref[0] == 1, state_ref[...].astype(jnp.float32) - estimate, estimate)
    out_ref[...] = value.astype(out_ref.dtype)


def result_of(index, times, mixed, state, lefts, rights):
    tokens, feats = mixed.shape
    depth = lefts[0].shape[1]

    def whole(array):
        return pl.BlockSpec(array.shape, lambda i, index: (0, 0))

    columns = pl.BlockSpec((depth, feats), lambda i, index: (0, index[1]))
    return pl.pallas_call(
        functools.partial(result_kernel, len(lefts)),
        grid_spec=pltpu.PrefetchScalarGridSpec(
            num_scalar_prefetch=1,
            grid=(1,),
            in_specs=[whole(array) for array in (times, mixed, state, *lefts)]
            + [columns] * len(rights),
            out_specs=whole(mixed),
        ),
        out_shape=jax.ShapeDtypeStruct((tokens, feats), jnp.bfloat16),
        compiler_params=params(),
        cost_estimate=pl.CostEstimate(
            flops=2 * tokens * depth * len(lefts) * feats,
            bytes_accessed=2 * len(lefts) * depth * (tokens + feats) + 6 * tokens * feats,
            transcendentals=0,
        ),
    )(index, times, mixed, state, *lefts, *rights)


def local(states, noise, span_lengths, step_index, gain, in_weights, out_weights):
    tokens_here, feats = states.shape[1:]
    group = lax.axis_index("grp")
    z, a, y, c = (lax.axis_index(name) for name in ("z", "a", "y", "c"))
    lengths = span_lengths[0]
    ends = jnp.cumsum(lengths)
    here = jnp.arange(tokens_here, dtype=jnp.int32)

    rows = crossed(jnp.transpose(in_weights[0], (1, 0, 2)))
    half = rows.shape[1]

    positions = (z * 2 + a) * tokens_here + here
    spans = jnp.sum((positions[:, None] >= ends[None, :]).astype(jnp.int32), axis=1)
    hits = spans[:, None] == jnp.arange(lengths.shape[0], dtype=jnp.int32)[None, :]
    picked = jnp.where(hits, (step_index[0][None, :] + 1).astype(jnp.float32), jnp.float32(0.0))
    times = (jnp.sum(picked, axis=1) / STEPS)[:, None]
    state = states[0].astype(jnp.float32)
    mixed = ((1.0 - times) * state + times * noise[0].astype(jnp.float32)).astype(jnp.bfloat16)

    kept = jnp.where(c == 0, mixed[:, :half], mixed[:, half:])
    given = jnp.where(c == 0, mixed[:, half:], mixed[:, :half])
    taken = swapped(given)
    mine = jnp.concatenate([jnp.where(c == 0, kept, taken), jnp.where(c == 0, taken, kept)], axis=1)
    own_gain = gain[0].reshape(8, 2, half)
    own_gain = jnp.where(c == 0, own_gain[:, 0], own_gain[:, 1]).reshape(4, 1, feats)

    other = shifted(tied(mine, rows)[0], "a", 1)
    near = both_ways(rows, rows, "z")
    mine_y = [mine, shifted(mine, "y", 1), None, shifted(mine, "y", -1)]
    mine_y[2] = shifted(tied(mine, mine_y[1], mine_y[3])[0], "y", 2)
    mine_y[1], mine_y[3], *near = tied(mine_y[1], mine_y[3], *near)
    middle = both_ways(*near, "z")

    def block_for(hop):
        return lax.dynamic_slice_in_dim(out_weights[0], (y - hop) % 4 * 2 * feats, 2 * feats, axis=1)

    other, *outs = tied(other, *[block_for(hop) for hop in range(4)])
    other_y = [other, shifted(other, "y", 1), None, shifted(other, "y", -1)]
    other_y[2] = shifted(tied(other, other_y[1], other_y[3], mine_y[2])[0], "y", 2)
    mine_y[2], other_y[1], other_y[3], *middle = tied(mine_y[2], other_y[1], other_y[3], *middle)
    distant = both_ways(*middle, "z")

    outs[1], outs[3], _ = tied(outs[1], outs[3], other_y[2])
    near_out = (shifted(outs[1], "y", 1), shifted(outs[3], "y", 3))

    along = jnp.arange(4, dtype=jnp.int32)
    order = (y + along) % 4
    laid = []
    squares = []
    for blocks in (mine_y, other_y):
        block, square = lay(blocks, own_gain, order)
        laid.append(block)
        squares.append(square)
    home = a == c
    square = jnp.where(home, squares[0], squares[1])
    square = square + swapped(jnp.where(home, squares[1], squares[0]))
    inverse_root = lax.rsqrt(square / (feats * 8) + 1e-06)
    at_home = jnp.full((1,), jnp.where(home, 1, 0), jnp.int32)

    def project_hops(hops, weights, part, last=False):
        where = jnp.stack([(z + hop) % 8 for hop in hops]).astype(jnp.int32)
        return project(where, at_home, *laid, weights, part, last)

    part = project_hops((0, 1, -1, 2, -2), [(rows,)] + [(block,) for block in (*near, *middle)], None)
    part, inverse_root, *distant = tied(part, inverse_root, *distant)
    last = both_ways(distant[0][:, :half // 2], distant[1][:, half // 2:], "z")
    partners = [swapped(outs[0]), None, None, None]
    part, *last, outs[1], outs[3], partners[0] = tied(part, *last, *near_out, partners[0])
    given, kept = project_hops((3, -3, 4), [(distant[0],), (distant[1],), tuple(last)], part, True)
    came = swapped(given)
    cols = given.shape[1] // 3
    query, pairs = finish(kept, came, inverse_root)

    queries = (query, swapped(query))
    places = jnp.concatenate([(z * 2 + c) * tokens_here + here, (z * 2 + 1 - c) * tokens_here + here])
    limit = jnp.min(
        jnp.where(ends[None, :] > places[:, None], ends[None, :], ends[-1]), axis=1
    )
    limit = jnp.where(group == 1, ends[-1], limit).astype(jnp.int32)[:, None]

    def attend(hops, blocks, stat, split=False):
        bases = [(((z + hop) % 8) * 2 + c) * tokens_here for hop in hops]
        return flash(jnp.stack(bases), limit, queries, blocks, stat, split)

    ahead, behind = both_ways(pairs, pairs, "z")
    outs[2] = shifted(tied(outs[2], pairs, outs[1])[0], "y", 2)
    partners[1] = swapped(outs[1])
    stat = attend((0,), [(pairs, 0, pairs, cols)], None)
    for hop in (1, 2, 3):
        ahead, behind, *stat = tied(ahead, behind, *stat)
        if hop == 2:
            partners[1], outs[2], ahead, behind = tied(partners[1], outs[2], ahead, behind)
            partners[3] = swapped(tied(outs[3], stat[0])[0])
        if hop == 3:
            partners[3], ahead, behind = tied(partners[3], ahead, behind)
            partners[2] = swapped(outs[2])
        if hop < 3:
            onward = both_ways(ahead, behind, "z")
        else:
            onward = both_ways(ahead[:, :cols], behind[:, cols:], "z")
        stat = attend((hop, -hop), [(ahead, 0, ahead, cols), (behind, 0, behind, cols)], stat, hop == 3)
        ahead, behind = onward
    own, own_stat, *theirs = stat
    ahead, behind, partners[2], own, own_stat, *theirs = tied(ahead, behind, partners[2], own, own_stat, *theirs)
    theirs = [swapped(array) for array in theirs]
    late, late_stat, *their_late = attend((4,), [(ahead, 0, behind, 0)], None, True)
    their_late = [swapped(array) for array in their_late]
    attended = merge(
        [own, theirs[0], late, their_late[0]], [own_stat, theirs[1], late_stat, their_late[1]]
    )

    lefts, rights = [], []
    for hop in (2, 1, 3, 0):
        block = crossed_along(attended, hop)
        lefts += [block, swapped(block)]
        rights += [outs[hop], partners[hop]]
    index = jnp.stack([group, c]).astype(jnp.int32)
    result = result_of(index, times, mixed, states[0], lefts, rights)
    return shifted(result, "grp", 1)[None]


def solution(mesh):
    fine = jax.sharding.Mesh(mesh.devices.reshape(2, 8, 2, 4, 2), ("grp", "z", "a", "y", "c"))
    tokens, features = ("z", "a"), ("y", "c")
    return jax.shard_map(
        local,
        mesh=fine,
        in_specs=(
            P("grp", tokens, features),
            P("grp", tokens, features),
            P("grp", None),
            P("grp", None),
            P("grp", None),
            P("grp", tokens, None, features),
            P("grp", features, None),
        ),
        out_specs=P("grp", tokens, features),
        check_vma=False,
    )
```

```python
import functools

import jax
import jax.numpy as jnp
from jax import lax
from jax.experimental import pallas as pl
from jax.experimental.pallas import tpu as pltpu
from jax.sharding import PartitionSpec as P

HEAD_DIM = 128
STEPS = 4
LOW = -1e30
SCALE2 = HEAD_DIM ** (-0.5) * 1.4426950408889634


def crossed(block):
    return lax.ppermute(block, ("a", "c"), [(0, 0), (1, 2), (2, 1), (3, 3)])


def crossed_along(block, hop):
    route = []
    for a in range(2):
        for y in range(4):
            for c in range(2):
                route.append(((a * 4 + y) * 2 + c, (c * 4 + (y - hop) % 4) * 2 + a))
    return lax.ppermute(block, ("a", "y", "c"), route)


def shifted(block, axis, hop):
    count = lax.axis_size(axis)
    return lax.ppermute(block, axis, [(i, (i - hop) % count) for i in range(count)])


def swapped(block):
    return shifted(block, "c", 1)


def both_ways(ahead, behind, axis):
    return shifted(ahead, axis, 1), shifted(behind, axis, -1)


def tied(*values):
    return lax.optimization_barrier(values)


def params():
    return pltpu.CompilerParams(vmem_limit_bytes=32 * 1024 * 1024)


def in_vmem():
    return pl.BlockSpec(memory_space=pltpu.VMEM)


def lay_kernel(order_ref, gain_ref, *refs):
    x_refs, out_ref, square_ref = refs[:-2], refs[-2], refs[-1]
    step = pl.program_id(0)
    half = out_ref.shape[2]
    for n, x_ref in enumerate(x_refs):

        @pl.when(step == n)
        def _():
            wide = x_ref[...].astype(jnp.float32)
            scaled = (wide * gain_ref[0]).astype(out_ref.dtype)
            out_ref[0] = scaled[:, :half]
            out_ref[1] = scaled[:, half:]
            square = jnp.sum(wide * wide, axis=1, keepdims=True)
            square_ref[...] = jnp.where(step == 0, square, square_ref[...] + square)


def lay(xs, gain, order):
    blocks = gain.shape[0]
    tokens, feats = xs[0].shape
    return pl.pallas_call(
        lay_kernel,
        grid_spec=pltpu.PrefetchScalarGridSpec(
            num_scalar_prefetch=1,
            grid=(blocks,),
            in_specs=[pl.BlockSpec((1, 1, feats), lambda i, where: (where[i], 0, 0))]
            + [pl.BlockSpec((tokens, feats), lambda i, where: (0, 0))] * blocks,
            out_specs=[
                pl.BlockSpec((2, tokens, feats // 2), lambda i, where: (where[i], 0, 0)),
                pl.BlockSpec((tokens, 1), lambda i, where: (0, 0)),
            ],
        ),
        out_shape=[
            jax.ShapeDtypeStruct((2 * blocks, tokens, feats // 2), jnp.bfloat16),
            jax.ShapeDtypeStruct((tokens, 1), jnp.float32),
        ],
        compiler_params=params(),
        cost_estimate=pl.CostEstimate(
            flops=3 * blocks * tokens * feats, bytes_accessed=4 * blocks * tokens * feats, transcendentals=0
        ),
    )(order, gain, *xs)


def project_kernel(parts, first, last, where_ref, home_ref, *refs):
    blocks = len(parts)
    acts, refs = refs[:2 * blocks], refs[2 * blocks:]
    weights = []
    for count in parts:
        weights.append(refs[:count])
        refs = refs[count:]
    if not first:
        part_ref, refs = refs[0], refs[1:]
    kinds, _, width = weights[0][0].shape
    home = home_ref[0]
    for side in range(2):
        for kind in range(kinds):
            cols = slice(kind * width, (kind + 1) * width)
            value = 0.0
            for n in range(blocks):
                mine, other = acts[2 * n][0], acts[2 * n + 1][0]
                if last:
                    left = jnp.where(home == side, mine, other)
                else:
                    left = (mine, other)[side]
                right = jnp.concatenate([ref[kind] for ref in weights[n]], axis=0)
                value = value + jnp.dot(left, right, preferred_element_type=jnp.float32)
            if last:
                value = value + part_ref[jnp.where(home == side, 0, 1), :, cols]
                refs[side][:, cols] = value.astype(refs[side].dtype)
            else:
                if not first:
                    value = value + part_ref[side, :, cols]
                refs[0][side, :, cols] = value


def project(where, home, mine, other, weights, part, last):
    tokens, depth = mine.shape[1:]
    kinds, _, width = weights[0][0].shape
    blocks = len(weights)

    def chosen(n):
        return pl.BlockSpec((1, tokens, depth), lambda i, where, home: (where[n], 0, 0))

    def whole(shape):
        return pl.BlockSpec(shape, lambda i, where, home: (0,) * len(shape))

    flat, deep = (tokens, kinds * width), (2, tokens, kinds * width)
    operands, in_specs = [], []
    for n in range(blocks):
        operands += [mine, other]
        in_specs += [chosen(n)] * 2
    for group in weights:
        operands += group
        in_specs += [whole(array.shape) for array in group]
    if part is not None:
        operands.append(part)
        in_specs.append(whole(deep))
    if last:
        out_specs = [whole(flat)] * 2
        out_shape = [jax.ShapeDtypeStruct(flat, jnp.bfloat16), jax.ShapeDtypeStruct(flat, jnp.float32)]
    else:
        out_specs, out_shape = whole(deep), jax.ShapeDtypeStruct(deep, jnp.float32)
    return pl.pallas_call(
        functools.partial(project_kernel, [len(group) for group in weights], part is None, last),
        grid_spec=pltpu.PrefetchScalarGridSpec(
            num_scalar_prefetch=2, grid=(1,), in_specs=in_specs, out_specs=out_specs
        ),
        out_shape=out_shape,
        compiler_params=params(),
        cost_estimate=pl.CostEstimate(
            flops=4 * tokens * depth * blocks * kinds * width,
            bytes_accessed=2 * blocks * depth * (2 * tokens + kinds * width) + 16 * tokens * kinds * width,
            transcendentals=0,
        ),
    )(where, home, *operands)


def finish_kernel(kept_ref, came_ref, scale_ref, query_ref, pairs_ref):
    value = (kept_ref[...] + came_ref[...].astype(jnp.float32)) * scale_ref[...]
    value = value.astype(query_ref.dtype)

    @pl.when(pl.program_id(0) == 0)
    def _():
        query_ref[...] = value

    @pl.when(pl.program_id(0) > 0)
    def _():
        pairs_ref[...] = value


def finish(kept, came, scale):
    tokens, width = kept.shape[0], kept.shape[1] // 3
    part = pl.BlockSpec((tokens, width), lambda i: (0, i))
    return pl.pallas_call(
        finish_kernel,
        grid=(3,),
        in_specs=[part, part, pl.BlockSpec((tokens, 1), lambda i: (0, 0))],
        out_specs=[
            pl.BlockSpec((tokens, width), lambda i: (0, 0)),
            pl.BlockSpec((tokens, width), lambda i: (0, jnp.maximum(i - 1, 0))),
        ],
        out_shape=[
            jax.ShapeDtypeStruct((tokens, width), jnp.bfloat16),
            jax.ShapeDtypeStruct((tokens, 2 * width), jnp.bfloat16),
        ],
        compiler_params=params(),
        cost_estimate=pl.CostEstimate(
            flops=2 * kept.size, bytes_accessed=8 * kept.size, transcendentals=0
        ),
    )(kept, came, scale)


def flash_kernel(spots, first, last, base_ref, limit_ref, *refs):
    n_blocks = len(spots)
    queries, refs = refs[:2], refs[2:]
    n_arrays = 1 + max(max(spot[0], spot[2]) for spot in spots)
    arrays, rest = refs[:n_arrays], refs[n_arrays:]
    if not first:
        acc_in, stat_in = rest[:2]
        rest = rest[2:]
    rows, width = queries[0].shape
    heads = width // HEAD_DIM
    for side in range(2):
        span = slice(side * rows, (side + 1) * rows)
        limit = limit_ref[span, :]
        for head in range(heads):
            cols = slice(head * HEAD_DIM, (head + 1) * HEAD_DIM)
            query = queries[side][:, cols]
            scores = []
            for block, (array, start, _, _) in enumerate(spots):
                start = start + head * HEAD_DIM
                score = lax.dot_general(
                    query, arrays[array][:, start:start + HEAD_DIM], (((1,), (1,)), ((), ())),
                    preferred_element_type=jnp.float32,
                )
                place = lax.broadcasted_iota(jnp.int32, score.shape, 1)
                scores.append(jnp.where(place < limit - base_ref[block], score, LOW))
            high = functools.reduce(
                jnp.maximum, [jnp.max(score, axis=1, keepdims=True) for score in scores]
            )
            if not first:
                before = stat_in[span, head:head + 1]
                high = jnp.maximum(high, before)
            shift = high * SCALE2
            total, output = 0.0, 0.0
            for block, (_, _, array, start) in enumerate(spots):
                start = start + head * HEAD_DIM
                weight = jnp.exp2(scores[block] * SCALE2 - shift)
                total = total + jnp.sum(weight, axis=1, keepdims=True)
                output = output + jnp.dot(
                    weight.astype(jnp.bfloat16), arrays[array][:, start:start + HEAD_DIM],
                    preferred_element_type=jnp.float32,
                )
            if not first:
                shrink = jnp.exp2((before - high) * SCALE2)
                total = total + stat_in[span, heads + head:heads + head + 1] * shrink
                output = output + acc_in[span, cols] * shrink
            acc_out, stat_out = rest[2 * side:2 * side + 2] if last else rest
            place = slice(0, rows) if last else span
            acc_out[place, cols] = output
            stat_out[place, head:head + 1] = high
            stat_out[place, heads + head:heads + head + 1] = total


def flash(bases, limit, queries, blocks, stat, last):
    rows, width = queries[0].shape
    count = blocks[0][0].shape[0]
    arrays, spots = [], []
    for key, key_start, value, value_start in blocks:
        spot = []
        for array, start in ((key, key_start), (value, value_start)):
            known = [n for n, seen in enumerate(arrays) if seen is array]
            if not known:
                known = [len(arrays)]
                arrays.append(array)
            spot += [known[0], start]
        spots.append(tuple(spot))
    operands = [bases, limit, *queries, *arrays]
    operands += [] if stat is None else list(stat)
    sides = 1 if last else 2
    shapes = [
        jax.ShapeDtypeStruct((sides * rows, width), jnp.float32),
        jax.ShapeDtypeStruct((sides * rows, 128), jnp.float32),
    ]
    work = 2 * rows * count * len(blocks) * width
    return pl.pallas_call(
        functools.partial(flash_kernel, tuple(spots), stat is None, last),
        in_specs=[pl.BlockSpec(memory_space=pltpu.SMEM)] + [in_vmem()] * (len(operands) - 1),
        out_specs=[in_vmem()] * (2 * (3 - sides)),
        out_shape=shapes * (3 - sides),
        compiler_params=params(),
        cost_estimate=pl.CostEstimate(
            flops=4 * work,
            bytes_accessed=4 * len(blocks) * count * width + 20 * rows * width,
            transcendentals=work // HEAD_DIM,
        ),
    )(*operands)


def merge_kernel(one_ref, one_stat, two_ref, two_stat, out_ref):
    heads = out_ref.shape[1] // HEAD_DIM
    for head in range(heads):
        cols = slice(head * HEAD_DIM, (head + 1) * HEAD_DIM)
        top, low = slice(head, head + 1), slice(heads + head, heads + head + 1)
        high = jnp.maximum(one_stat[:, top], two_stat[:, top])
        one = jnp.exp2((one_stat[:, top] - high) * SCALE2)
        two = jnp.exp2((two_stat[:, top] - high) * SCALE2)
        total = one_stat[:, low] * one + two_stat[:, low] * two
        value = (one_ref[:, cols] * one + two_ref[:, cols] * two) / total
        out_ref[:, cols] = value.astype(out_ref.dtype)


def merge(one, one_stat, two, two_stat):
    return pl.pallas_call(
        merge_kernel,
        in_specs=[in_vmem()] * 4,
        out_specs=in_vmem(),
        out_shape=jax.ShapeDtypeStruct(one.shape, jnp.bfloat16),
        compiler_params=params(),
        cost_estimate=pl.CostEstimate(flops=4 * one.size, bytes_accessed=10 * one.size, transcendentals=0),
    )(one, one_stat, two, two_stat)


def result_kernel(n_blocks, index_ref, times_ref, mixed_ref, state_ref, *refs):
    lefts, rights, out_ref = refs[:n_blocks], refs[n_blocks:-1], refs[-1]
    velocity = 0.0
    for left, right in zip(lefts, rights):
        velocity = velocity + jnp.dot(left[...], right[...], preferred_element_type=jnp.float32)
    estimate = mixed_ref[...].astype(jnp.float32) - times_ref[...] * velocity
    value = jnp.where(index_ref[0] == 1, state_ref[...].astype(jnp.float32) - estimate, estimate)
    out_ref[...] = value.astype(out_ref.dtype)


def result_of(index, times, mixed, state, lefts, rights):
    tokens, feats = mixed.shape
    depth = lefts[0].shape[1]

    def whole(array):
        return pl.BlockSpec(array.shape, lambda i, index: (0, 0))

    columns = pl.BlockSpec((depth, feats), lambda i, index: (0, index[1]))
    return pl.pallas_call(
        functools.partial(result_kernel, len(lefts)),
        grid_spec=pltpu.PrefetchScalarGridSpec(
            num_scalar_prefetch=1,
            grid=(1,),
            in_specs=[whole(array) for array in (times, mixed, state, *lefts)]
            + [columns] * len(rights),
            out_specs=whole(mixed),
        ),
        out_shape=jax.ShapeDtypeStruct((tokens, feats), jnp.bfloat16),
        compiler_params=params(),
        cost_estimate=pl.CostEstimate(
            flops=2 * tokens * depth * len(lefts) * feats,
            bytes_accessed=2 * len(lefts) * depth * (tokens + feats) + 6 * tokens * feats,
            transcendentals=0,
        ),
    )(index, times, mixed, state, *lefts, *rights)


def local(states, noise, span_lengths, step_index, gain, in_weights, out_weights):
    tokens_here, feats = states.shape[1:]
    group = lax.axis_index("grp")
    z, a, y, c = (lax.axis_index(name) for name in ("z", "a", "y", "c"))
    lengths = span_lengths[0]
    ends = jnp.cumsum(lengths)
    here = jnp.arange(tokens_here, dtype=jnp.int32)

    rows = crossed(jnp.transpose(in_weights[0], (1, 0, 2)))
    half = rows.shape[1]

    positions = (z * 2 + a) * tokens_here + here
    spans = jnp.sum((positions[:, None] >= ends[None, :]).astype(jnp.int32), axis=1)
    hits = spans[:, None] == jnp.arange(lengths.shape[0], dtype=jnp.int32)[None, :]
    picked = jnp.where(hits, (step_index[0][None, :] + 1).astype(jnp.float32), jnp.float32(0.0))
    times = (jnp.sum(picked, axis=1) / STEPS)[:, None]
    state = states[0].astype(jnp.float32)
    mixed = ((1.0 - times) * state + times * noise[0].astype(jnp.float32)).astype(jnp.bfloat16)

    kept = jnp.where(c == 0, mixed[:, :half], mixed[:, half:])
    given = jnp.where(c == 0, mixed[:, half:], mixed[:, :half])
    taken = swapped(given)
    mine = jnp.concatenate([jnp.where(c == 0, kept, taken), jnp.where(c == 0, taken, kept)], axis=1)
    own_gain = gain[0].reshape(8, 2, half)
    own_gain = jnp.where(c == 0, own_gain[:, 0], own_gain[:, 1]).reshape(4, 1, feats)

    other = shifted(tied(mine, rows)[0], "a", 1)
    near = both_ways(rows, rows, "z")
    mine_y = [mine, shifted(mine, "y", 1), None, shifted(mine, "y", -1)]
    mine_y[2] = shifted(tied(mine, mine_y[1], mine_y[3])[0], "y", 2)
    mine_y[1], mine_y[3], *near = tied(mine_y[1], mine_y[3], *near)
    middle = both_ways(*near, "z")
    other_y = [other, shifted(other, "y", 1), None, shifted(other, "y", -1)]
    other_y[2] = shifted(tied(other, other_y[1], other_y[3], mine_y[2])[0], "y", 2)
    mine_y[2], other_y[1], other_y[3], *middle = tied(mine_y[2], other_y[1], other_y[3], *middle)
    distant = both_ways(*middle, "z")

    def block_for(hop):
        return lax.dynamic_slice_in_dim(out_weights[0], (y - hop) % 4 * 2 * feats, 2 * feats, axis=1)

    near_out = tied(block_for(1), block_for(3), other_y[2])
    near_out = (shifted(near_out[0], "y", 1), shifted(near_out[1], "y", 3))

    along = jnp.arange(4, dtype=jnp.int32)
    order = (y + along) % 4
    laid = []
    squares = []
    for blocks in (mine_y, other_y):
        block, square = lay(blocks, own_gain, order)
        laid.append(block)
        squares.append(square)
    home = a == c
    square = jnp.where(home, squares[0], squares[1])
    square = square + swapped(jnp.where(home, squares[1], squares[0]))
    inverse_root = lax.rsqrt(square / (feats * 8) + 1e-06)
    at_home = jnp.full((1,), jnp.where(home, 1, 0), jnp.int32)

    def project_hops(hops, weights, part, last=False):
        where = jnp.stack([(z + hop) % 8 for hop in hops]).astype(jnp.int32)
        return project(where, at_home, *laid, weights, part, last)

    part = project_hops((0,), [(rows,)], None)
    part = project_hops((1, -1), [(near[0],), (near[1],)], part)
    part, inverse_root, *distant = tied(part, inverse_root, *distant)
    part = project_hops((2, -2), [(middle[0],), (middle[1],)], part)
    last = both_ways(distant[0][:, :half // 2], distant[1][:, half // 2:], "z")
    part = project_hops((3, -3), [(distant[0],), (distant[1],)], part)
    part, *last, one_out, three_out = tied(part, *last, *near_out)
    given, kept = project_hops((4,), [tuple(last)], part, True)
    cols = given.shape[1] // 3
    query, pairs = finish(kept, swapped(given), inverse_root)

    queries = (query, swapped(query))
    places = jnp.concatenate([(z * 2 + c) * tokens_here + here, (z * 2 + 1 - c) * tokens_here + here])
    limit = jnp.min(
        jnp.where(ends[None, :] > places[:, None], ends[None, :], ends[-1]), axis=1
    )
    limit = jnp.where(group == 1, ends[-1], limit).astype(jnp.int32)[:, None]

    def attend(hops, blocks, stat):
        bases = [(((z + hop) % 8) * 2 + c) * tokens_here for hop in hops]
        return flash(jnp.stack(bases), limit, queries, blocks, stat, hops == (4,))

    ahead, behind = both_ways(pairs, pairs, "z")
    two_out = shifted(tied(block_for(2), pairs, one_out)[0], "y", 2)
    stat = attend((0,), [(pairs, 0, pairs, cols)], None)
    for hop in (1, 2, 3):
        ahead, behind, *stat = tied(ahead, behind, *stat)
        if hop == 3:
            two_out, one_out, three_out, ahead, behind = tied(two_out, one_out, three_out, ahead, behind)
            outs = [block_for(0), one_out, two_out, three_out]
            partners = [swapped(block) for block in outs]
        if hop < 3:
            onward = both_ways(ahead, behind, "z")
        else:
            onward = both_ways(ahead[:, :cols], behind[:, cols:], "z")
        stat = attend((hop, -hop), [(ahead, 0, ahead, cols), (behind, 0, behind, cols)], stat)
        ahead, behind = onward
    ahead, behind, *rest = tied(ahead, behind, *stat, *partners)
    stat, partners = rest[:2], rest[2:]
    one, one_stat, two, two_stat = attend((4,), [(ahead, 0, behind, 0)], stat)
    attended = merge(one, one_stat, swapped(two), swapped(two_stat))

    lefts, rights = [], []
    for hop in (2, 1, 3, 0):
        block = crossed_along(attended, hop)
        lefts += [block, swapped(block)]
        rights += [outs[hop], partners[hop]]
    index = jnp.stack([group, c]).astype(jnp.int32)
    result = result_of(index, times, mixed, states[0], lefts, rights)
    return shifted(result, "grp", 1)[None]


def solution(mesh):
    fine = jax.sharding.Mesh(mesh.devices.reshape(2, 8, 2, 4, 2), ("grp", "z", "a", "y", "c"))
    tokens, features = ("z", "a"), ("y", "c")
    return jax.shard_map(
        local,
        mesh=fine,
        in_specs=(
            P("grp", tokens, features),
            P("grp", tokens, features),
            P("grp", None),
            P("grp", None),
            P("grp", None),
            P("grp", tokens, None, features),
            P("grp", features, None),
        ),
        out_specs=P("grp", tokens, features),
        check_vma=False,
    )
```

```python
import functools

import jax
import jax.numpy as jnp
from jax import lax
from jax.experimental import pallas as pl
from jax.experimental.pallas import tpu as pltpu
from jax.sharding import PartitionSpec as P

HEAD_DIM = 128
STEPS = 4
LOW = -1e30
SCALE2 = HEAD_DIM ** (-0.5) * 1.4426950408889634


def crossed(block):
    return lax.ppermute(block, ("a", "c"), [(0, 0), (1, 2), (2, 1), (3, 3)])


def crossed_along(block, hop):
    route = []
    for a in range(2):
        for y in range(4):
            for c in range(2):
                route.append(((a * 4 + y) * 2 + c, (c * 4 + (y - hop) % 4) * 2 + a))
    return lax.ppermute(block, ("a", "y", "c"), route)


def shifted(block, axis, hop):
    count = lax.axis_size(axis)
    return lax.ppermute(block, axis, [(i, (i - hop) % count) for i in range(count)])


def swapped(block):
    return shifted(block, "c", 1)


def both_ways(ahead, behind, axis):
    return shifted(ahead, axis, 1), shifted(behind, axis, -1)


def tied(*values):
    return lax.optimization_barrier(values)


def params():
    return pltpu.CompilerParams(vmem_limit_bytes=22 * 1024 * 1024)


def in_vmem():
    return pl.BlockSpec(memory_space=pltpu.VMEM)


def lay_kernel(order_ref, gain_ref, *refs):
    x_refs, out_ref, square_ref = refs[:-2], refs[-2], refs[-1]
    step = pl.program_id(0)
    half = out_ref.shape[2]
    for n, x_ref in enumerate(x_refs):

        @pl.when(step == n)
        def _():
            wide = x_ref[...].astype(jnp.float32)
            scaled = (wide * gain_ref[0]).astype(out_ref.dtype)
            out_ref[0] = scaled[:, :half]
            out_ref[1] = scaled[:, half:]
            square = jnp.sum(wide * wide, axis=1, keepdims=True)
            square_ref[...] = jnp.where(step == 0, square, square_ref[...] + square)


def lay(xs, gain, order):
    blocks = gain.shape[0]
    tokens, feats = xs[0].shape
    return pl.pallas_call(
        lay_kernel,
        grid_spec=pltpu.PrefetchScalarGridSpec(
            num_scalar_prefetch=1,
            grid=(blocks,),
            in_specs=[pl.BlockSpec((1, 1, feats), lambda i, where: (where[i], 0, 0))]
            + [pl.BlockSpec((tokens, feats), lambda i, where: (0, 0))] * blocks,
            out_specs=[
                pl.BlockSpec((2, tokens, feats // 2), lambda i, where: (where[i], 0, 0)),
                pl.BlockSpec((tokens, 1), lambda i, where: (0, 0)),
            ],
        ),
        out_shape=[
            jax.ShapeDtypeStruct((2 * blocks, tokens, feats // 2), jnp.bfloat16),
            jax.ShapeDtypeStruct((tokens, 1), jnp.float32),
        ],
        compiler_params=params(),
        cost_estimate=pl.CostEstimate(
            flops=3 * blocks * tokens * feats, bytes_accessed=4 * blocks * tokens * feats, transcendentals=0
        ),
    )(order, gain, *xs)


def project_kernel(parts, first, last, where_ref, home_ref, *refs):
    blocks = len(parts)
    acts, refs = refs[:2 * blocks], refs[2 * blocks:]
    weights = []
    for count in parts:
        weights.append(refs[:count])
        refs = refs[count:]
    if not first:
        part_ref, refs = refs[0], refs[1:]
    kinds, _, width = weights[0][0].shape
    home = home_ref[0]
    for side in range(2):
        for kind in range(kinds):
            cols = slice(kind * width, (kind + 1) * width)
            value = 0.0
            for n in range(blocks):
                mine, other = acts[2 * n][0], acts[2 * n + 1][0]
                if last:
                    left = jnp.where(home == side, mine, other)
                else:
                    left = (mine, other)[side]
                right = jnp.concatenate([ref[kind] for ref in weights[n]], axis=0)
                value = value + jnp.dot(left, right, preferred_element_type=jnp.float32)
            if last:
                value = value + part_ref[jnp.where(home == side, 0, 1), :, cols]
                refs[side][:, cols] = value.astype(refs[side].dtype)
            else:
                if not first:
                    value = value + part_ref[side, :, cols]
                refs[0][side, :, cols] = value


def project(where, home, mine, other, weights, part, last):
    tokens, depth = mine.shape[1:]
    kinds, _, width = weights[0][0].shape
    blocks = len(weights)

    def chosen(n):
        return pl.BlockSpec((1, tokens, depth), lambda i, where, home: (where[n], 0, 0))

    def whole(shape):
        return pl.BlockSpec(shape, lambda i, where, home: (0,) * len(shape))

    flat, deep = (tokens, kinds * width), (2, tokens, kinds * width)
    operands, in_specs = [], []
    for n in range(blocks):
        operands += [mine, other]
        in_specs += [chosen(n)] * 2
    for group in weights:
        operands += group
        in_specs += [whole(array.shape) for array in group]
    if part is not None:
        operands.append(part)
        in_specs.append(whole(deep))
    if last:
        out_specs = [whole(flat)] * 2
        out_shape = [jax.ShapeDtypeStruct(flat, jnp.bfloat16)] * 2
    else:
        out_specs, out_shape = whole(deep), jax.ShapeDtypeStruct(deep, jnp.float32)
    return pl.pallas_call(
        functools.partial(project_kernel, [len(group) for group in weights], part is None, last),
        grid_spec=pltpu.PrefetchScalarGridSpec(
            num_scalar_prefetch=2, grid=(1,), in_specs=in_specs, out_specs=out_specs
        ),
        out_shape=out_shape,
        compiler_params=params(),
        cost_estimate=pl.CostEstimate(
            flops=4 * tokens * depth * blocks * kinds * width,
            bytes_accessed=2 * blocks * depth * (2 * tokens + kinds * width) + 16 * tokens * kinds * width,
            transcendentals=0,
        ),
    )(where, home, *operands)


def finish_kernel(kept_ref, came_ref, scale_ref, query_ref, pairs_ref):
    value = (kept_ref[...].astype(jnp.float32) + came_ref[...].astype(jnp.float32)) * scale_ref[...]
    value = value.astype(query_ref.dtype)

    @pl.when(pl.program_id(0) == 0)
    def _():
        query_ref[...] = value

    @pl.when(pl.program_id(0) > 0)
    def _():
        pairs_ref[...] = value


def finish(kept, came, scale):
    tokens, width = kept.shape[0], kept.shape[1] // 3
    part = pl.BlockSpec((tokens, width), lambda i: (0, i))
    return pl.pallas_call(
        finish_kernel,
        grid=(3,),
        in_specs=[part, part, pl.BlockSpec((tokens, 1), lambda i: (0, 0))],
        out_specs=[
            pl.BlockSpec((tokens, width), lambda i: (0, 0)),
            pl.BlockSpec((tokens, width), lambda i: (0, jnp.maximum(i - 1, 0))),
        ],
        out_shape=[
            jax.ShapeDtypeStruct((tokens, width), jnp.bfloat16),
            jax.ShapeDtypeStruct((tokens, 2 * width), jnp.bfloat16),
        ],
        compiler_params=params(),
        cost_estimate=pl.CostEstimate(
            flops=2 * kept.size, bytes_accessed=8 * kept.size, transcendentals=0
        ),
    )(kept, came, scale)


def flash_kernel(spots, first, last, base_ref, limit_ref, *refs):
    n_blocks = len(spots)
    queries, refs = refs[:2], refs[2:]
    n_arrays = 1 + max(max(spot[0], spot[2]) for spot in spots)
    arrays, rest = refs[:n_arrays], refs[n_arrays:]
    if not first:
        acc_in, stat_in = rest[:2]
        rest = rest[2:]
    rows, width = queries[0].shape
    heads = width // HEAD_DIM
    for side in range(2):
        span = slice(side * rows, (side + 1) * rows)
        limit = limit_ref[span, :]
        for head in range(heads):
            cols = slice(head * HEAD_DIM, (head + 1) * HEAD_DIM)
            query = queries[side][:, cols]
            scores = []
            for block, (array, start, _, _) in enumerate(spots):
                start = start + head * HEAD_DIM
                score = lax.dot_general(
                    query, arrays[array][:, start:start + HEAD_DIM], (((1,), (1,)), ((), ())),
                    preferred_element_type=jnp.float32,
                )
                place = lax.broadcasted_iota(jnp.int32, score.shape, 1)
                scores.append(jnp.where(place < limit - base_ref[block], score, LOW))
            high = functools.reduce(
                jnp.maximum, [jnp.max(score, axis=1, keepdims=True) for score in scores]
            )
            if not first:
                before = stat_in[span, head:head + 1]
                high = jnp.maximum(high, before)
            shift = high * SCALE2
            total, output = 0.0, 0.0
            for block, (_, _, array, start) in enumerate(spots):
                start = start + head * HEAD_DIM
                weight = jnp.exp2(scores[block] * SCALE2 - shift)
                total = total + jnp.sum(weight, axis=1, keepdims=True)
                output = output + jnp.dot(
                    weight.astype(jnp.bfloat16), arrays[array][:, start:start + HEAD_DIM],
                    preferred_element_type=jnp.float32,
                )
            if not first:
                shrink = jnp.exp2((before - high) * SCALE2)
                total = total + stat_in[span, heads + head:heads + head + 1] * shrink
                output = output + acc_in[span, cols] * shrink
            acc_out, stat_out = rest[2 * side:2 * side + 2] if last else rest
            place = slice(0, rows) if last else span
            acc_out[place, cols] = output
            stat_out[place, head:head + 1] = high
            stat_out[place, heads + head:heads + head + 1] = total


def flash(bases, limit, queries, blocks, stat, last):
    rows, width = queries[0].shape
    count = blocks[0][0].shape[0]
    arrays, spots = [], []
    for key, key_start, value, value_start in blocks:
        spot = []
        for array, start in ((key, key_start), (value, value_start)):
            known = [n for n, seen in enumerate(arrays) if seen is array]
            if not known:
                known = [len(arrays)]
                arrays.append(array)
            spot += [known[0], start]
        spots.append(tuple(spot))
    operands = [bases, limit, *queries, *arrays]
    operands += [] if stat is None else list(stat)
    sides = 1 if last else 2
    shapes = [
        jax.ShapeDtypeStruct((sides * rows, width), jnp.float32),
        jax.ShapeDtypeStruct((sides * rows, 128), jnp.float32),
    ]
    work = 2 * rows * count * len(blocks) * width
    return pl.pallas_call(
        functools.partial(flash_kernel, tuple(spots), stat is None, last),
        in_specs=[pl.BlockSpec(memory_space=pltpu.SMEM)] + [in_vmem()] * (len(operands) - 1),
        out_specs=[in_vmem()] * (2 * (3 - sides)),
        out_shape=shapes * (3 - sides),
        compiler_params=params(),
        cost_estimate=pl.CostEstimate(
            flops=4 * work,
            bytes_accessed=4 * len(blocks) * count * width + 20 * rows * width,
            transcendentals=work // HEAD_DIM,
        ),
    )(*operands)


def merge_kernel(one_ref, one_stat, two_ref, two_stat, out_ref):
    heads = out_ref.shape[1] // HEAD_DIM
    for head in range(heads):
        cols = slice(head * HEAD_DIM, (head + 1) * HEAD_DIM)
        top, low = slice(head, head + 1), slice(heads + head, heads + head + 1)
        high = jnp.maximum(one_stat[:, top], two_stat[:, top])
        one = jnp.exp2((one_stat[:, top] - high) * SCALE2)
        two = jnp.exp2((two_stat[:, top] - high) * SCALE2)
        total = one_stat[:, low] * one + two_stat[:, low] * two
        value = (one_ref[:, cols] * one + two_ref[:, cols] * two) / total
        out_ref[:, cols] = value.astype(out_ref.dtype)


def merge(one, one_stat, two, two_stat):
    return pl.pallas_call(
        merge_kernel,
        in_specs=[in_vmem()] * 4,
        out_specs=in_vmem(),
        out_shape=jax.ShapeDtypeStruct(one.shape, jnp.bfloat16),
        compiler_params=params(),
        cost_estimate=pl.CostEstimate(flops=4 * one.size, bytes_accessed=10 * one.size, transcendentals=0),
    )(one, one_stat, two, two_stat)


def result_kernel(n_blocks, index_ref, times_ref, mixed_ref, state_ref, *refs):
    lefts, rights, out_ref = refs[:n_blocks], refs[n_blocks:-1], refs[-1]
    velocity = 0.0
    for left, right in zip(lefts, rights):
        velocity = velocity + jnp.dot(left[...], right[...], preferred_element_type=jnp.float32)
    estimate = mixed_ref[...].astype(jnp.float32) - times_ref[...] * velocity
    value = jnp.where(index_ref[0] == 1, state_ref[...].astype(jnp.float32) - estimate, estimate)
    out_ref[...] = value.astype(out_ref.dtype)


def result_of(index, times, mixed, state, lefts, rights):
    tokens, feats = mixed.shape
    depth = lefts[0].shape[1]

    def whole(array):
        return pl.BlockSpec(array.shape, lambda i, index: (0, 0))

    columns = pl.BlockSpec((depth, feats), lambda i, index: (0, index[1]))
    return pl.pallas_call(
        functools.partial(result_kernel, len(lefts)),
        grid_spec=pltpu.PrefetchScalarGridSpec(
            num_scalar_prefetch=1,
            grid=(1,),
            in_specs=[whole(array) for array in (times, mixed, state, *lefts)]
            + [columns] * len(rights),
            out_specs=whole(mixed),
        ),
        out_shape=jax.ShapeDtypeStruct((tokens, feats), jnp.bfloat16),
        compiler_params=params(),
        cost_estimate=pl.CostEstimate(
            flops=2 * tokens * depth * len(lefts) * feats,
            bytes_accessed=2 * len(lefts) * depth * (tokens + feats) + 6 * tokens * feats,
            transcendentals=0,
        ),
    )(index, times, mixed, state, *lefts, *rights)


def local(states, noise, span_lengths, step_index, gain, in_weights, out_weights):
    tokens_here, feats = states.shape[1:]
    group = lax.axis_index("grp")
    z, a, y, c = (lax.axis_index(name) for name in ("z", "a", "y", "c"))
    lengths = span_lengths[0]
    ends = jnp.cumsum(lengths)
    here = jnp.arange(tokens_here, dtype=jnp.int32)

    rows = crossed(jnp.transpose(in_weights[0], (1, 0, 2)))
    half = rows.shape[1]

    positions = (z * 2 + a) * tokens_here + here
    spans = jnp.sum((positions[:, None] >= ends[None, :]).astype(jnp.int32), axis=1)
    hits = spans[:, None] == jnp.arange(lengths.shape[0], dtype=jnp.int32)[None, :]
    picked = jnp.where(hits, (step_index[0][None, :] + 1).astype(jnp.float32), jnp.float32(0.0))
    times = (jnp.sum(picked, axis=1) / STEPS)[:, None]
    state = states[0].astype(jnp.float32)
    mixed = ((1.0 - times) * state + times * noise[0].astype(jnp.float32)).astype(jnp.bfloat16)

    kept = jnp.where(c == 0, mixed[:, :half], mixed[:, half:])
    given = jnp.where(c == 0, mixed[:, half:], mixed[:, :half])
    taken = swapped(given)
    mine = jnp.concatenate([jnp.where(c == 0, kept, taken), jnp.where(c == 0, taken, kept)], axis=1)
    own_gain = gain[0].reshape(8, 2, half)
    own_gain = jnp.where(c == 0, own_gain[:, 0], own_gain[:, 1]).reshape(4, 1, feats)

    other = shifted(tied(mine, rows)[0], "a", 1)
    near = both_ways(rows, rows, "z")
    mine_y = [mine, shifted(mine, "y", 1), None, shifted(mine, "y", -1)]
    mine_y[2] = shifted(tied(mine, mine_y[1], mine_y[3])[0], "y", 2)
    mine_y[1], mine_y[3], *near = tied(mine_y[1], mine_y[3], *near)
    middle = both_ways(*near, "z")
    other_y = [other, shifted(other, "y", 1), None, shifted(other, "y", -1)]
    other_y[2] = shifted(tied(other, other_y[1], other_y[3], mine_y[2])[0], "y", 2)
    mine_y[2], other_y[1], other_y[3], *middle = tied(mine_y[2], other_y[1], other_y[3], *middle)
    distant = both_ways(*middle, "z")

    def block_for(hop):
        return lax.dynamic_slice_in_dim(out_weights[0], (y - hop) % 4 * 2 * feats, 2 * feats, axis=1)

    near_out = tied(block_for(1), block_for(3), other_y[2])
    near_out = (shifted(near_out[0], "y", 1), shifted(near_out[1], "y", 3))

    along = jnp.arange(4, dtype=jnp.int32)
    order = (y + along) % 4
    laid = []
    squares = []
    for blocks in (mine_y, other_y):
        block, square = lay(blocks, own_gain, order)
        laid.append(block)
        squares.append(square)
    home = a == c
    square = jnp.where(home, squares[0], squares[1])
    square = square + swapped(jnp.where(home, squares[1], squares[0]))
    inverse_root = lax.rsqrt(square / (feats * 8) + 1e-06)
    at_home = jnp.full((1,), jnp.where(home, 1, 0), jnp.int32)

    def project_hops(hops, weights, part, last=False):
        where = jnp.stack([(z + hop) % 8 for hop in hops]).astype(jnp.int32)
        return project(where, at_home, *laid, weights, part, last)

    part = project_hops((0,), [(rows,)], None)
    part = project_hops((1, -1), [(near[0],), (near[1],)], part)
    part, inverse_root, *distant = tied(part, inverse_root, *distant)
    part = project_hops((2, -2), [(middle[0],), (middle[1],)], part)
    last = both_ways(distant[0][:, :half // 2], distant[1][:, half // 2:], "z")
    part = project_hops((3, -3), [(distant[0],), (distant[1],)], part)
    part, *last, one_out, three_out = tied(part, *last, *near_out)
    given, kept = project_hops((4,), [tuple(last)], part, True)
    cols = given.shape[1] // 3
    query, pairs = finish(kept, swapped(given), inverse_root)

    queries = (query, swapped(query))
    places = jnp.concatenate([(z * 2 + c) * tokens_here + here, (z * 2 + 1 - c) * tokens_here + here])
    limit = jnp.min(
        jnp.where(ends[None, :] > places[:, None], ends[None, :], ends[-1]), axis=1
    )
    limit = jnp.where(group == 1, ends[-1], limit).astype(jnp.int32)[:, None]

    def attend(hops, blocks, stat):
        bases = [(((z + hop) % 8) * 2 + c) * tokens_here for hop in hops]
        return flash(jnp.stack(bases), limit, queries, blocks, stat, hops == (4,))

    ahead, behind = both_ways(pairs, pairs, "z")
    two_out = shifted(tied(block_for(2), pairs, one_out)[0], "y", 2)
    stat = attend((0,), [(pairs, 0, pairs, cols)], None)
    for hop in (1, 2, 3):
        ahead, behind, *stat = tied(ahead, behind, *stat)
        if hop == 3:
            two_out, one_out, three_out, ahead, behind = tied(two_out, one_out, three_out, ahead, behind)
            outs = [block_for(0), one_out, two_out, three_out]
            partners = [swapped(block) for block in outs]
        if hop < 3:
            onward = both_ways(ahead, behind, "z")
        else:
            onward = both_ways(ahead[:, :cols], behind[:, cols:], "z")
        stat = attend((hop, -hop), [(ahead, 0, ahead, cols), (behind, 0, behind, cols)], stat)
        ahead, behind = onward
    ahead, behind, *rest = tied(ahead, behind, *stat, *partners)
    stat, partners = rest[:2], rest[2:]
    one, one_stat, two, two_stat = attend((4,), [(ahead, 0, behind, 0)], stat)
    attended = merge(one, one_stat, swapped(two), swapped(two_stat))

    lefts, rights = [], []
    for hop in (2, 1, 3, 0):
        block = crossed_along(attended, hop)
        lefts += [block, swapped(block)]
        rights += [outs[hop], partners[hop]]
    index = jnp.stack([group, c]).astype(jnp.int32)
    result = result_of(index, times, mixed, states[0], lefts, rights)
    return shifted(result, "grp", 1)[None]


def solution(mesh):
    fine = jax.sharding.Mesh(mesh.devices.reshape(2, 8, 2, 4, 2), ("grp", "z", "a", "y", "c"))
    tokens, features = ("z", "a"), ("y", "c")
    return jax.shard_map(
        local,
        mesh=fine,
        in_specs=(
            P("grp", tokens, features),
            P("grp", tokens, features),
            P("grp", None),
            P("grp", None),
            P("grp", None),
            P("grp", tokens, None, features),
            P("grp", features, None),
        ),
        out_specs=P("grp", tokens, features),
        check_vma=False,
    )
```
